512 devices in a mesh: lon: 16 (over x_hi, z), lat: 32 (over x_lo, y, core).
Axes of the slice: x: 4 (x_hi: 2, x_lo: 2; x = x_hi * 2 + x_lo), y: 8, z: 8, core: 2. Of those that a mesh axis runs over, the one named last changes fastest.
Arguments:
- temp: float32 [8, 1024, 4096], P(None, 'lat', 'lon'), may hold values from -6 to 6
- salt: float32 [8, 1024, 4096], P(None, 'lat', 'lon'), may hold values from -6 to 6
- u_courant: float32 [8, 1024, 4096], P(None, 'lat', 'lon'), may hold values from -0.4 to 0.4
- v_courant: float32 [8, 1024, 4096], P(None, 'lat', 'lon'), may hold values from -0.4 to 0.4
- diffusion: float32 [8, 1024, 4096], P(None, 'lat', 'lon'), may hold values from 0.02 to 0.12
- slope_x: float32 [8, 1024, 4096], P(None, 'lat', 'lon'), may hold values from -1 to 1
- slope_y: float32 [8, 1024, 4096], P(None, 'lat', 'lon'), may hold values from -1 to 1
- u_mask: int32 [8, 1024, 4096], P(None, 'lat', 'lon'), may hold values 0 or 1
- v_mask: int32 [8, 1024, 4096], P(None, 'lat', 'lon'), may hold values 0 or 1
Outputs:
- temp_next: float32 [8, 1024, 4096], P(None, 'lat', 'lon')
- salt_next: float32 [8, 1024, 4096], P(None, 'lat', 'lon')
The draws below stay inside these ranges and needn't reach their ends.
All inputs are finite; a program needn't handle non-finite values. No bound on the sum of `u_mask` or of `v_mask` on one device may be relied on, other than what follows from the above.
Results may differ from the reference program's by a relative error of at most 0.0003.
Values sent between devices are 32-bit elements; how exact they have to be, the bound alone decides.
No kernel may reach another device: no remote copies, remote signals or barrier semaphores. Data moves between devices by JAX's collectives and lax.ppermute only.
A program may use at most 64 MiB of HBM per device.

```python
import math
import jax
import jax.numpy as jnp

LEVELS = 8
STEPS = 4
NX = 4096
NY = 1024


def set_ends(drawn, key, smallest, high):
    place = [jax.random.randint(jax.random.fold_in(key, axis), (), 0, length) for axis, length in enumerate(drawn.shape)]
    longest = drawn.shape.index(max(drawn.shape))
    beside = place[:longest] + [(place[longest] + 1) % drawn.shape[longest]] + place[longest + 1:]
    return drawn.at[tuple(place)].set(smallest).at[tuple(beside)].set(high)


def block_levels(stream_key, shape, shards, least, high):
    level, own = 1.0, jax.random.fold_in(stream_key, 6)
    for position, blocks in shards:
        steps = jnp.exp(jax.random.uniform(jax.random.fold_in(own, position), (blocks,), jnp.float32, least / len(shards), high / len(shards)))
        level = level * jnp.repeat(steps, shape[position] // blocks).reshape([-1 if axis == position else 1 for axis in range(len(shape))])
    return level


def normal_values(rng, shape, spread, most, shards=(), dtype=jnp.bfloat16):
    entries = jax.random.normal(rng, shape, jnp.float32) * spread
    if len(shards) > 0:
        entries = block_levels(rng, shape, shards, -0.22, 0.18) * entries
    return jnp.clip(entries, min=-most, max=most).astype(dtype)


def setup_inputs(seed: int = 0) -> dict:
    key_of = jax.random.split(jax.random.key(seed), 10)
    temp = normal_values(key_of[0], (LEVELS, NY, NX), 1.0, 6.0, ((1, 32), (2, 16)), jnp.float32)
    salt = normal_values(key_of[1], (LEVELS, NY, NX), 1.0, 6.0, ((1, 32), (2, 16)), jnp.float32)
    u_courant = jnp.clip(jax.random.uniform(key_of[2], (LEVELS, NY, NX), jnp.float32, -0.4, 0.4) * block_levels(key_of[2], (LEVELS, NY, NX), ((1, 32), (2, 16)), -0.4, 0.0), -0.4, 0.4)
    v_courant = jnp.clip(jax.random.uniform(key_of[3], (LEVELS, NY, NX), jnp.float32, -0.4, 0.4) * block_levels(key_of[3], (LEVELS, NY, NX), ((1, 32), (2, 16)), -0.4, 0.0), -0.4, 0.4)
    diffusion = jnp.clip(jnp.exp(math.log(0.12) - 1.7917595 * jax.random.uniform(key_of[4], (LEVELS, NY, NX), jnp.float32) ** block_levels(key_of[4], (LEVELS, NY, NX), ((1, 32), (2, 16)), -0.2, 0.2)), 0.02, 0.12)
    slope_x = jnp.clip(jax.random.uniform(key_of[5], (LEVELS, NY, NX), jnp.float32, -1.0, 1.0) * block_levels(key_of[5], (LEVELS, NY, NX), ((1, 32), (2, 16)), -0.4, 0.0), -1.0, 1.0)
    slope_y = jnp.clip(jax.random.uniform(key_of[6], (LEVELS, NY, NX), jnp.float32, -1.0, 1.0) * block_levels(key_of[6], (LEVELS, NY, NX), ((1, 32), (2, 16)), -0.4, 0.0), -1.0, 1.0)
    u_mask = set_ends((jax.random.randint(key_of[7], (LEVELS, NY, NX), 0, 8) < 7).astype(jnp.int32), jax.random.fold_in(key_of[7], 1), 0, 1)
    v_mask = set_ends((jax.random.randint(key_of[8], (LEVELS, NY, NX), 0, 8) < 7).astype(jnp.int32), jax.random.fold_in(key_of[8], 1), 0, 1)
    return {"temp": temp, "salt": salt, "u_courant": u_courant, "v_courant": v_courant, "diffusion": diffusion, "slope_x": slope_x, "slope_y": slope_y, "u_mask": u_mask, "v_mask": v_mask}


def minmod(first, second):
    return 0.5 * (jnp.sign(first) + jnp.sign(second)) * jnp.minimum(jnp.abs(first), jnp.abs(second))

def vertical_grad(field):
    upper = jnp.concatenate([field[..., 1:, :, :], field[..., -1:, :, :]], axis=-3)
    lower = jnp.concatenate([field[..., :1, :, :], field[..., :-1, :, :]], axis=-3)
    return 0.5 * (upper - lower)

def face_flux(far_back, here_cell, next_cell, far_next, grad_here, grad_next, faces):
    velocity, diffuse, slope, wetness = (faces[0], faces[1], faces[2], faces[3])
    forward = velocity >= 0.0
    jump_diff = next_cell - here_cell
    upwind_value = jnp.where(forward, here_cell, next_cell)
    upwind_diff = jnp.where(forward, here_cell - far_back, far_next - next_cell)
    speed = jnp.abs(velocity)
    advected = velocity * upwind_value + 0.5 * speed * (1.0 - speed) * minmod(jump_diff, upwind_diff)
    diffused = diffuse * (jump_diff - slope * 0.5 * (grad_here + grad_next))
    return wetness * (advected - diffused)

def advance(tracers, lon_ext, lat_ext, east_faces, north_faces):
    width = tracers.shape[-1]
    height = tracers.shape[-2]
    grad_x = vertical_grad(lon_ext)
    grad_y = vertical_grad(lat_ext)
    flux_x = face_flux(lon_ext[..., 0:width + 1], lon_ext[..., 1:width + 2], lon_ext[..., 2:width + 3], lon_ext[..., 3:width + 4], grad_x[..., 1:width + 2], grad_x[..., 2:width + 3], east_faces)
    flux_y = face_flux(lat_ext[..., 0:height + 1, :], lat_ext[..., 1:height + 2, :], lat_ext[..., 2:height + 3, :], lat_ext[..., 3:height + 4, :], grad_y[..., 1:height + 2, :], grad_y[..., 2:height + 3, :], north_faces)
    return tracers - (flux_x[..., 1:] - flux_x[..., :-1]) - (flux_y[..., 1:, :] - flux_y[..., :-1, :])

def reference(temp, salt, u_courant, v_courant, diffusion, slope_x, slope_y, u_mask, v_mask):
    east_stack = jnp.stack([u_courant, diffusion, slope_x, u_mask.astype(jnp.float32)])
    north_stack = jnp.stack([v_courant, diffusion, slope_y, v_mask.astype(jnp.float32)])
    east_faces = jnp.concatenate([east_stack[..., -1:], east_stack], axis=-1)
    south_zero = jnp.zeros_like(north_stack[..., :1, :])
    north_faces = jnp.concatenate([south_zero, north_stack], axis=-2)
    tracers = jnp.stack([temp, salt])
    for substep in range(STEPS):
        lon_ext = jnp.concatenate([tracers[..., -2:], tracers, tracers[..., :2]], axis=-1)
        folded = tracers[..., -2:, :][..., ::-1, ::-1]
        south_rows = jnp.zeros_like(tracers[..., :2, :])
        lat_ext = jnp.concatenate([south_rows, tracers, folded], axis=-2)
        tracers = advance(tracers, lon_ext, lat_ext, east_faces, north_faces)
    return (tracers[0], tracers[1])
```

```python
import functools

import jax
import jax.numpy as jnp
from jax import lax
from jax.experimental import pallas as pl
from jax.experimental.pallas import tpu as pltpu
from jax.sharding import PartitionSpec as P

STEPS = 4
HALO = 2 * STEPS
LEVELS = 8
HEIGHT = 32
WIDTH = 256
EXT = HEIGHT + 2 * HALO
TOP = HALO + HEIGHT - 1
F32 = jnp.float32
VMEM = pl.BlockSpec(memory_space=pltpu.VMEM)
SMEM = pl.BlockSpec(memory_space=pltpu.SMEM)
PARAMS = pltpu.CompilerParams(vmem_limit_bytes=48 * 2**20)

TRACERS, XF, YF = (0, 1), (2, 3, 4), (5, 6, 7)
MESSAGE = 2 * 8 + 3 * 6 + 3 * 7


def slot(field, k):
    if field < 2:
        return field * 8 + k
    if field < 5:
        return 16 + (field - 2) * 6 + k
    return 34 + (field - 5) * 7 + k


def rows_of(field):
    return 8 if field < 2 else 6 if field < 5 else 7


def level_major(x):
    x = x.reshape(LEVELS, HEIGHT // 8, 8, WIDTH // 128, 128)
    return x.transpose(0, 1, 3, 2, 4).reshape(-1, 128)


def from_level_major(x):
    x = x.reshape(LEVELS, HEIGHT // 8, WIDTH // 128, 8, 128)
    return x.transpose(0, 1, 3, 2, 4).reshape(LEVELS, HEIGHT, WIDTH)


def places(j):
    start = (j // 8) * 16 + j % 8
    return [pl.ds(start + 8 * c, LEVELS, stride=2 * HEIGHT) for c in range(2)]


def load_row(ref, j):
    return jnp.concatenate([ref[at, :] for at in places(j)], axis=1)


def lanes(width):
    return lax.broadcasted_iota(jnp.int32, (LEVELS, width), 1)


def roll(x, by):
    return pltpu.roll(x, by % x.shape[-1], 1)


def pack_kernel(flags, temp, salt, u, v, diff, sx, sy, mu, mv, rows, odd_msg, even_msg):
    def one(j, _):
        def at(ref):
            return load_row(ref, j)

        wet_u, wet_v = at(mu).astype(F32), at(mv).astype(F32)
        r = at(diff)
        rows[0, j] = at(temp)
        rows[1, j] = at(salt)
        rows[2, j] = at(u) * wet_u
        rows[3, j] = r * wet_u
        rows[4, j] = at(sx)
        rows[5, j] = at(v) * wet_v
        rows[6, j] = r * wet_v
        rows[7, j] = at(sy)
        return 0

    lax.fori_loop(0, HEIGHT, one, 0, unroll=4)
    odd = flags[0]
    for f in range(8):
        n = rows_of(f)
        north = HEIGHT - n
        for k in range(n):
            odd_msg[slot(f, k)] = rows[f, odd * north + k]
            even_msg[slot(f, k)] = rows[f, (1 - odd) * north + k]


def mirrored(x):
    n = x.shape[-1] // 128
    back = 127 - lanes(128)
    parts = [x[:, 128 * i : 128 * (i + 1)] for i in range(n)]
    return jnp.concatenate([jnp.take_along_axis(p, back, axis=1) for p in reversed(parts)], axis=1)


def ghost_kernel(flags, rows, odd_msg, even_msg, ghost, odd_strip, even_strip):
    odd, top, lon_odd = flags[0], flags[1], flags[2]
    is_odd = odd == 1
    for f in range(8):
        n = rows_of(f)
        for k in range(n):
            a, b = odd_msg[slot(f, k)], even_msg[slot(f, k)]
            ghost[f, HALO - n + k] = jnp.where(is_odd, b, a)
            if k < n - (f >= 5):
                ghost[f, HALO + k] = jnp.where(is_odd, a, b)
        if f >= 5:
            ghost[f, 0] = rows[f, HEIGHT - 1]

    @pl.when(top == 1)
    def _():
        for f in range(8):
            n = rows_of(f)
            sign = -1.0 if f in (2, 4, 5, 7) else 1.0
            for k in range(n):
                x = mirrored(odd_msg[slot(f, n - 1 - k)]) * sign
                if f < 5:
                    ghost[f, HALO + k] = x
                elif k == 0:
                    ghost[f, 0] = x
                else:
                    ghost[f, HALO + k - 1] = x

    lane = lanes(128)
    swap = lon_odd == 1
    for r in range(EXT // 2):
        even_out = jnp.zeros((LEVELS, 128), F32)
        odd_out = jnp.zeros((LEVELS, 128), F32)
        for half in range(2):
            idx = r + half * (EXT // 2)
            for f in range(8):
                if idx < HALO:
                    x = ghost[f, idx]
                elif idx <= TOP:
                    x = rows[f, idx - HALO]
                else:
                    x = ghost[f, idx - HEIGHT]
                s = 8 * (f + 8 * half)
                west, east = roll(x[:, :128], s), roll(x[:, 128:], s + 8)
                here = (lane >= s) & (lane < s + 8)
                even_out = jnp.where(here, jnp.where(swap, west, east), even_out)
                odd_out = jnp.where(here, jnp.where(swap, east, west), odd_out)
        even_strip[r] = even_out
        odd_strip[r] = odd_out


def minmod(p, t):
    return jnp.maximum(jnp.minimum(p, t), jnp.minimum(jnp.maximum(p, t), 0.0))


def vertical(q):
    level = lax.broadcasted_iota(jnp.int32, q.shape, 0)
    e = jnp.where(level == 0, 0.0, q - pltpu.roll(q, 1, 0))
    return e + pltpu.roll(e, LEVELS - 1, 0)


def coefficients(c, r, s):
    plus, minus = jnp.maximum(c, 0.0), jnp.minimum(c, 0.0)
    return (
        plus + r,
        0.5 * plus * (1.0 - plus),
        0.25 * r * s,
        minus - r,
        -0.5 * minus * (1.0 + minus),
    )


def store_x(cx, idx, c, r, s):
    p, lp, t, e, ln = coefficients(c, r, s)
    for n, x in enumerate((p, lp, t, roll(e, 1), roll(ln, 1), roll(t, 1))):
        cx[n, idx] = x


def store_y(cy, idx, c, r, s):
    for n, x in enumerate(coefficients(c, r, s)):
        cy[n, idx] = x


def sweep(read, write, cx, cy, lo, hi, streams):
    def face(idx, q0, q1, m0, m1, g0, g1):
        return (
            cy[0, idx] * q0 + cy[3, idx] * q1 + (cy[1, idx] * m0 + cy[4, idx] * m1)
            + cy[2, idx] * (g0 + g1)
        )

    def row(idx, carry, seam=False):
        out = []
        for n in range(streams):
            q0, q1, d0, m0, g0, south = carry[n]
            q2 = read(n, idx + 2)
            d1 = q2 - q1
            m1 = minmod(d0, d1)
            g1 = vertical(q1)
            north = face(idx, q0, q1, m0, m1, g0, g1)
            d = roll(q0, -1) - q0
            m = minmod(d, roll(d, 1))
            a = cx[0, idx] * q0 + cx[1, idx] * m + cx[2, idx] * g0
            b = cx[3, idx] * q0 + cx[4, idx] * m + cx[5, idx] * g0
            write(n, idx, q0 + ((b - a) + (roll(a, 1) - roll(b, -1))) + (south - north))
            if seam:
                north = face(0, q0, q1, m0, m1, g0, g1)
            out.append((q1, q2, d1, m1, g1, north))
        return tuple(out)

    carry = []
    for n in range(streams):
        q = [read(n, lo - 2 + k) for k in range(4)]
        d = [q[k + 1] - q[k] for k in range(3)]
        m0, m1 = minmod(d[0], d[1]), minmod(d[1], d[2])
        g0, g1 = vertical(q[1]), vertical(q[2])
        carry.append((q[2], q[3], d[2], m1, g1, face(lo - 1, q[1], q[2], m0, m1, g0, g1)))
    carry = tuple(carry)
    if hi <= TOP:
        lax.fori_loop(lo, hi + 1, row, carry)
        return
    carry = lax.fori_loop(lo, TOP, row, carry)
    carry = row(TOP, carry, seam=True)
    lax.fori_loop(TOP + 1, hi + 1, row, carry)


def main_kernel(flags, rows, ghost, result, qa, qb, cx, cy):
    top = flags[1] == 1
    for n in TRACERS:
        for k in range(HALO):
            qa[n, k] = ghost[n, k]
            qa[n, TOP + 1 + k] = ghost[n, HALO + k]

        def copy(j, _):
            qa[n, HALO + j] = rows[n, j]
            return 0

        lax.fori_loop(0, HEIGHT, copy, 0, unroll=4)

    def faces(j, _):
        store_x(cx, HALO + j, *(rows[f, j] for f in XF))
        store_y(cy, HALO + j, *(rows[f, j] for f in YF))
        return 0

    lax.fori_loop(0, HEIGHT, faces, 0, unroll=2)

    def low(k, _):
        store_x(cx, k, *(ghost[f, k] for f in XF))
        return 0

    lax.fori_loop(2, HALO, low, 0)

    def high(k, _):
        x = [ghost[f, HALO + k] for f in XF]
        store_x(cx, TOP + 1 + k, *(jnp.where(top, roll(y, -1), y) for y in x))
        store_y(cy, TOP + 1 + k, *(ghost[f, HALO + k] for f in YF))
        return 0

    lax.fori_loop(0, HALO - 2, high, 0)

    def low_y(k, _):
        store_y(cy, k, *(ghost[f, k] for f in YF))
        return 0

    lax.fori_loop(0, HALO, low_y, 0)
    for step in range(STEPS):
        src, dst = (qa, qb) if step % 2 == 0 else (qb, qa)
        lo, hi = 2 * (step + 1), EXT - 1 - 2 * (step + 1)
        last = step == STEPS - 1

        def read(n, idx, src=src):
            return src[n, idx]

        def write(n, idx, x, dst=dst, last=last):
            if last:
                result[n, idx - HALO] = x
            else:
                dst[n, idx] = x

        sweep(read, write, cx, cy, lo, hi, 2)


def edge_kernel(flags, rows, ghost, odd_strip, even_strip, result, temp, salt, qa, qb, cx, cy):
    top, swap = flags[1] == 1, flags[2] == 1
    lane = lanes(128)
    first = lane < 64

    def within(lo, hi):
        return (lane >= lo) & (lane < hi)

    in_left, in_w, in_e, in_right = within(8, 16), within(16, 32), within(32, 48), within(48, 56)
    for idx in range(EXT):
        r, half = idx % (EXT // 2), idx // (EXT // 2)
        a, b = odd_strip[r], even_strip[r]
        left, right = jnp.where(swap, b, a), jnp.where(swap, a, b)
        base = []
        for f in range(8):
            if idx < HALO:
                x = ghost[f, idx]
            elif idx <= TOP:
                x = rows[f, idx - HALO]
            else:
                x = ghost[f, idx - HEIGHT]
            s = 8 * (f + 8 * half)
            y = jnp.where(in_w, roll(x[:, :128], 16), roll(x[:, 128:], 48))
            y = jnp.where(in_left, roll(left, 8 - s), y)
            y = jnp.where(in_right, roll(right, 48 - s), y)
            base.append(y)
        qa[0, idx] = jnp.where(first, base[0], roll(base[1], 64))

        def both(y):
            return jnp.where(first, y, roll(y, 64))

        if 2 <= idx < EXT - 2:
            x = [both(base[f]) for f in XF]
            if idx > TOP:
                x = [jnp.where(top, roll(y, -1), y) for y in x]
            store_x(cx, idx, *x)
        if idx < EXT - 2:
            store_y(cy, idx, *(both(base[f]) for f in YF))
    for step in range(STEPS):
        src, dst = (qa, qb) if step % 2 == 0 else (qb, qa)
        lo, hi = 2 * (step + 1), EXT - 1 - 2 * (step + 1)

        def read(n, idx, src=src):
            return src[n, idx]

        def write(n, idx, x, dst=dst):
            dst[n, idx] = x

        sweep(read, write, cx, cy, lo, hi, 1)

    def patch(j, _):
        e = qa[0, HALO + j]
        for n, out in enumerate((temp, salt)):
            x = result[n, j]
            w = jnp.where(lane < 8, roll(e, -16 - 64 * n), x[:, :128])
            z = jnp.where(lane >= 120, roll(e, 80 - 64 * n), x[:, 128:])
            for at, y in zip(places(j), (w, z)):
                out[at, :] = y
        return 0

    lax.fori_loop(0, HEIGHT, patch, 0, unroll=4)


def call(kernel, outs, args, scratch=()):
    return pl.pallas_call(
        kernel,
        out_shape=[jax.ShapeDtypeStruct(s, F32) for s in outs],
        in_specs=[SMEM] + [VMEM] * (len(args) - 1),
        out_specs=[VMEM] * len(outs),
        scratch_shapes=[pltpu.VMEM(s, F32) for s in scratch],
        compiler_params=PARAMS,
    )(*args)


def on_device(lon_count, lat_count, *args):
    lon, lat = lax.axis_index("lon"), lax.axis_index("lat")
    flags = jnp.stack([lat % 2, (lat == lat_count - 1).astype(jnp.int32), lon % 2])
    flat = [level_major(x) for x in args]

    def index(i, j):
        return i * lat_count + j

    lons, lats = range(lon_count), range(lat_count)
    lat_even = [(index(i, j), index(i, j ^ 1)) for i in lons for j in lats]
    lat_odd = [
        (index(i, j), index(lon_count - 1 - i, j) if j == lat_count - 1 else index(i, j + 1 if j % 2 else j - 1))
        for i in lons
        for j in lats
        if j > 0
    ]
    lon_even = [(i, i ^ 1) for i in lons]
    lon_odd = [(i, (i + 1 if i % 2 else i - 1) % lon_count) for i in lons]
    row = (LEVELS, WIDTH)
    rows, odd_msg, even_msg = call(
        pack_kernel, [(8, HEIGHT, *row), (MESSAGE, *row), (MESSAGE, *row)], [flags, *flat]
    )
    odd_in = lax.ppermute(odd_msg, ("lon", "lat"), lat_odd)
    even_in = lax.ppermute(even_msg, ("lon", "lat"), lat_even)
    strip = (EXT // 2, LEVELS, 128)
    ghost, odd_strip, even_strip = call(
        ghost_kernel, [(8, 2 * HALO, *row), strip, strip], [flags, rows, odd_in, even_in]
    )
    odd_strip = lax.ppermute(odd_strip, "lon", lon_odd)
    even_strip = lax.ppermute(even_strip, "lon", lon_even)
    state = (2, EXT, *row)
    (result,) = call(
        main_kernel,
        [(2, HEIGHT, *row)],
        [flags, rows, ghost],
        [state, state, (6, EXT, *row), (5, EXT, *row)],
    )
    tile = (LEVELS, 128)
    temp, salt = call(
        edge_kernel,
        [(2 * LEVELS * HEIGHT, 128)] * 2,
        [flags, rows, ghost, odd_strip, even_strip, result],
        [(1, EXT, *tile), (1, EXT, *tile), (6, EXT, *tile), (5, EXT, *tile)],
    )
    return from_level_major(temp), from_level_major(salt)


def solution(mesh):
    spec = P(None, "lat", "lon")
    return jax.shard_map(
        functools.partial(on_device, mesh.shape["lon"], mesh.shape["lat"]),
        mesh=mesh,
        in_specs=(spec,) * 9,
        out_specs=(spec, spec),
        check_vma=False,
    )
```

```python
import functools

import jax
import jax.numpy as jnp
from jax import lax
from jax.experimental import pallas as pl
from jax.experimental.pallas import tpu as pltpu
from jax.sharding import PartitionSpec as P

STEPS = 4
HALO = 2 * STEPS
LEVELS = 8
HEIGHT = 32
WIDTH = 256
EXT = HEIGHT + 2 * HALO
TOP = HALO + HEIGHT - 1
F32 = jnp.float32
VMEM = pl.BlockSpec(memory_space=pltpu.VMEM)
SMEM = pl.BlockSpec(memory_space=pltpu.SMEM)
PARAMS = pltpu.CompilerParams(vmem_limit_bytes=20 * 2**20)
COST = pl.CostEstimate(flops=50_000_000, bytes_accessed=8_000_000, transcendentals=0)

TRACERS, XF, YF = (0, 1), (2, 3, 4), (5, 6, 7)
MESSAGE = 2 * 8 + 3 * 6 + 3 * 7


def slot(field, k):
    if field < 2:
        return field * 8 + k
    if field < 5:
        return 16 + (field - 2) * 6 + k
    return 34 + (field - 5) * 7 + k


def rows_of(field):
    return 8 if field < 2 else 6 if field < 5 else 7


def level_major(x):
    x = x.reshape(LEVELS, HEIGHT // 8, 8, WIDTH // 128, 128)
    return x.transpose(0, 1, 3, 2, 4).reshape(-1, 128)


def from_level_major(x):
    x = x.reshape(LEVELS, HEIGHT // 8, WIDTH // 128, 8, 128)
    return x.transpose(0, 1, 3, 2, 4).reshape(LEVELS, HEIGHT, WIDTH)


def places(j):
    start = (j // 8) * 16 + j % 8
    return [pl.ds(start + 8 * c, LEVELS, stride=2 * HEIGHT) for c in range(2)]


def load_row(ref, j):
    return jnp.concatenate([ref[at, :] for at in places(j)], axis=1)


def lanes(width):
    return lax.broadcasted_iota(jnp.int32, (LEVELS, width), 1)


def roll(x, by):
    return pltpu.roll(x, by % x.shape[-1], 1)


def pack_kernel(flags, *refs):
    args, (rows, odd_msg, even_msg), held, sems = refs[:9], refs[9:12], refs[12:21], refs[21]
    copies = [pltpu.make_async_copy(x, y, sems.at[n]) for n, (x, y) in enumerate(zip(args, held))]
    for copy in copies:
        copy.start()
    for copy in copies:
        copy.wait()
    temp, salt, u, v, diff, sx, sy, mu, mv = held

    def one(j, _):
        wet_u, wet_v = load_row(mu, j).astype(F32), load_row(mv, j).astype(F32)
        r = load_row(diff, j)
        rows[0, j] = load_row(temp, j)
        rows[1, j] = load_row(salt, j)
        rows[2, j] = load_row(u, j) * wet_u
        rows[3, j] = r * wet_u
        rows[4, j] = load_row(sx, j)
        rows[5, j] = load_row(v, j) * wet_v
        rows[6, j] = r * wet_v
        rows[7, j] = load_row(sy, j)
        return 0

    lax.fori_loop(0, HEIGHT, one, 0, unroll=4)
    odd = flags[0]
    for f in range(8):
        n = rows_of(f)
        north = HEIGHT - n

        def two(k, _, f=f, north=north):
            odd_msg[slot(f, k)] = rows[f, odd * north + k]
            even_msg[slot(f, k)] = rows[f, (1 - odd) * north + k]
            return 0

        lax.fori_loop(0, n, two, 0, unroll=n)


def mirrored(x):
    n = x.shape[-1] // 128
    back = 127 - lanes(128)
    parts = [x[:, 128 * i : 128 * (i + 1)] for i in range(n)]
    return jnp.concatenate([jnp.take_along_axis(p, back, axis=1) for p in reversed(parts)], axis=1)


def ghost_kernel(flags, rows, odd_msg, even_msg, _, ghost, odd_strip, even_strip):
    odd, top, lon_odd = flags[0], flags[1], flags[2]
    is_odd = odd == 1
    for f in range(8):
        n = rows_of(f)
        for k in range(n):
            a, b = odd_msg[slot(f, k)], even_msg[slot(f, k)]
            ghost[f, HALO - n + k] = jnp.where(is_odd, b, a)
            if k < n - (f >= 5):
                ghost[f, HALO + k] = jnp.where(is_odd, a, b)
        if f >= 5:
            ghost[f, 0] = rows[f, HEIGHT - 1]

    @pl.when(top == 1)
    def _():
        for f in range(8):
            n = rows_of(f)
            sign = -1.0 if f in (2, 4, 5, 7) else 1.0
            for k in range(n):
                x = mirrored(odd_msg[slot(f, n - 1 - k)]) * sign
                if f < 5:
                    ghost[f, HALO + k] = x
                elif k == 0:
                    ghost[f, 0] = x
                else:
                    ghost[f, HALO + k - 1] = x

    lane = lanes(128)
    swap = lon_odd == 1
    for r in range(EXT // 2):
        even_out = jnp.zeros((LEVELS, 128), F32)
        odd_out = jnp.zeros((LEVELS, 128), F32)
        for half in range(2):
            idx = r + half * (EXT // 2)
            for f in range(8):
                if idx < HALO:
                    x = ghost[f, idx]
                elif idx <= TOP:
                    x = rows[f, idx - HALO]
                else:
                    x = ghost[f, idx - HEIGHT]
                s = 8 * (f + 8 * half)
                west, east = roll(x[:, :128], s), roll(x[:, 128:], s + 8)
                here = (lane >= s) & (lane < s + 8)
                even_out = jnp.where(here, jnp.where(swap, west, east), even_out)
                odd_out = jnp.where(here, jnp.where(swap, east, west), odd_out)
        even_strip[r] = even_out
        odd_strip[r] = odd_out


def minmod(p, t):
    return jnp.maximum(jnp.minimum(p, t), jnp.minimum(jnp.maximum(p, t), 0.0))


def vertical(q):
    level = lax.broadcasted_iota(jnp.int32, q.shape, 0)
    up = jnp.where(level == LEVELS - 1, q, pltpu.roll(q, LEVELS - 1, 0))
    down = jnp.where(level == 0, q, pltpu.roll(q, 1, 0))
    return up - down


def shifted(tiles, by):
    lane = lanes(128)
    rolled = [roll(t, by) for t in tiles]
    if len(tiles) == 1:
        return rolled
    seam = lane == (0 if by == 1 else 127)
    return [jnp.where(seam, rolled[1 - n], rolled[n]) for n in range(2)]


def coefficients(c, r, s):
    plus, minus = jnp.maximum(c, 0.0), jnp.minimum(c, 0.0)
    return (
        plus + r,
        0.5 * plus * (1.0 - plus),
        0.25 * r * s,
        minus - r,
        -0.5 * minus * (1.0 + minus),
    )


def store_x(cx, idx, c, r, s):
    p, lp, t, e, ln = coefficients(c, r, s)
    for n, x in enumerate((p, lp, t, roll(e, 1), roll(ln, 1), roll(t, 1))):
        cx[n, idx] = x


def store_y(cy, idx, c, r, s):
    for n, x in enumerate(coefficients(c, r, s)):
        cy[n, idx] = x


def sweep(read, write, cx, cy, first, count, streams, tiles, chunk, seam):
    every = [(n, t) for n in range(streams) for t in range(tiles)]

    def at(ref, n, idx, t):
        return ref[n, idx, :, 128 * t : 128 * (t + 1)]

    def face(idx, t, q0, q1, m0, m1, g0, g1):
        c = [at(cy, n, idx, t) for n in range(5)]
        return (c[0] * q0 + c[3] * q1) + (c[1] * m0 + c[4] * m1) + c[2] * (g0 + g1)

    def row(idx, carry):
        out = []
        for n in range(streams):
            q0 = [carry[n * tiles + t][0] for t in range(tiles)]
            d = [x - y for x, y in zip(shifted(q0, -1), q0)]
            m = [minmod(x, y) for x, y in zip(d, shifted(d, 1))]
            a, b = [], []
            for t in range(tiles):
                g0 = carry[n * tiles + t][4]
                c = [at(cx, k, idx, t) for k in range(6)]
                a.append(c[0] * q0[t] + c[1] * m[t] + c[2] * g0)
                b.append(c[3] * q0[t] + c[4] * m[t] + c[5] * g0)
            x = [(b[t] - a[t]) + (p - r) for t, (p, r) in enumerate(zip(shifted(a, 1), shifted(b, -1)))]
            for t in range(tiles):
                q0, q1, d0, m0, g0, south = carry[n * tiles + t]
                q2 = read(n, idx + 2, t)
                d1 = q2 - q1
                m1 = minmod(d0, d1)
                g1 = vertical(q1)
                north = face(idx, t, q0, q1, m0, m1, g0, g1)
                write(n, idx, t, q0 + x[t] + (south - north))
                if seam and idx == TOP:
                    north = face(0, t, q0, q1, m0, m1, g0, g1)
                out.append((q1, q2, d1, m1, g1, north))
        return tuple(out)

    carry = []
    for n, t in every:
        q = [read(n, first - 2 + k, t) for k in range(4)]
        d = [q[k + 1] - q[k] for k in range(3)]
        m0, m1 = minmod(d[0], d[1]), minmod(d[1], d[2])
        g0, g1 = vertical(q[1]), vertical(q[2])
        carry.append((q[2], q[3], d[2], m1, g1, face(first - 1, t, q[1], q[2], m0, m1, g0, g1)))

    def several(i, carry):
        for k in range(chunk):
            carry = row(first + i * chunk + k, carry)
        return carry

    if count == 1:
        several(0, tuple(carry))
    else:
        lax.fori_loop(0, count, several, tuple(carry))


def window(src, dst, cx, cy, first, count, streams, tiles, chunk, seam=False):
    def read(n, idx, t):
        return src[n, idx, :, 128 * t : 128 * (t + 1)]

    def write(n, idx, t, x):
        dst[n, idx, :, 128 * t : 128 * (t + 1)] = x

    sweep(read, write, cx, cy, first, count, streams, tiles, chunk, seam)


def inner_kernel(rows, s1, s2, s3, s4, s0, cx, cy):
    def own(j, _):
        for n in TRACERS:
            s0[n, HALO + j] = rows[n, j]
        store_x(cx, HALO + j, *(rows[f, j] for f in XF))
        store_y(cy, HALO + j, *(rows[f, j] for f in YF))
        return 0

    lax.fori_loop(0, HEIGHT, own, 0, unroll=4)
    for src, dst, first, count in ((s0, s1, 0, 4), (s1, s2, 4, 3), (s2, s3, 4, 3), (s3, s4, 8, 2)):
        window(src, dst, cx, cy, HALO + first, count, 2, 2, 8)


def edges_of(x, in_w):
    return jnp.where(in_w, roll(x[:, :128], 16), roll(x[:, 128:], 48))


def within(lo, hi):
    lane = lanes(128)
    return (lane >= lo) & (lane < hi)


def outer_kernel(flags, rows, ghost, i1, i2, i3, i4, result, base, s0, s1, s2, s3, s4, cx, cy):
    top = flags[1] == 1
    in_w = within(16, 32)

    def near(k, _):
        for f in range(8):
            base[f, HALO + k] = edges_of(rows[f, k], in_w)
        for start in (0, HEIGHT - HALO):
            j = start + k
            for n in TRACERS:
                s0[n, HALO + j] = rows[n, j]
            store_x(cx, HALO + j, *(rows[f, j] for f in XF))
            store_y(cy, HALO + j, *(rows[f, j] for f in YF))
        return 0

    lax.fori_loop(0, HALO, near, 0, unroll=2)
    store_y(cy, TOP - HALO, *(rows[f, HEIGHT - HALO - 1] for f in YF))

    def beyond(k, _):
        to = jnp.where(k < HALO, k, HEIGHT + k)
        for f in range(8):
            base[f, to] = edges_of(ghost[f, k], in_w)
        for n in TRACERS:
            s0[n, to] = ghost[n, k]
        x = [ghost[f, k] for f in XF]
        turn = top & (k >= HALO)
        store_x(cx, to, *(jnp.where(turn, roll(y, -1), y) for y in x))
        store_y(cy, to, *(ghost[f, k] for f in YF))
        return 0

    lax.fori_loop(0, 2 * HALO, beyond, 0, unroll=2)

    def rest(j, _):
        for f in range(8):
            base[f, HALO + j] = edges_of(rows[f, j], in_w)
        return 0

    lax.fori_loop(HALO, HEIGHT, rest, 0, unroll=4)
    states = (s0, s1, s2, s3, s4)
    inner = (None, i1, i2, i3, None)
    for step in range(1, STEPS + 1):
        src, dst = states[step - 1], states[step]
        if inner[step - 1] is not None:
            for n in TRACERS:
                for k in range(4):
                    low = 2 * step + HALO - 2 + k
                    high = EXT - 1 - low
                    src[n, low] = inner[step - 1][n, low]
                    src[n, high] = inner[step - 1][n, high]
        window(src, dst, cx, cy, 2 * step, 1, 2, 2, 8)
        window(src, dst, cx, cy, EXT - 8 - 2 * step, 1, 2, 2, 8, seam=step < STEPS)

    def out(j, _):
        for n in TRACERS:
            result[n, j] = s4[n, HALO + j]
            result[n, HEIGHT - HALO + j] = s4[n, HEIGHT + j]
            result[n, HALO + j] = i4[n, 2 * HALO + j]
            result[n, 2 * HALO + j] = i4[n, 3 * HALO + j]
        return 0

    lax.fori_loop(0, HALO, out, 0, unroll=2)


def edge_kernel(flags, base, odd_strip, even_strip, result, temp, salt, qa, qb, cx, cy):
    top, swap = flags[1] == 1, flags[2] == 1
    lane = lanes(128)
    first = lane < 64
    in_left, in_right = within(8, 16), within(48, 56)

    def both(y):
        return jnp.where(first, y, roll(y, 64))

    half_rows = EXT // 2

    def assemble(r, _):
        a, b = odd_strip[r], even_strip[r]
        left, right = jnp.where(swap, b, a), jnp.where(swap, a, b)
        for half in range(2):
            to = r + half * half_rows
            y = []
            for f in range(8):
                s = 8 * (f + 8 * half)
                x = jnp.where(in_left, roll(left, 8 - s), base[f, to])
                y.append(jnp.where(in_right, roll(right, 48 - s), x))
            qa[0, to] = jnp.where(first, y[0], roll(y[1], 64))
            x = [both(y[f]) for f in XF]
            if half == 1:
                turn = top & (to > TOP)
                x = [jnp.where(turn, roll(z, -1), z) for z in x]
            store_x(cx, to, *x)
            store_y(cy, to, *(both(y[f]) for f in YF))
        return 0

    lax.fori_loop(0, half_rows, assemble, 0, unroll=2)

    def two(_, c):
        for src, dst in ((qa, qb), (qb, qa)):
            window(src, dst, cx, cy, 2, 1, 1, 1, EXT - 4, seam=True)
        return c

    lax.fori_loop(0, STEPS // 2, two, 0)

    def patch(j, _):
        e = qa[0, HALO + j]
        for n, out in enumerate((temp, salt)):
            x = result[n, j]
            w = jnp.where(lane < 8, roll(e, -16 - 64 * n), x[:, :128])
            z = jnp.where(lane >= 120, roll(e, 80 - 64 * n), x[:, 128:])
            for at, y in zip(places(j), (w, z)):
                out[at, :] = y
        return 0

    lax.fori_loop(0, HEIGHT, patch, 0, unroll=4)


def call(kernel, outs, args, scratch=(), args_in=VMEM, flags=None):
    first = [] if flags is None else [flags]
    return pl.pallas_call(
        kernel,
        out_shape=[jax.ShapeDtypeStruct(s, F32) for s in outs],
        in_specs=[SMEM] * len(first) + [args_in] * len(args),
        out_specs=[VMEM] * len(outs),
        scratch_shapes=[pltpu.VMEM(s, F32) if isinstance(s, tuple) else s for s in scratch],
        compiler_params=PARAMS,
        cost_estimate=COST,
    )(*first, *args)


ROW = (LEVELS, WIDTH)
TILE = (LEVELS, 128)
STRIP = (EXT // 2, *TILE)
STATE = (2, EXT, *ROW)
FLAT = (2 * LEVELS * HEIGHT, 128)


def pack(flags, args):
    held = [pltpu.VMEM(FLAT, x.dtype) for x in args]
    return call(
        pack_kernel,
        [(8, HEIGHT, *ROW), (MESSAGE, *ROW), (MESSAGE, *ROW)],
        args,
        [*held, pltpu.SemaphoreType.DMA((9,))],
        pl.BlockSpec(memory_space=pltpu.HBM),
        flags,
    )


def inner(rows):
    return call(inner_kernel, [STATE] * 4, [rows], [STATE, (6, EXT, *ROW), (5, EXT, *ROW)])


def fill_ghost(flags, rows, odd_in, even_in, after):
    return call(ghost_kernel, [(8, 2 * HALO, *ROW), STRIP, STRIP], [rows, odd_in, even_in, after], flags=flags)


def outer(flags, rows, ghost, states):
    return call(
        outer_kernel,
        [(2, HEIGHT, *ROW), (8, EXT, *TILE)],
        [rows, ghost, *states],
        [STATE] * 5 + [(6, EXT, *ROW), (5, EXT, *ROW)],
        flags=flags,
    )


def edge(flags, base, odd_strip, even_strip, result):
    return call(
        edge_kernel,
        [FLAT] * 2,
        [base, odd_strip, even_strip, result],
        [(1, EXT, *TILE)] * 2 + [(6, EXT, *TILE), (5, EXT, *TILE)],
        flags=flags,
    )


def on_device(lon_count, lat_count, *args):
    lon, lat = lax.axis_index("lon"), lax.axis_index("lat")
    flags = jnp.stack([lat % 2, (lat == lat_count - 1).astype(jnp.int32), lon % 2])
    flat = [level_major(x) for x in args]

    def index(i, j):
        return i * lat_count + j

    lons, lats = range(lon_count), range(lat_count)
    lat_even = [(index(i, j), index(i, j ^ 1)) for i in lons for j in lats]
    lat_odd = [
        (index(i, j), index(lon_count - 1 - i, j) if j == lat_count - 1 else index(i, j + 1 if j % 2 else j - 1))
        for i in lons
        for j in lats
        if j > 0
    ]
    lon_even = [(i, i ^ 1) for i in lons]
    lon_odd = [(i, (i + 1 if i % 2 else i - 1) % lon_count) for i in lons]
    flat = [pltpu.with_memory_space_constraint(x, pltpu.HBM) for x in flat]
    rows, odd_msg, even_msg = pack(flags, flat)
    odd_in = lax.ppermute(odd_msg, ("lon", "lat"), lat_odd)
    even_in = lax.ppermute(even_msg, ("lon", "lat"), lat_even)
    states = inner(rows)
    ghost, odd_strip, even_strip = fill_ghost(flags, rows, odd_in, even_in, states[3])
    odd_strip = lax.ppermute(odd_strip, "lon", lon_odd)
    even_strip = lax.ppermute(even_strip, "lon", lon_even)
    result, base = outer(flags, rows, ghost, states)
    temp, salt = edge(flags, base, odd_strip, even_strip, result)
    return from_level_major(temp), from_level_major(salt)


def solution(mesh):
    spec = P(None, "lat", "lon")
    return jax.shard_map(
        functools.partial(on_device, mesh.shape["lon"], mesh.shape["lat"]),
        mesh=mesh,
        in_specs=(spec,) * 9,
        out_specs=(spec, spec),
        check_vma=False,
    )
```

```python
import functools

import jax
import jax.numpy as jnp
from jax import lax
from jax.experimental import pallas as pl
from jax.experimental.pallas import tpu as pltpu
from jax.sharding import PartitionSpec as P

STEPS = 4
HALO = 2 * STEPS
PAD = 4
LEVELS = 8
HEIGHT = 32
WIDTH = 256
EXT = HEIGHT + 2 * HALO
TOP = HALO + HEIGHT - 1
EDGE_DEPTH = EXT + 2 * PAD
F32 = jnp.float32
VMEM = pl.BlockSpec(memory_space=pltpu.VMEM)
SMEM = pl.BlockSpec(memory_space=pltpu.SMEM)
PARAMS = pltpu.CompilerParams(vmem_limit_bytes=20 * 2**20)
COST = pl.CostEstimate(flops=50_000_000, bytes_accessed=8_000_000, transcendentals=0)

TRACERS, XF, YF = (0, 1), (2, 3, 4), (5, 6, 7)
MESSAGE = 2 * 8 + 3 * 6 + 3 * 7


def slot(field, k):
    if field < 2:
        return field * 8 + k
    if field < 5:
        return 16 + (field - 2) * 6 + k
    return 34 + (field - 5) * 7 + k


def rows_of(field):
    return 8 if field < 2 else 6 if field < 5 else 7


def level_major(x):
    x = x.reshape(LEVELS, HEIGHT // 8, 8, WIDTH // 128, 128)
    return x.transpose(0, 1, 3, 2, 4).reshape(-1, 128)


def from_level_major(x):
    x = x.reshape(LEVELS, HEIGHT // 8, WIDTH // 128, 8, 128)
    return x.transpose(0, 1, 3, 2, 4).reshape(LEVELS, HEIGHT, WIDTH)


def places(j):
    start = (j // 8) * 16 + j % 8
    return [pl.ds(start + 8 * c, LEVELS, stride=2 * HEIGHT) for c in range(2)]


def load_row(ref, j):
    return jnp.concatenate([ref[at, :] for at in places(j)], axis=1)


def lanes(width):
    return lax.broadcasted_iota(jnp.int32, (LEVELS, width), 1)


def within(lo, hi):
    lane = lanes(128)
    return (lane >= lo) & (lane < hi)


def roll(x, by):
    return pltpu.roll(x, by % x.shape[-1], 1)


def pack_kernel(flags, *refs):
    args, (rows, odd_msg, even_msg), held, sems = refs[:9], refs[9:12], refs[12:21], refs[21]
    copies = [pltpu.make_async_copy(x, y, sems.at[n]) for n, (x, y) in enumerate(zip(args, held))]
    for copy in copies:
        copy.start()
    for copy in copies:
        copy.wait()
    temp, salt, u, v, diff, sx, sy, mu, mv = held

    def one(j, _):
        wet_u, wet_v = load_row(mu, j).astype(F32), load_row(mv, j).astype(F32)
        r = load_row(diff, j)
        rows[0, j] = load_row(temp, j)
        rows[1, j] = load_row(salt, j)
        rows[2, j] = load_row(u, j) * wet_u
        rows[3, j] = r * wet_u
        rows[4, j] = load_row(sx, j)
        rows[5, j] = load_row(v, j) * wet_v
        rows[6, j] = r * wet_v
        rows[7, j] = load_row(sy, j)
        return 0

    lax.fori_loop(0, HEIGHT, one, 0, unroll=4)
    odd = flags[0]
    for f in range(8):
        n = rows_of(f)
        north = HEIGHT - n

        def two(k, _, f=f, north=north):
            odd_msg[slot(f, k)] = rows[f, odd * north + k]
            even_msg[slot(f, k)] = rows[f, (1 - odd) * north + k]
            return 0

        lax.fori_loop(0, n, two, 0, unroll=n)


def mirrored(x):
    n = x.shape[-1] // 128
    back = 127 - lanes(128)
    parts = [x[:, 128 * i : 128 * (i + 1)] for i in range(n)]
    return jnp.concatenate([jnp.take_along_axis(p, back, axis=1) for p in reversed(parts)], axis=1)


def ghost_kernel(flags, rows, odd_msg, even_msg, _, ghost, odd_strip, even_strip):
    odd, top, lon_odd = flags[0], flags[1], flags[2]
    is_odd = odd == 1
    for f in range(8):
        n = rows_of(f)
        for k in range(n):
            a, b = odd_msg[slot(f, k)], even_msg[slot(f, k)]
            ghost[f, HALO - n + k] = jnp.where(is_odd, b, a)
            if k < n - (f >= 5):
                ghost[f, HALO + k] = jnp.where(is_odd, a, b)
        if f >= 5:
            ghost[f, 0] = rows[f, HEIGHT - 1]

    @pl.when(top == 1)
    def _():
        for f in range(8):
            n = rows_of(f)
            sign = -1.0 if f in (2, 4, 5, 7) else 1.0
            for k in range(n):
                x = mirrored(odd_msg[slot(f, n - 1 - k)]) * sign
                if f < 5:
                    ghost[f, HALO + k] = x
                elif k == 0:
                    ghost[f, 0] = x
                else:
                    ghost[f, HALO + k - 1] = x

    swap = lon_odd == 1
    for r in range(EXT // 2):
        east, west = jnp.zeros((LEVELS, 128), F32), jnp.zeros((LEVELS, 128), F32)
        for half in range(2):
            idx = r + half * (EXT // 2)
            for f in range(8):
                if idx < HALO:
                    x = ghost[f, idx]
                elif idx <= TOP:
                    x = rows[f, idx - HALO]
                else:
                    x = ghost[f, idx - HEIGHT]
                to = 8 * f + 64 * half
                east = jnp.where(within(to, to + 8), roll(x[:, 128:], to + 8), east)
                to = 8 * f + 64 * (1 - half)
                west = jnp.where(within(to, to + 8), roll(x[:, :128], to), west)
        even_strip[r] = jnp.where(swap, west, east)
        odd_strip[r] = jnp.where(swap, east, west)


def minmod(p, t):
    return jnp.maximum(jnp.minimum(p, t), jnp.minimum(jnp.maximum(p, t), 0.0))


def vertical(q):
    level = lax.broadcasted_iota(jnp.int32, q.shape, 0)
    up = jnp.where(level == LEVELS - 1, q, pltpu.roll(q, LEVELS - 1, 0))
    down = jnp.where(level == 0, q, pltpu.roll(q, 1, 0))
    return up - down


def shifted(tiles, by):
    lane = lanes(128)
    rolled = [roll(t, by) for t in tiles]
    if len(tiles) == 1:
        return rolled
    seam = lane == (0 if by == 1 else 127)
    return [jnp.where(seam, rolled[1 - n], rolled[n]) for n in range(2)]


def coefficients(c, r, s):
    plus, minus = jnp.maximum(c, 0.0), jnp.minimum(c, 0.0)
    return (
        plus + r,
        0.5 * plus * (1.0 - plus),
        0.25 * r * s,
        minus - r,
        -0.5 * minus * (1.0 + minus),
    )


def store_x(cx, idx, c, r, s):
    p, lp, t, e, ln = coefficients(c, r, s)
    for n, x in enumerate((p, lp, t, roll(e, 1), roll(ln, 1), roll(t, 1))):
        cx[n, idx] = x


def store_y(cy, idx, c, r, s):
    for n, x in enumerate(coefficients(c, r, s)):
        cy[n, idx] = x


def rows_forward(src, dst, cx, cy, first, chunk, streams, tiles, seam=False, pad=0):
    def at(ref, n, idx, t):
        return ref[n, pad + idx, :, 128 * t : 128 * (t + 1)]

    def face(idx, t, q0, q1, m0, m1, g0, g1):
        c = [at(cy, n, idx, t) for n in range(5)]
        return (c[0] * q0 + c[3] * q1) + (c[1] * m0 + c[4] * m1) + c[2] * (g0 + g1)

    south = jnp.where(first == TOP + 1, 0, first - 1)
    carry = []
    for n in range(streams):
        for t in range(tiles):
            q = [at(src, n, first - 2 + k, t) for k in range(4)]
            d = [q[k + 1] - q[k] for k in range(3)]
            m0, m1 = minmod(d[0], d[1]), minmod(d[1], d[2])
            g0, g1 = vertical(q[1]), vertical(q[2])
            carry.append((q[2], q[3], d[2], m1, g1, face(south, t, q[1], q[2], m0, m1, g0, g1)))
    for k in range(chunk):
        idx = first + k
        out = []
        for n in range(streams):
            q0 = [carry[n * tiles + t][0] for t in range(tiles)]
            d = [x - y for x, y in zip(shifted(q0, -1), q0)]
            m = [minmod(x, y) for x, y in zip(d, shifted(d, 1))]
            a, b = [], []
            for t in range(tiles):
                g0 = carry[n * tiles + t][4]
                c = [at(cx, i, idx, t) for i in range(6)]
                a.append(c[0] * q0[t] + c[1] * m[t] + c[2] * g0)
                b.append(c[3] * q0[t] + c[4] * m[t] + c[5] * g0)
            x = [(b[t] - a[t]) + (p - r) for t, (p, r) in enumerate(zip(shifted(a, 1), shifted(b, -1)))]
            for t in range(tiles):
                q0, q1, d0, m0, g0, south = carry[n * tiles + t]
                q2 = at(src, n, idx + 2, t)
                d1 = q2 - q1
                m1 = minmod(d0, d1)
                g1 = vertical(q1)
                north = face(idx, t, q0, q1, m0, m1, g0, g1)
                dst[n, pad + idx, :, 128 * t : 128 * (t + 1)] = q0 + x[t] + (south - north)
                if isinstance(idx, int):
                    if idx == TOP and seam:
                        north = face(0, t, q0, q1, m0, m1, g0, g1)
                elif seam and k % 2 == 1 and k < chunk - 1:
                    at_seam = jnp.full((LEVELS, 128), idx, jnp.int32) == TOP
                    north = jnp.where(at_seam, face(0, t, q0, q1, m0, m1, g0, g1), north)
                out.append((q1, q2, d1, m1, g1, north))
        carry = out


def loop(count, body, unroll=1):
    def step(i, _):
        body(i)
        return 0

    lax.fori_loop(0, count, step, 0, unroll=unroll)


SALT = 24


def edges_of(x):
    return jnp.where(within(16, 32), roll(x[:, :128], 16), roll(x[:, 128:], 72))


def inner_kernel(rows, cuts, mid, base, s0, s1, s2, s3, s4, cx, cy):
    def own(j):
        for n in TRACERS:
            s0[n, HALO + j] = rows[n, j]
        x = [rows[f, j] for f in range(8)]
        store_x(cx, HALO + j, *(x[f] for f in XF))
        store_y(cy, HALO + j, *(x[f] for f in YF))
        for f in range(8):
            base[f, j] = edges_of(x[f])

    loop(HEIGHT, own, 4)
    for src, dst, first, count in ((s0, s1, 0, 4), (s1, s2, 4, 3), (s2, s3, 4, 3), (s3, s4, 8, 2)):
        loop(count, lambda i: rows_forward(src, dst, cx, cy, HALO + first + 8 * i, 8, 2, 2))
    for n in TRACERS:
        for step, s in enumerate((s1, s2, s3), 1):
            low = HALO + 2 * step
            for k in range(4):
                cuts[step - 1, n, k] = s[n, low + k]
                cuts[step - 1, n, 4 + k] = s[n, EXT - 4 - low + k]

        def out(j, n=n):
            mid[n, j] = s4[n, 2 * HALO + j]

        loop(2 * HALO, out, 4)


def outer_kernel(flags, rows, ghost, cuts, mid, result, base, qa, qb, cx, cy):
    top = flags[1] == 1

    def near(k):
        for start in (0, HEIGHT - HALO):
            j = start + k
            for n in TRACERS:
                qa[n, HALO + j] = rows[n, j]
            store_x(cx, HALO + j, *(rows[f, j] for f in XF))
            store_y(cy, HALO + j, *(rows[f, j] for f in YF))

    loop(HALO, near, 4)
    store_y(cy, TOP - HALO, *(rows[f, HEIGHT - HALO - 1] for f in YF))

    def beyond(k):
        to = jnp.where(k < HALO, k, HEIGHT + k)
        x = [ghost[f, k] for f in range(8)]
        for f in range(8):
            base[f, k] = edges_of(x[f])
        for n in TRACERS:
            qa[n, to] = x[n]
        turn = top & (k >= HALO)
        store_x(cx, to, *(jnp.where(turn, roll(x[f], -1), x[f]) for f in XF))
        store_y(cy, to, *(x[f] for f in YF))

    loop(2 * HALO, beyond, 4)

    def one(src, dst, step):
        low = HALO + 2 * step
        for n in TRACERS:
            for k in range(4):
                dst[n, low + k] = cuts[step - 1, n, k]
                dst[n, EXT - 4 - low + k] = cuts[step - 1, n, 4 + k]
        loop(2, lambda w: rows_forward(src, dst, cx, cy, 2 * step + w * (EXT - 8 - 4 * step), 8, 2, 2, seam=True))

    def two(i):
        one(qa, qb, 2 * i + 1)
        one(qb, qa, 2 * i + 2)

    loop(STEPS // 2, two)

    def out(j):
        for n in TRACERS:
            result[n, j] = qa[n, HALO + j]
            result[n, HEIGHT - HALO + j] = qa[n, HEIGHT + j]
            result[n, HALO + j] = mid[n, j]
            result[n, 2 * HALO + j] = mid[n, HALO + j]

    loop(HALO, out, 2)


def edge_kernel(flags, base, beyond, odd_strip, even_strip, result, temp, salt, qa, qb, cx, cy):
    top = flags[1] == 1
    lane = lanes(128)
    from_odd = (lane < 64).astype(jnp.int32) != flags[2]
    is_temp = within(8, 32) | within(56, 80)
    beside = within(8, 16) | within(72, 80)

    def both(y):
        return jnp.where(is_temp, y, roll(y, SALT))

    def assemble(ref, k, r, half, turn=None):
        a, b = odd_strip[r], even_strip[r]
        halo = jnp.where(from_odd, a, b) if half == 0 else jnp.where(from_odd, b, a)
        y = [jnp.where(beside, roll(halo, 8 - 8 * f - 64 * half), ref[f, k]) for f in range(8)]
        to = PAD + r + half * (EXT // 2)
        qa[0, to] = jnp.where(is_temp, y[0], roll(y[1], SALT))
        x = [both(y[f]) for f in XF]
        if turn is not None:
            x = [jnp.where(turn, roll(z, -1), z) for z in x]
        store_x(cx, to, *x)
        store_y(cy, to, *(both(y[f]) for f in YF))

    def ghosts(k):
        assemble(beyond, k, k, 0)
        assemble(beyond, HALO + k, 2 * HALO + k, 1, top)

    loop(HALO, ghosts, 4)

    def own(k):
        assemble(base, k, HALO + k, 0)
        assemble(base, 2 * HALO + k, k, 1)

    loop(2 * HALO, own, 4)

    def two(_):
        for src, dst in ((qa, qb), (qb, qa)):
            rows_forward(src, dst, cx, cy, 2, EXT - 4, 1, 1, seam=True, pad=PAD)

    loop(STEPS // 2, two)

    def patch(j):
        e = qa[0, PAD + HALO + j]
        for n, out in enumerate((temp, salt)):
            x = result[n, j]
            w = jnp.where(lane < 8, roll(e, -16 - SALT * n), x[:, :128])
            z = jnp.where(lane >= 120, roll(e, 56 - SALT * n), x[:, 128:])
            for at, y in zip(places(j), (w, z)):
                out[at, :] = y

    loop(HEIGHT, patch, 8)


def call(kernel, outs, args, scratch=(), args_in=VMEM, flags=None):
    first = [] if flags is None else [flags]
    return pl.pallas_call(
        kernel,
        out_shape=[jax.ShapeDtypeStruct(s, F32) for s in outs],
        in_specs=[SMEM] * len(first) + [args_in] * len(args),
        out_specs=[VMEM] * len(outs),
        scratch_shapes=[pltpu.VMEM(s, F32) if isinstance(s, tuple) else s for s in scratch],
        compiler_params=PARAMS,
        cost_estimate=COST,
    )(*first, *args)


ROW = (LEVELS, WIDTH)
TILE = (LEVELS, 128)
STRIP = (EXT // 2, *TILE)
STATE = (2, EXT, *ROW)
FLAT = (2 * LEVELS * HEIGHT, 128)


def pack(flags, args):
    held = [pltpu.VMEM(FLAT, x.dtype) for x in args]
    return call(
        pack_kernel,
        [(8, HEIGHT, *ROW), (MESSAGE, *ROW), (MESSAGE, *ROW)],
        args,
        [*held, pltpu.SemaphoreType.DMA((9,))],
        pl.BlockSpec(memory_space=pltpu.HBM),
        flags,
    )


def inner(rows):
    return call(
        inner_kernel,
        [(STEPS, 2, 8, *ROW), (2, 2 * HALO, *ROW), (8, HEIGHT, *TILE)],
        [rows],
        [STATE] * 5 + [(6, EXT, *ROW), (5, EXT, *ROW)],
    )


def fill_ghost(flags, rows, odd_in, even_in, after):
    return call(
        ghost_kernel, [(8, 2 * HALO, *ROW), STRIP, STRIP], [rows, odd_in, even_in, after], flags=flags
    )


def outer(flags, rows, ghost, cuts, mid):
    return call(
        outer_kernel,
        [(2, HEIGHT, *ROW), (8, 2 * HALO, *TILE)],
        [rows, ghost, cuts, mid],
        [STATE] * 2 + [(6, EXT, *ROW), (5, EXT, *ROW)],
        flags=flags,
    )


def edge(flags, base, beyond, odd_strip, even_strip, result):
    return call(
        edge_kernel,
        [FLAT] * 2,
        [base, beyond, odd_strip, even_strip, result],
        [(1, EDGE_DEPTH, *TILE)] * 2 + [(6, EDGE_DEPTH, *TILE), (5, EDGE_DEPTH, *TILE)],
        flags=flags,
    )


def on_device(lon_count, lat_count, *args):
    lon, lat = lax.axis_index("lon"), lax.axis_index("lat")
    flags = jnp.stack([lat % 2, (lat == lat_count - 1).astype(jnp.int32), lon % 2])
    flat = [level_major(x) for x in args]

    def index(i, j):
        return i * lat_count + j

    lons, lats = range(lon_count), range(lat_count)
    lat_even = [(index(i, j), index(i, j ^ 1)) for i in lons for j in lats]
    lat_odd = [
        (index(i, j), index(lon_count - 1 - i, j) if j == lat_count - 1 else index(i, j + 1 if j % 2 else j - 1))
        for i in lons
        for j in lats
        if j > 0
    ]
    lon_even = [(i, i ^ 1) for i in lons]
    lon_odd = [(i, (i + 1 if i % 2 else i - 1) % lon_count) for i in lons]
    flat = [pltpu.with_memory_space_constraint(x, pltpu.HBM) for x in flat]
    rows, odd_msg, even_msg = pack(flags, flat)
    odd_in = lax.ppermute(odd_msg, ("lon", "lat"), lat_odd)
    even_in = lax.ppermute(even_msg, ("lon", "lat"), lat_even)
    cuts, mid, base = inner(rows)
    ghost, odd_strip, even_strip = fill_ghost(flags, rows, odd_in, even_in, mid)
    odd_strip = lax.ppermute(odd_strip, "lon", lon_odd)
    even_strip = lax.ppermute(even_strip, "lon", lon_even)
    result, beyond = outer(flags, rows, ghost, cuts, mid)
    temp, salt = edge(flags, base, beyond, odd_strip, even_strip, result)
    return from_level_major(temp), from_level_major(salt)


def solution(mesh):
    spec = P(None, "lat", "lon")
    return jax.shard_map(
        functools.partial(on_device, mesh.shape["lon"], mesh.shape["lat"]),
        mesh=mesh,
        in_specs=(spec,) * 9,
        out_specs=(spec, spec),
        check_vma=False,
    )
```

```python
import functools

import jax
import jax.numpy as jnp
from jax import lax
from jax.experimental import pallas as pl
from jax.experimental.pallas import tpu as pltpu
from jax.sharding import PartitionSpec as P

STEPS = 4
HALO = 2 * STEPS
PAD = 4
INNER_FIRST = 4
OUTER_FIRST = 3
LEVELS = 8
HEIGHT = 32
WIDTH = 256
EXT = HEIGHT + 2 * HALO
TOP = HALO + HEIGHT - 1
EDGE_DEPTH = EXT + 2 * PAD
F32 = jnp.float32
VMEM = pl.BlockSpec(memory_space=pltpu.VMEM)
SMEM = pl.BlockSpec(memory_space=pltpu.SMEM)
PARAMS = pltpu.CompilerParams(vmem_limit_bytes=24 * 2**20)
COST = pl.CostEstimate(flops=50_000_000, bytes_accessed=8_000_000, transcendentals=0)

TRACERS, XF, YF = (0, 1), (2, 3, 4), (5, 6, 7)
FLIPPED = (2, 4, 5, 7)
MESSAGE = 2 * 8 + 3 * 6 + 3 * 7


def slot(field, k):
    if field < 2:
        return field * 8 + k
    if field < 5:
        return 16 + (field - 2) * 6 + k
    return 34 + (field - 5) * 7 + k


def rows_of(field):
    return 8 if field < 2 else 6 if field < 5 else 7


def level_major(x):
    x = x.reshape(LEVELS, HEIGHT // 8, 8, WIDTH // 128, 128)
    return x.transpose(0, 1, 3, 2, 4).reshape(-1, 128)


def from_level_major(x):
    x = x.reshape(LEVELS, HEIGHT // 8, WIDTH // 128, 8, 128)
    return x.transpose(0, 1, 3, 2, 4).reshape(LEVELS, HEIGHT, WIDTH)


def places(j):
    start = (j // 8) * 16 + j % 8
    return [pl.ds(start + 8 * c, LEVELS, stride=2 * HEIGHT) for c in range(2)]


def load_row(ref, j):
    return jnp.concatenate([ref[at, :] for at in places(j)], axis=1)


def lanes(width):
    return lax.broadcasted_iota(jnp.int32, (LEVELS, width), 1)


def within(lo, hi):
    lane = lanes(128)
    return (lane >= lo) & (lane < hi)


def roll(x, by):
    return pltpu.roll(x, by % x.shape[-1], 1)


def fields(held, at):
    temp, salt, u, v, diff, sx, sy, mu, mv = (at(ref) for ref in held)
    wet_u, wet_v = mu.astype(F32), mv.astype(F32)
    return temp, salt, u * wet_u, diff * wet_u, sx, v * wet_v, diff * wet_v, sy


def pack_kernel(flags, *refs):
    args, (odd_msg, even_msg, sides), held, sems = refs[:9], refs[9:12], refs[12:21], refs[21]
    copies = []
    for n, (x, y) in enumerate(zip(args, held)):
        for part, start in enumerate((0, 2 * HEIGHT - 16)):
            copies.append(pltpu.make_async_copy(x.at[:, pl.ds(start, 16), :], y.at[part], sems.at[n, part]))
    for copy in copies:
        copy.start()
    for copy in copies:
        copy.wait()

    def fill(part, msg):
        for k in range(8):

            def at(ref):
                flat = ref.at[part].reshape(LEVELS * 16, 128)
                return jnp.concatenate([flat[pl.ds(8 * c + k, LEVELS, stride=16), :] for c in range(2)], axis=1)

            for f, x in enumerate(fields(held, at)):
                to = k - (8 - rows_of(f)) * part
                if 0 <= to < rows_of(f):
                    msg[slot(f, to)] = x

    @pl.when(flags[0] == 1)
    def _():
        fill(1, odd_msg)
        fill(0, even_msg)

    @pl.when(flags[0] == 0)
    def _():
        fill(0, odd_msg)
        fill(1, even_msg)

    @pl.when(flags[1] == 1)
    def _():
        for m in range(9):
            out = jnp.zeros((LEVELS, 128), F32)
            for f in range(8):
                k = 7 - m if f < 2 else 5 - m if m < 8 else 6
                if k < 0 or (m == 8 and f < 5):
                    continue
                x = odd_msg[slot(f, k)]
                west, east = 8 * (7 - f), 8 * (15 - f)
                out = jnp.where(within(west, west + 8), roll(x[:, :128], west), out)
                out = jnp.where(within(east, east + 8), roll(x[:, 128:], -8 * f), out)
            sides[m] = out


def rows_kernel(flags, *refs):
    args, _, outs, held, sems = refs[:9], refs[9], refs[10:14], refs[14:23], refs[23]
    rows, cuts, mid, base = outs
    copies = [pltpu.make_async_copy(x, y, sems.at[n]) for n, (x, y) in enumerate(zip(args, held))]
    for copy in copies:
        copy.start()
    for copy in copies:
        copy.wait()

    def one(j):
        for f, x in enumerate(fields(held, lambda ref: load_row(ref, j))):
            rows[f, j] = x

    loop(HEIGHT, one, 4)

    @pl.when(flags[3] == 1)
    def _():
        inner_part(rows, cuts, mid, base, *refs[24:])


def mirrored(x):
    n = x.shape[-1] // 128
    back = 127 - lanes(128)
    parts = [x[:, 128 * i : 128 * (i + 1)] for i in range(n)]
    return jnp.concatenate([jnp.take_along_axis(p, back, axis=1) for p in reversed(parts)], axis=1)


def fold_rows(msg, ghost):
    for f in range(8):
        n = rows_of(f)
        sign = -1.0 if f in FLIPPED else 1.0
        for k in range(n):
            x = mirrored(msg[slot(f, n - 1 - k)]) * sign
            if f < 5:
                ghost[f, HALO + k] = x
            elif k == 0:
                ghost[f, 0] = x
            else:
                ghost[f, HALO + k - 1] = x


def ghost_kernel(flags, rows, odd_msg, even_msg, sides, cuts, mid, ghost, odd_strip, even_strip, result, base, *scratch):
    is_odd = flags[0] == 1
    for f in range(8):
        n = rows_of(f)
        for k in range(n):
            a, b = odd_msg[slot(f, k)], even_msg[slot(f, k)]
            ghost[f, HALO - n + k] = jnp.where(is_odd, b, a)
            if k < n - (f >= 5):
                ghost[f, HALO + k] = jnp.where(is_odd, a, b)
        if f >= 5:
            ghost[f, 0] = rows[f, HEIGHT - 1]

    swap = flags[2] == 1
    for r in range(EXT // 2):
        east, west = jnp.zeros((LEVELS, 128), F32), jnp.zeros((LEVELS, 128), F32)
        for half in range(2):
            idx = r + half * (EXT // 2)
            for f in range(8):
                if idx < HALO:
                    x = ghost[f, idx]
                elif idx <= TOP:
                    x = rows[f, idx - HALO]
                else:
                    x = ghost[f, idx - HEIGHT]
                to = 8 * f + 64 * half
                east = jnp.where(within(to, to + 8), roll(x[:, 128:], to + 8), east)
                to = 8 * f + 64 * (1 - half)
                west = jnp.where(within(to, to + 8), roll(x[:, :128], to), west)
        even_strip[r] = jnp.where(swap, west, east)
        odd_strip[r] = jnp.where(swap, east, west)

    @pl.when(flags[1] == 1)
    def _():
        lane = lanes(128)
        field = (lane // 8) % 8
        flip = (field == 2) | (field == 4) | (field == 5) | (field == 7)
        for m in range(9):
            x = jnp.take_along_axis(sides[m], 127 - lane, axis=1)
            x = jnp.where(flip, -x, x)
            r = 2 * HALO + m
            in_east, in_west = lane >= 64, lane < 64
            if m == 8:
                r, x = 0, roll(x, 64)
                in_east, in_west = within(40, 64), within(104, 128)
            a, b = even_strip[r], odd_strip[r]
            east = jnp.where(in_east, x, jnp.where(swap, b, a))
            west = jnp.where(in_west, x, jnp.where(swap, a, b))
            even_strip[r] = jnp.where(swap, west, east)
            odd_strip[r] = jnp.where(swap, east, west)

    @pl.when(flags[4] == 1)
    def _():
        outer_part(flags, rows, ghost, cuts, mid, result, base, *scratch)


def minmod(p, t):
    return jnp.maximum(jnp.minimum(p, t), jnp.minimum(jnp.maximum(p, t), 0.0))


def vertical(q):
    level = lax.broadcasted_iota(jnp.int32, q.shape, 0)
    up = jnp.where(level == LEVELS - 1, q, pltpu.roll(q, LEVELS - 1, 0))
    down = jnp.where(level == 0, q, pltpu.roll(q, 1, 0))
    return up - down


def shifted(tiles, by):
    lane = lanes(128)
    rolled = [roll(t, by) for t in tiles]
    if len(tiles) == 1:
        return rolled
    seam = lane == (0 if by == 1 else 127)
    return [jnp.where(seam, rolled[1 - n], rolled[n]) for n in range(2)]


def coefficients(c, r, s):
    plus, minus = jnp.maximum(c, 0.0), jnp.minimum(c, 0.0)
    return (
        plus + r,
        0.5 * plus * (1.0 - plus),
        0.25 * r * s,
        minus - r,
        -0.5 * minus * (1.0 + minus),
    )


def store_x(cx, idx, c, r, s):
    p, lp, t, e, ln = coefficients(c, r, s)
    for n, x in enumerate((p, lp, t, roll(e, 1), roll(ln, 1), roll(t, 1))):
        cx[n, idx] = x


def store_y(cy, idx, c, r, s):
    for n, x in enumerate(coefficients(c, r, s)):
        cy[n, idx] = x


def rows_forward(src, dst, cx, cy, first, chunk, streams, tiles, seam=False, pad=0):
    def at(ref, n, idx, t):
        return ref[n, pad + idx, :, 128 * t : 128 * (t + 1)]

    def face(idx, t, q0, q1, m0, m1, g0, g1):
        c = [at(cy, n, idx, t) for n in range(5)]
        return (c[0] * q0 + c[3] * q1) + (c[1] * m0 + c[4] * m1) + c[2] * (g0 + g1)

    south = jnp.where(first == TOP + 1, 0, first - 1)
    carry = []
    for n in range(streams):
        for t in range(tiles):
            q = [at(src, n, first - 2 + k, t) for k in range(4)]
            d = [q[k + 1] - q[k] for k in range(3)]
            m0, m1 = minmod(d[0], d[1]), minmod(d[1], d[2])
            g0, g1 = vertical(q[1]), vertical(q[2])
            carry.append((q[2], q[3], d[2], m1, g1, face(south, t, q[1], q[2], m0, m1, g0, g1)))
    for k in range(chunk):
        idx = first + k
        out = []
        for n in range(streams):
            q0 = [carry[n * tiles + t][0] for t in range(tiles)]
            d = [x - y for x, y in zip(shifted(q0, -1), q0)]
            m = [minmod(x, y) for x, y in zip(d, shifted(d, 1))]
            a, b = [], []
            for t in range(tiles):
                g0 = carry[n * tiles + t][4]
                c = [at(cx, i, idx, t) for i in range(6)]
                a.append(c[0] * q0[t] + c[1] * m[t] + c[2] * g0)
                b.append(c[3] * q0[t] + c[4] * m[t] + c[5] * g0)
            x = [(b[t] - a[t]) + (p - r) for t, (p, r) in enumerate(zip(shifted(a, 1), shifted(b, -1)))]
            for t in range(tiles):
                q0, q1, d0, m0, g0, south = carry[n * tiles + t]
                q2 = at(src, n, idx + 2, t)
                d1 = q2 - q1
                m1 = minmod(d0, d1)
                g1 = vertical(q1)
                north = face(idx, t, q0, q1, m0, m1, g0, g1)
                dst[n, pad + idx, :, 128 * t : 128 * (t + 1)] = q0 + x[t] + (south - north)
                if isinstance(idx, int):
                    if idx == TOP and seam:
                        north = face(0, t, q0, q1, m0, m1, g0, g1)
                elif seam and k % 2 == 1 and k < chunk - 1:
                    at_seam = jnp.full((LEVELS, 128), idx, jnp.int32) == TOP
                    north = jnp.where(at_seam, face(0, t, q0, q1, m0, m1, g0, g1), north)
                out.append((q1, q2, d1, m1, g1, north))
        carry = out


def loop(count, body, unroll=1):
    def step(i, _):
        body(i)
        return 0

    lax.fori_loop(0, count, step, 0, unroll=unroll)


SALT = 24


def edges_of(x):
    return jnp.where(within(16, 32), roll(x[:, :128], 16), roll(x[:, 128:], 72))


def inner_part(rows, cuts, mid, base, s0, s1, s2, s3, s4, cx, cy):
    def own(j):
        for n in TRACERS:
            s0[n, HALO + j] = rows[n, j]
        x = [rows[f, j] for f in range(8)]
        store_x(cx, HALO + j, *(x[f] for f in XF))
        store_y(cy, HALO + j, *(x[f] for f in YF))
        for f in range(8):
            base[f, j] = edges_of(x[f])

    loop(HEIGHT, own, 4)
    for src, dst, first, count in ((s0, s1, 0, 4), (s1, s2, 4, 3), (s2, s3, 4, 3), (s3, s4, 8, 2)):
        loop(count, lambda i: rows_forward(src, dst, cx, cy, HALO + first + 8 * i, 8, 2, 2))
    for n in TRACERS:
        for step, s in enumerate((s1, s2, s3), 1):
            low = HALO + 2 * step
            for k in range(4):
                cuts[step - 1, n, k] = s[n, low + k]
                cuts[step - 1, n, 4 + k] = s[n, EXT - 4 - low + k]

        def out(j, n=n):
            mid[n, j] = s4[n, 2 * HALO + j]

        loop(2 * HALO, out, 4)


def outer_part(flags, rows, ghost, cuts, mid, result, base, qa, qb, cx, cy):
    top = flags[1] == 1

    def near(k):
        for start in (0, HEIGHT - HALO):
            j = start + k
            for n in TRACERS:
                qa[n, HALO + j] = rows[n, j]
            store_x(cx, HALO + j, *(rows[f, j] for f in XF))
            store_y(cy, HALO + j, *(rows[f, j] for f in YF))

    loop(HALO, near, 4)
    store_y(cy, TOP - HALO, *(rows[f, HEIGHT - HALO - 1] for f in YF))

    def beyond(k):
        to = jnp.where(k < HALO, k, HEIGHT + k)
        x = [ghost[f, k] for f in range(8)]
        for f in range(8):
            base[f, k] = edges_of(x[f])
        for n in TRACERS:
            qa[n, to] = x[n]
        turn = top & (k >= HALO)
        store_x(cx, to, *(jnp.where(turn, roll(x[f], -1), x[f]) for f in XF))
        store_y(cy, to, *(x[f] for f in YF))

    loop(2 * HALO, beyond, 4)

    def one(src, dst, step):
        low = HALO + 2 * step
        for n in TRACERS:
            for k in range(4):
                dst[n, low + k] = cuts[step - 1, n, k]
                dst[n, EXT - 4 - low + k] = cuts[step - 1, n, 4 + k]
        loop(2, lambda w: rows_forward(src, dst, cx, cy, 2 * step + w * (EXT - 8 - 4 * step), 8, 2, 2, seam=True))

    def two(i):
        one(qa, qb, 2 * i + 1)
        one(qb, qa, 2 * i + 2)

    loop(STEPS // 2, two)

    def out(j):
        for n in TRACERS:
            result[n, j] = qa[n, HALO + j]
            result[n, HEIGHT - HALO + j] = qa[n, HEIGHT + j]
            result[n, HALO + j] = mid[n, j]
            result[n, 2 * HALO + j] = mid[n, HALO + j]

    loop(HALO, out, 2)


def late_kernel(flags, rows, ghost, fold, cuts, mid, result, base, beyond, gh, my_cuts, my_mid, *scratch):
    states, (cx, cy) = scratch[:5], scratch[5:]

    @pl.when(flags[3] == 0)
    def _():
        inner_part(rows, my_cuts, my_mid, base, *states, cx, cy)

    @pl.when(flags[4] == 0)
    def _():
        @pl.when(flags[3] == 1)
        def _():
            def copy(k):
                for n in TRACERS:
                    for step in range(STEPS - 1):
                        my_cuts[step, n, k] = cuts[step, n, k]
                    my_mid[n, k] = mid[n, k]
                    my_mid[n, 8 + k] = mid[n, 8 + k]

            loop(8, copy, 4)

        def copy(k):
            for f in range(8):
                gh[f, k] = ghost[f, k]

        loop(2 * HALO, copy, 4)

        @pl.when(flags[1] == 1)
        def _():
            fold_rows(fold, gh)

        outer_part(flags, rows, gh, my_cuts, my_mid, result, beyond, *states[:2], cx, cy)


def edge_kernel(flags, base1, base2, beyond1, beyond2, odd_strip, even_strip, result1, result2, temp, salt, qa, qb, cx, cy):
    top, inner_first, outer_first = flags[1] == 1, flags[3] == 1, flags[4] == 1
    lane = lanes(128)
    from_odd = (lane < 64).astype(jnp.int32) != flags[2]
    is_temp = within(8, 32) | within(56, 80)
    beside = within(8, 16) | within(72, 80)

    def both(y):
        return jnp.where(is_temp, y, roll(y, SALT))

    def base(f, k):
        return jnp.where(inner_first, base1[f, k], base2[f, k])

    def beyond(f, k):
        return jnp.where(outer_first, beyond1[f, k], beyond2[f, k])

    def assemble(either, k, r, half, turn=None):
        a, b = odd_strip[r], even_strip[r]
        halo = jnp.where(from_odd, a, b) if half == 0 else jnp.where(from_odd, b, a)
        y = [jnp.where(beside, roll(halo, 8 - 8 * f - 64 * half), either(f, k)) for f in range(8)]
        to = PAD + r + half * (EXT // 2)
        qa[0, to] = jnp.where(is_temp, y[0], roll(y[1], SALT))
        x = [both(y[f]) for f in XF]
        if turn is not None:
            x = [jnp.where(turn, roll(z, -1), z) for z in x]
        store_x(cx, to, *x)
        store_y(cy, to, *(both(y[f]) for f in YF))

    def ghosts(k):
        assemble(beyond, k, k, 0)
        assemble(beyond, HALO + k, 2 * HALO + k, 1, top)

    loop(HALO, ghosts, 4)

    def own(k):
        assemble(base, k, HALO + k, 0)
        assemble(base, 2 * HALO + k, k, 1)

    loop(2 * HALO, own, 4)

    def two(_):
        for src, dst in ((qa, qb), (qb, qa)):
            rows_forward(src, dst, cx, cy, 2, EXT - 4, 1, 1, seam=True, pad=PAD)

    loop(STEPS // 2, two)

    def patch(j):
        e = qa[0, PAD + HALO + j]
        for n, out in enumerate((temp, salt)):
            x = jnp.where(outer_first, result1[n, j], result2[n, j])
            w = jnp.where(lane < 8, roll(e, -16 - SALT * n), x[:, :128])
            z = jnp.where(lane >= 120, roll(e, 56 - SALT * n), x[:, 128:])
            for at, y in zip(places(j), (w, z)):
                out[at, :] = y

    loop(HEIGHT, patch, 8)


def call(kernel, outs, args, scratch=(), args_in=None, flags=None):
    first = [] if flags is None else [flags]
    return pl.pallas_call(
        kernel,
        out_shape=[jax.ShapeDtypeStruct(s, F32) for s in outs],
        in_specs=[SMEM] * len(first) + (args_in or [VMEM] * len(args)),
        out_specs=[VMEM] * len(outs),
        scratch_shapes=[pltpu.VMEM(s, F32) if isinstance(s, tuple) else s for s in scratch],
        compiler_params=PARAMS,
        cost_estimate=COST,
    )(*first, *args)


ROW = (LEVELS, WIDTH)
TILE = (LEVELS, 128)
STRIP = (EXT // 2, *TILE)
STATE = (2, EXT, *ROW)
FLAT = (2 * LEVELS * HEIGHT, 128)


STATES = [STATE] * 5 + [(6, EXT, *ROW), (5, EXT, *ROW)]
OUTER = [STATE] * 2 + [(6, EXT, *ROW), (5, EXT, *ROW)]
RESULT = (2, HEIGHT, *ROW)
CUTS, MID, BASE, BEYOND = (STEPS, 2, 8, *ROW), (2, 2 * HALO, *ROW), (8, HEIGHT, *TILE), (8, 2 * HALO, *TILE)
GHOST = (8, 2 * HALO, *ROW)
IN_HBM = pl.BlockSpec(memory_space=pltpu.HBM)


def pack(flags, args):
    held = [pltpu.VMEM((2, LEVELS, 16, 128), x.dtype) for x in args]
    args = [pltpu.with_memory_space_constraint(x.reshape(LEVELS, -1, 128), pltpu.HBM) for x in args]
    return call(
        pack_kernel,
        [(MESSAGE, *ROW), (MESSAGE, *ROW), (9, *TILE)],
        args,
        [*held, pltpu.SemaphoreType.DMA((9, 2))],
        [IN_HBM] * 9,
        flags,
    )


def transpose(flags, args, after):
    held = [pltpu.VMEM(FLAT, x.dtype) for x in args]
    args = [pltpu.with_memory_space_constraint(x, pltpu.HBM) for x in args]
    return call(
        rows_kernel,
        [(8, HEIGHT, *ROW), CUTS, MID, BASE],
        [*args, after],
        [*held, pltpu.SemaphoreType.DMA((9,)), *STATES],
        [IN_HBM] * 9 + [VMEM],
        flags,
    )


def fill_ghost(flags, rows, odd_in, even_in, sides, cuts, mid):
    return call(
        ghost_kernel,
        [GHOST, STRIP, STRIP, RESULT, BEYOND],
        [rows, odd_in, even_in, sides, cuts, mid],
        OUTER,
        flags=flags,
    )


def late(flags, rows, ghost, fold, cuts, mid):
    return call(
        late_kernel,
        [RESULT, BASE, BEYOND],
        [rows, ghost, fold, cuts, mid],
        [GHOST, CUTS, MID, *STATES],
        flags=flags,
    )


def edge(flags, *args):
    return call(
        edge_kernel,
        [FLAT] * 2,
        args,
        [(1, EDGE_DEPTH, *TILE)] * 2 + [(6, EDGE_DEPTH, *TILE), (5, EDGE_DEPTH, *TILE)],
        flags=flags,
    )


def on_device(lon_count, lat_count, *args):
    lon, lat = lax.axis_index("lon"), lax.axis_index("lat")
    top = (lat == lat_count - 1).astype(jnp.int32)
    place = lon % 8
    inner_first = (place < INNER_FIRST).astype(jnp.int32)
    outer_first = (place < OUTER_FIRST).astype(jnp.int32) * (1 - top)
    flags = jnp.stack([lat % 2, top, lon % 2, inner_first, outer_first])
    flat = [level_major(x) for x in args]

    def index(i, j):
        return i * lat_count + j

    lons, lats = range(lon_count), range(lat_count)
    lat_even = [(index(i, j), index(i, j ^ 1)) for i in lons for j in lats]
    lat_odd = [
        (index(i, j), index(i, j + 1 if j % 2 else j - 1)) for i in lons for j in range(1, lat_count - 1)
    ]
    fold = [(index(i, lat_count - 1), index(lon_count - 1 - i, lat_count - 1)) for i in lons]
    lon_even = [(i, i ^ 1) for i in lons]
    lon_odd = [(i, (i + 1 if i % 2 else i - 1) % lon_count) for i in lons]
    both = ("lon", "lat")
    odd_msg, even_msg, sides = pack(flags, flat)
    fold_in = lax.ppermute(odd_msg, both, fold)
    odd_in = lax.ppermute(odd_msg, both, lat_odd)
    even_in = lax.ppermute(even_msg, both, lat_even)
    sides = lax.ppermute(sides, both, fold)
    rows, cuts, mid, base1 = transpose(flags, flat, odd_msg)
    ghost, odd_strip, even_strip, result1, beyond1 = fill_ghost(flags, rows, odd_in, even_in, sides, cuts, mid)
    odd_strip = lax.ppermute(odd_strip, "lon", lon_odd)
    even_strip = lax.ppermute(even_strip, "lon", lon_even)
    result2, base2, beyond2 = late(flags, rows, ghost, fold_in, cuts, mid)
    temp, salt = edge(flags, base1, base2, beyond1, beyond2, odd_strip, even_strip, result1, result2)
    return from_level_major(temp), from_level_major(salt)


def solution(mesh):
    spec = P(None, "lat", "lon")
    return jax.shard_map(
        functools.partial(on_device, mesh.shape["lon"], mesh.shape["lat"]),
        mesh=mesh,
        in_specs=(spec,) * 9,
        out_specs=(spec, spec),
        check_vma=False,
    )
```

```python
import functools

import jax
import jax.numpy as jnp
from jax import lax
from jax.experimental import pallas as pl
from jax.experimental.pallas import tpu as pltpu
from jax.sharding import PartitionSpec as P

STEPS = 4
HALO = 2 * STEPS
PAD = 4
INNER_FIRST = 4
OUTER_FIRST = 3
LEVELS = 8
HEIGHT = 32
WIDTH = 256
EXT = HEIGHT + 2 * HALO
TOP = HALO + HEIGHT - 1
EDGE_DEPTH = EXT + 2 * PAD
F32 = jnp.float32
VMEM = pl.BlockSpec(memory_space=pltpu.VMEM)
SMEM = pl.BlockSpec(memory_space=pltpu.SMEM)
PARAMS = pltpu.CompilerParams(vmem_limit_bytes=24 * 2**20)
COST = pl.CostEstimate(flops=50_000_000, bytes_accessed=8_000_000, transcendentals=0)

TRACERS, XF, YF = (0, 1), (2, 3, 4), (5, 6, 7)
FLIPPED = (2, 4, 5, 7)
MESSAGE = 2 * 8 + 3 * 6 + 3 * 7


def slot(field, k):
    if field < 2:
        return field * 8 + k
    if field < 5:
        return 16 + (field - 2) * 6 + k
    return 34 + (field - 5) * 7 + k


def rows_of(field):
    return 8 if field < 2 else 6 if field < 5 else 7


def level_major(x):
    x = x.reshape(LEVELS, HEIGHT // 8, 8, WIDTH // 128, 128)
    return x.transpose(0, 1, 3, 2, 4).reshape(-1, 128)


def from_level_major(x):
    x = x.reshape(LEVELS, HEIGHT // 8, WIDTH // 128, 8, 128)
    return x.transpose(0, 1, 3, 2, 4).reshape(LEVELS, HEIGHT, WIDTH)


def places(j):
    start = (j // 8) * 16 + j % 8
    return [pl.ds(start + 8 * c, LEVELS, stride=2 * HEIGHT) for c in range(2)]


def load_row(ref, j):
    return jnp.concatenate([ref[at, :] for at in places(j)], axis=1)


def lanes(width):
    return lax.broadcasted_iota(jnp.int32, (LEVELS, width), 1)


def within(lo, hi):
    lane = lanes(128)
    return (lane >= lo) & (lane < hi)


def roll(x, by):
    return pltpu.roll(x, by % x.shape[-1], 1)


def fields(held, at):
    temp, salt, u, v, diff, sx, sy, mu, mv = (at(ref) for ref in held)
    wet_u, wet_v = mu.astype(F32), mv.astype(F32)
    return temp, salt, u * wet_u, diff * wet_u, sx, v * wet_v, diff * wet_v, sy


def pack_kernel(flags, *refs):
    args, (odd_msg, even_msg), held, sems = refs[:9], refs[9:11], refs[11:20], refs[20]
    copies = []
    for n, (x, y) in enumerate(zip(args, held)):
        for part, start in enumerate((0, 2 * HEIGHT - 16)):
            copies.append(pltpu.make_async_copy(x.at[:, pl.ds(start, 16), :], y.at[part], sems.at[n, part]))
    for copy in copies:
        copy.start()
    for copy in copies:
        copy.wait()

    def fill(part, msg):
        for k in range(8):

            def at(ref):
                flat = ref.at[part].reshape(LEVELS * 16, 128)
                return jnp.concatenate([flat[pl.ds(8 * c + k, LEVELS, stride=16), :] for c in range(2)], axis=1)

            for f, x in enumerate(fields(held, at)):
                to = k - (8 - rows_of(f)) * part
                if 0 <= to < rows_of(f):
                    msg[slot(f, to)] = x

    @pl.when(flags[0] == 1)
    def _():
        fill(1, odd_msg)
        fill(0, even_msg)

    @pl.when(flags[0] == 0)
    def _():
        fill(0, odd_msg)
        fill(1, even_msg)


def rows_kernel(flags, *refs):
    args, _, outs, held, sems = refs[:9], refs[9], refs[10:14], refs[14:23], refs[23]
    rows, cuts, mid, base = outs
    copies = [pltpu.make_async_copy(x, y, sems.at[n]) for n, (x, y) in enumerate(zip(args, held))]
    for copy in copies:
        copy.start()
    for copy in copies:
        copy.wait()

    def one(j):
        for f, x in enumerate(fields(held, lambda ref: load_row(ref, j))):
            rows[f, j] = x

    loop(HEIGHT, one, 4)

    @pl.when(flags[3] == 1)
    def _():
        inner_part(rows, cuts, mid, base, *refs[24:])


def mirrored(x):
    n = x.shape[-1] // 128
    back = 127 - lanes(128)
    parts = [x[:, 128 * i : 128 * (i + 1)] for i in range(n)]
    return jnp.concatenate([jnp.take_along_axis(p, back, axis=1) for p in reversed(parts)], axis=1)


def fold_rows(msg, ghost):
    for f in range(8):
        n = rows_of(f)
        sign = -1.0 if f in FLIPPED else 1.0
        for k in range(n):
            x = mirrored(msg[slot(f, n - 1 - k)]) * sign
            if f < 5:
                ghost[f, HALO + k] = x
            elif k == 0:
                ghost[f, 0] = x
            else:
                ghost[f, HALO + k - 1] = x


def ghost_kernel(flags, rows, odd_msg, even_msg, cuts, mid, ghost, odd_strip, even_strip, result, base, *scratch):
    is_odd = flags[0] == 1
    for f in range(8):
        n = rows_of(f)
        for k in range(n):
            a, b = odd_msg[slot(f, k)], even_msg[slot(f, k)]
            ghost[f, HALO - n + k] = jnp.where(is_odd, b, a)
            if k < n - (f >= 5):
                ghost[f, HALO + k] = jnp.where(is_odd, a, b)
        if f >= 5:
            ghost[f, 0] = rows[f, HEIGHT - 1]

    @pl.when(flags[1] == 1)
    def _():
        fold_rows(odd_msg, ghost)

    swap = flags[2] == 1
    for r in range(EXT // 2):
        east, west = jnp.zeros((LEVELS, 128), F32), jnp.zeros((LEVELS, 128), F32)
        for half in range(2):
            idx = r + half * (EXT // 2)
            for f in range(8):
                if idx < HALO:
                    x = ghost[f, idx]
                elif idx <= TOP:
                    x = rows[f, idx - HALO]
                else:
                    x = ghost[f, idx - HEIGHT]
                to = 8 * f + 64 * half
                east = jnp.where(within(to, to + 8), roll(x[:, 128:], to + 8), east)
                to = 8 * f + 64 * (1 - half)
                west = jnp.where(within(to, to + 8), roll(x[:, :128], to), west)
        even_strip[r] = jnp.where(swap, west, east)
        odd_strip[r] = jnp.where(swap, east, west)

    @pl.when(flags[4] == 1)
    def _():
        outer_part(flags, rows, ghost, cuts, mid, result, base, *scratch)


def minmod(p, t):
    return jnp.maximum(jnp.minimum(p, t), jnp.minimum(jnp.maximum(p, t), 0.0))


def vertical(q):
    level = lax.broadcasted_iota(jnp.int32, q.shape, 0)
    up = jnp.where(level == LEVELS - 1, q, pltpu.roll(q, LEVELS - 1, 0))
    down = jnp.where(level == 0, q, pltpu.roll(q, 1, 0))
    return up - down


def shifted(tiles, by):
    lane = lanes(128)
    rolled = [roll(t, by) for t in tiles]
    if len(tiles) == 1:
        return rolled
    seam = lane == (0 if by == 1 else 127)
    return [jnp.where(seam, rolled[1 - n], rolled[n]) for n in range(2)]


def coefficients(c, r, s):
    plus, minus = jnp.maximum(c, 0.0), jnp.minimum(c, 0.0)
    return (
        plus + r,
        0.5 * plus * (1.0 - plus),
        0.25 * r * s,
        minus - r,
        -0.5 * minus * (1.0 + minus),
    )


def store_x(cx, idx, c, r, s):
    p, lp, t, e, ln = coefficients(c, r, s)
    for n, x in enumerate((p, lp, t, roll(e, 1), roll(ln, 1), roll(t, 1))):
        cx[n, idx] = x


def store_y(cy, idx, c, r, s):
    for n, x in enumerate(coefficients(c, r, s)):
        cy[n, idx] = x


def rows_forward(src, dst, cx, cy, first, chunk, streams, tiles, seam=False, pad=0):
    def at(ref, n, idx, t):
        return ref[n, pad + idx, :, 128 * t : 128 * (t + 1)]

    def face(idx, t, q0, q1, m0, m1, g0, g1):
        c = [at(cy, n, idx, t) for n in range(5)]
        return (c[0] * q0 + c[3] * q1) + (c[1] * m0 + c[4] * m1) + c[2] * (g0 + g1)

    south = jnp.where(first == TOP + 1, 0, first - 1)
    carry = []
    for n in range(streams):
        for t in range(tiles):
            q = [at(src, n, first - 2 + k, t) for k in range(4)]
            d = [q[k + 1] - q[k] for k in range(3)]
            m0, m1 = minmod(d[0], d[1]), minmod(d[1], d[2])
            g0, g1 = vertical(q[1]), vertical(q[2])
            carry.append((q[2], q[3], d[2], m1, g1, face(south, t, q[1], q[2], m0, m1, g0, g1)))
    for k in range(chunk):
        idx = first + k
        out = []
        for n in range(streams):
            q0 = [carry[n * tiles + t][0] for t in range(tiles)]
            d = [x - y for x, y in zip(shifted(q0, -1), q0)]
            m = [minmod(x, y) for x, y in zip(d, shifted(d, 1))]
            a, b = [], []
            for t in range(tiles):
                g0 = carry[n * tiles + t][4]
                c = [at(cx, i, idx, t) for i in range(6)]
                a.append(c[0] * q0[t] + c[1] * m[t] + c[2] * g0)
                b.append(c[3] * q0[t] + c[4] * m[t] + c[5] * g0)
            x = [(b[t] - a[t]) + (p - r) for t, (p, r) in enumerate(zip(shifted(a, 1), shifted(b, -1)))]
            for t in range(tiles):
                q0, q1, d0, m0, g0, south = carry[n * tiles + t]
                q2 = at(src, n, idx + 2, t)
                d1 = q2 - q1
                m1 = minmod(d0, d1)
                g1 = vertical(q1)
                north = face(idx, t, q0, q1, m0, m1, g0, g1)
                dst[n, pad + idx, :, 128 * t : 128 * (t + 1)] = q0 + x[t] + (south - north)
                if isinstance(idx, int):
                    if idx == TOP and seam:
                        north = face(0, t, q0, q1, m0, m1, g0, g1)
                elif seam and k % 2 == 1 and k < chunk - 1:
                    at_seam = jnp.full((LEVELS, 128), idx, jnp.int32) == TOP
                    north = jnp.where(at_seam, face(0, t, q0, q1, m0, m1, g0, g1), north)
                out.append((q1, q2, d1, m1, g1, north))
        carry = out


def loop(count, body, unroll=1):
    def step(i, _):
        body(i)
        return 0

    lax.fori_loop(0, count, step, 0, unroll=unroll)


SALT = 24


def edges_of(x):
    return jnp.where(within(16, 32), roll(x[:, :128], 16), roll(x[:, 128:], 72))


def inner_part(rows, cuts, mid, base, s0, s1, s2, s3, s4, cx, cy):
    def own(j):
        for n in TRACERS:
            s0[n, HALO + j] = rows[n, j]
        x = [rows[f, j] for f in range(8)]
        store_x(cx, HALO + j, *(x[f] for f in XF))
        store_y(cy, HALO + j, *(x[f] for f in YF))
        for f in range(8):
            base[f, j] = edges_of(x[f])

    loop(HEIGHT, own, 4)
    for src, dst, first, count in ((s0, s1, 0, 4), (s1, s2, 4, 3), (s2, s3, 4, 3), (s3, s4, 8, 2)):
        loop(count, lambda i: rows_forward(src, dst, cx, cy, HALO + first + 8 * i, 8, 2, 2))
    for n in TRACERS:
        for step, s in enumerate((s1, s2, s3), 1):
            low = HALO + 2 * step
            for k in range(4):
                cuts[step - 1, n, k] = s[n, low + k]
                cuts[step - 1, n, 4 + k] = s[n, EXT - 4 - low + k]

        def out(j, n=n):
            mid[n, j] = s4[n, 2 * HALO + j]

        loop(2 * HALO, out, 4)


def outer_part(flags, rows, ghost, cuts, mid, result, base, qa, qb, cx, cy):
    top = flags[1] == 1

    def near(k):
        for start in (0, HEIGHT - HALO):
            j = start + k
            for n in TRACERS:
                qa[n, HALO + j] = rows[n, j]
            store_x(cx, HALO + j, *(rows[f, j] for f in XF))
            store_y(cy, HALO + j, *(rows[f, j] for f in YF))

    loop(HALO, near, 4)
    store_y(cy, TOP - HALO, *(rows[f, HEIGHT - HALO - 1] for f in YF))

    def beyond(k):
        to = jnp.where(k < HALO, k, HEIGHT + k)
        x = [ghost[f, k] for f in range(8)]
        for f in range(8):
            base[f, k] = edges_of(x[f])
        for n in TRACERS:
            qa[n, to] = x[n]
        turn = top & (k >= HALO)
        store_x(cx, to, *(jnp.where(turn, roll(x[f], -1), x[f]) for f in XF))
        store_y(cy, to, *(x[f] for f in YF))

    loop(2 * HALO, beyond, 4)

    def one(src, dst, step):
        low = HALO + 2 * step
        for n in TRACERS:
            for k in range(4):
                dst[n, low + k] = cuts[step - 1, n, k]
                dst[n, EXT - 4 - low + k] = cuts[step - 1, n, 4 + k]
        loop(2, lambda w: rows_forward(src, dst, cx, cy, 2 * step + w * (EXT - 8 - 4 * step), 8, 2, 2, seam=True))

    def two(i):
        one(qa, qb, 2 * i + 1)
        one(qb, qa, 2 * i + 2)

    loop(STEPS // 2, two)

    def out(j):
        for n in TRACERS:
            result[n, j] = qa[n, HALO + j]
            result[n, HEIGHT - HALO + j] = qa[n, HEIGHT + j]
            result[n, HALO + j] = mid[n, j]
            result[n, 2 * HALO + j] = mid[n, HALO + j]

    loop(HALO, out, 2)


def late_kernel(flags, rows, ghost, cuts, mid, result, base, beyond, my_cuts, my_mid, *scratch):
    states, (cx, cy) = scratch[:5], scratch[5:]

    @pl.when(flags[3] == 0)
    def _():
        inner_part(rows, my_cuts, my_mid, base, *states, cx, cy)

    @pl.when(flags[4] == 0)
    def _():
        @pl.when(flags[3] == 1)
        def _():
            def copy(k):
                for n in TRACERS:
                    for step in range(STEPS - 1):
                        my_cuts[step, n, k] = cuts[step, n, k]
                    my_mid[n, k] = mid[n, k]
                    my_mid[n, 8 + k] = mid[n, 8 + k]

            loop(8, copy, 4)

        outer_part(flags, rows, ghost, my_cuts, my_mid, result, beyond, *states[:2], cx, cy)


def edge_kernel(flags, base1, base2, beyond1, beyond2, odd_strip, even_strip, result1, result2, temp, salt, qa, qb, cx, cy):
    top, inner_first, outer_first = flags[1] == 1, flags[3] == 1, flags[4] == 1
    lane = lanes(128)
    from_odd = (lane < 64).astype(jnp.int32) != flags[2]
    is_temp = within(8, 32) | within(56, 80)
    beside = within(8, 16) | within(72, 80)

    def both(y):
        return jnp.where(is_temp, y, roll(y, SALT))

    def base(f, k):
        return jnp.where(inner_first, base1[f, k], base2[f, k])

    def beyond(f, k):
        return jnp.where(outer_first, beyond1[f, k], beyond2[f, k])

    def assemble(either, k, r, half, turn=None):
        a, b = odd_strip[r], even_strip[r]
        halo = jnp.where(from_odd, a, b) if half == 0 else jnp.where(from_odd, b, a)
        y = [jnp.where(beside, roll(halo, 8 - 8 * f - 64 * half), either(f, k)) for f in range(8)]
        to = PAD + r + half * (EXT // 2)
        qa[0, to] = jnp.where(is_temp, y[0], roll(y[1], SALT))
        x = [both(y[f]) for f in XF]
        if turn is not None:
            x = [jnp.where(turn, roll(z, -1), z) for z in x]
        store_x(cx, to, *x)
        store_y(cy, to, *(both(y[f]) for f in YF))

    def ghosts(k):
        assemble(beyond, k, k, 0)
        assemble(beyond, HALO + k, 2 * HALO + k, 1, top)

    loop(HALO, ghosts, 4)

    def own(k):
        assemble(base, k, HALO + k, 0)
        assemble(base, 2 * HALO + k, k, 1)

    loop(2 * HALO, own, 4)

    def two(_):
        for src, dst in ((qa, qb), (qb, qa)):
            rows_forward(src, dst, cx, cy, 2, EXT - 4, 1, 1, seam=True, pad=PAD)

    loop(STEPS // 2, two)

    def patch(j):
        e = qa[0, PAD + HALO + j]
        for n, out in enumerate((temp, salt)):
            x = jnp.where(outer_first, result1[n, j], result2[n, j])
            w = jnp.where(lane < 8, roll(e, -16 - SALT * n), x[:, :128])
            z = jnp.where(lane >= 120, roll(e, 56 - SALT * n), x[:, 128:])
            for at, y in zip(places(j), (w, z)):
                out[at, :] = y

    loop(HEIGHT, patch, 8)


def call(kernel, outs, args, scratch=(), args_in=None, flags=None):
    first = [] if flags is None else [flags]
    return pl.pallas_call(
        kernel,
        out_shape=[jax.ShapeDtypeStruct(s, F32) for s in outs],
        in_specs=[SMEM] * len(first) + (args_in or [VMEM] * len(args)),
        out_specs=[VMEM] * len(outs),
        scratch_shapes=[pltpu.VMEM(s, F32) if isinstance(s, tuple) else s for s in scratch],
        compiler_params=PARAMS,
        cost_estimate=COST,
    )(*first, *args)


ROW = (LEVELS, WIDTH)
TILE = (LEVELS, 128)
STRIP = (EXT // 2, *TILE)
STATE = (2, EXT, *ROW)
FLAT = (2 * LEVELS * HEIGHT, 128)


STATES = [STATE] * 5 + [(6, EXT, *ROW), (5, EXT, *ROW)]
OUTER = [STATE] * 2 + [(6, EXT, *ROW), (5, EXT, *ROW)]
RESULT = (2, HEIGHT, *ROW)
CUTS, MID, BASE, BEYOND = (STEPS, 2, 8, *ROW), (2, 2 * HALO, *ROW), (8, HEIGHT, *TILE), (8, 2 * HALO, *TILE)
GHOST = (8, 2 * HALO, *ROW)
IN_HBM = pl.BlockSpec(memory_space=pltpu.HBM)


def pack(flags, args):
    held = [pltpu.VMEM((2, LEVELS, 16, 128), x.dtype) for x in args]
    args = [pltpu.with_memory_space_constraint(x.reshape(LEVELS, -1, 128), pltpu.HBM) for x in args]
    return call(
        pack_kernel,
        [(MESSAGE, *ROW)] * 2,
        args,
        [*held, pltpu.SemaphoreType.DMA((9, 2))],
        [IN_HBM] * 9,
        flags,
    )


def transpose(flags, args, after):
    held = [pltpu.VMEM(FLAT, x.dtype) for x in args]
    args = [pltpu.with_memory_space_constraint(x, pltpu.HBM) for x in args]
    return call(
        rows_kernel,
        [(8, HEIGHT, *ROW), CUTS, MID, BASE],
        [*args, after],
        [*held, pltpu.SemaphoreType.DMA((9,)), *STATES],
        [IN_HBM] * 9 + [VMEM],
        flags,
    )


def fill_ghost(flags, rows, odd_in, even_in, cuts, mid):
    return call(
        ghost_kernel,
        [GHOST, STRIP, STRIP, RESULT, BEYOND],
        [rows, odd_in, even_in, cuts, mid],
        OUTER,
        flags=flags,
    )


def late(flags, rows, ghost, cuts, mid):
    return call(
        late_kernel,
        [RESULT, BASE, BEYOND],
        [rows, ghost, cuts, mid],
        [CUTS, MID, *STATES],
        flags=flags,
    )


def edge(flags, *args):
    return call(
        edge_kernel,
        [FLAT] * 2,
        args,
        [(1, EDGE_DEPTH, *TILE)] * 2 + [(6, EDGE_DEPTH, *TILE), (5, EDGE_DEPTH, *TILE)],
        flags=flags,
    )


def on_device(lon_count, lat_count, *args):
    lon, lat = lax.axis_index("lon"), lax.axis_index("lat")
    top = (lat == lat_count - 1).astype(jnp.int32)
    place = lon % 8
    inner_first = (place < INNER_FIRST).astype(jnp.int32)
    outer_first = (place < OUTER_FIRST).astype(jnp.int32) * (1 - top)
    flags = jnp.stack([lat % 2, top, lon % 2, inner_first, outer_first])
    flat = [level_major(x) for x in args]

    def index(i, j):
        return i * lat_count + j

    lons, lats = range(lon_count), range(lat_count)
    lat_even = [(index(i, j), index(i, j ^ 1)) for i in lons for j in lats]
    lat_odd = [
        (index(i, j), index(lon_count - 1 - i, j) if j == lat_count - 1 else index(i, j + 1 if j % 2 else j - 1))
        for i in lons
        for j in lats
        if j > 0
    ]
    lon_even = [(i, i ^ 1) for i in lons]
    lon_odd = [(i, (i + 1 if i % 2 else i - 1) % lon_count) for i in lons]
    both = ("lon", "lat")
    odd_msg, even_msg = pack(flags, flat)
    odd_in = lax.ppermute(odd_msg, both, lat_odd)
    even_in = lax.ppermute(even_msg, both, lat_even)
    rows, cuts, mid, base1 = transpose(flags, flat, odd_msg)
    ghost, odd_strip, even_strip, result1, beyond1 = fill_ghost(flags, rows, odd_in, even_in, cuts, mid)
    odd_strip = lax.ppermute(odd_strip, "lon", lon_odd)
    even_strip = lax.ppermute(even_strip, "lon", lon_even)
    result2, base2, beyond2 = late(flags, rows, ghost, cuts, mid)
    temp, salt = edge(flags, base1, base2, beyond1, beyond2, odd_strip, even_strip, result1, result2)
    return from_level_major(temp), from_level_major(salt)


def solution(mesh):
    spec = P(None, "lat", "lon")
    return jax.shard_map(
        functools.partial(on_device, mesh.shape["lon"], mesh.shape["lat"]),
        mesh=mesh,
        in_specs=(spec,) * 9,
        out_specs=(spec, spec),
        check_vma=False,
    )
```

```python
import functools

import jax
import jax.numpy as jnp
from jax import lax
from jax.experimental import pallas as pl
from jax.experimental.pallas import tpu as pltpu
from jax.sharding import PartitionSpec as P

STEPS = 4
HALO = 2 * STEPS
PAD = 4
INNER_FIRST = 4
OUTER_FIRST = 3
WAITS_FROM = 6
LEVELS = 8
HEIGHT = 32
WIDTH = 256
EXT = HEIGHT + 2 * HALO
TOP = HALO + HEIGHT - 1
EDGE_DEPTH = EXT + 2 * PAD
F32 = jnp.float32
VMEM = pl.BlockSpec(memory_space=pltpu.VMEM)
SMEM = pl.BlockSpec(memory_space=pltpu.SMEM)
PARAMS = pltpu.CompilerParams(vmem_limit_bytes=24 * 2**20)
COST = pl.CostEstimate(flops=50_000_000, bytes_accessed=8_000_000, transcendentals=0)

TRACERS, XF, YF = (0, 1), (2, 3, 4), (5, 6, 7)
FLIPPED = (2, 4, 5, 7)
MESSAGE = 2 * 8 + 3 * 6 + 3 * 7


def slot(field, k):
    if field < 2:
        return field * 8 + k
    if field < 5:
        return 16 + (field - 2) * 6 + k
    return 34 + (field - 5) * 7 + k


def rows_of(field):
    return 8 if field < 2 else 6 if field < 5 else 7


def level_major(x):
    x = x.reshape(LEVELS, HEIGHT // 8, 8, WIDTH // 128, 128)
    return x.transpose(0, 1, 3, 2, 4).reshape(-1, 128)


def from_level_major(x):
    x = x.reshape(LEVELS, HEIGHT // 8, WIDTH // 128, 8, 128)
    return x.transpose(0, 1, 3, 2, 4).reshape(LEVELS, HEIGHT, WIDTH)


def places(j):
    start = (j // 8) * 16 + j % 8
    return [pl.ds(start + 8 * c, LEVELS, stride=2 * HEIGHT) for c in range(2)]


def load_row(ref, j):
    return jnp.concatenate([ref[at, :] for at in places(j)], axis=1)


def lanes(width):
    return lax.broadcasted_iota(jnp.int32, (LEVELS, width), 1)


def within(lo, hi):
    lane = lanes(128)
    return (lane >= lo) & (lane < hi)


def roll(x, by):
    return pltpu.roll(x, by % x.shape[-1], 1)


def fields(held, at):
    temp, salt, u, v, diff, sx, sy, mu, mv = (at(ref) for ref in held)
    wet_u, wet_v = mu.astype(F32), mv.astype(F32)
    return temp, salt, u * wet_u, diff * wet_u, sx, v * wet_v, diff * wet_v, sy


def pack_kernel(flags, *refs):
    args, (odd_msg, even_msg, done), held, sems = refs[:9], refs[9:12], refs[12:21], refs[21]
    done[...] = jnp.zeros((LEVELS, 128), F32)
    copies = []
    for n, (x, y) in enumerate(zip(args, held)):
        for part, start in enumerate((0, 2 * HEIGHT - 16)):
            copies.append(pltpu.make_async_copy(x.at[:, pl.ds(start, 16), :], y.at[part], sems.at[n, part]))
    for copy in copies:
        copy.start()
    for copy in copies:
        copy.wait()

    odd = flags[0]

    def row(i):
        for msg, part in ((odd_msg, odd), (even_msg, 1 - odd)):
            k = jnp.where(part == 1, i, 7 - i)

            def at(ref):
                flat = ref.at[part].reshape(LEVELS * 16, 128)
                return jnp.concatenate([flat[pl.ds(8 * c + k, LEVELS, stride=16), :] for c in range(2)], axis=1)

            for f, x in enumerate(fields(held, at)):
                n = rows_of(f)
                msg[slot(f, 0) + jnp.clip(k - (8 - n) * part, 0, n - 1)] = x

    loop(8, row, 4)


def add_sides(parts, x, half):
    east, west = parts
    for f in range(8):
        to = 8 * f + 64 * half
        east = jnp.where(within(to, to + 8), roll(x[f][:, 128:], to + 8), east)
        to = 8 * f + 64 * (1 - half)
        west = jnp.where(within(to, to + 8), roll(x[f][:, :128], to), west)
    return east, west


def rows_kernel(flags, *refs):
    args, _, outs, held, sems = refs[:9], refs[9], refs[10:16], refs[16:25], refs[25]
    rows, east_own, west_own, cuts, mid, base = outs
    copies = [pltpu.make_async_copy(x, y, sems.at[n]) for n, (x, y) in enumerate(zip(args, held))]
    for copy in copies:
        copy.start()
    for copy in copies:
        copy.wait()

    def one(j):
        for f, x in enumerate(fields(held, lambda ref: load_row(ref, j))):
            rows[f, j] = x

    loop(HEIGHT, one, 4)

    def sides(r):
        parts = [jnp.zeros((LEVELS, 128), F32)] * 2
        for half in range(2):
            idx = r + half * (EXT // 2)
            j = jnp.clip(idx - HALO, 0, HEIGHT - 1)
            parts = add_sides(parts, [rows[f, j] for f in range(8)], half)
        east_own[r], west_own[r] = parts

    loop(EXT // 2, sides, 4)

    @pl.when(flags[3] == 1)
    def _():
        inner_part(rows, cuts, mid, base, *refs[26:])


def mirrored(x):
    n = x.shape[-1] // 128
    back = 127 - lanes(128)
    parts = [x[:, 128 * i : 128 * (i + 1)] for i in range(n)]
    return jnp.concatenate([jnp.take_along_axis(p, back, axis=1) for p in reversed(parts)], axis=1)


def fold_rows(msg, ghost):
    for f in range(8):
        n = rows_of(f)
        sign = -1.0 if f in FLIPPED else 1.0
        for k in range(n):
            x = mirrored(msg[slot(f, n - 1 - k)]) * sign
            if f < 5:
                ghost[f, HALO + k] = x
            elif k == 0:
                ghost[f, 0] = x
            else:
                ghost[f, HALO + k - 1] = x


def ghost_kernel(flags, rows, odd_msg, even_msg, east_own, west_own, cuts, mid, ghost, odd_strip, even_strip, result, base, *scratch):
    is_odd = flags[0] == 1
    for f in range(8):
        n = rows_of(f)
        for k in range(n):
            a, b = odd_msg[slot(f, k)], even_msg[slot(f, k)]
            ghost[f, HALO - n + k] = jnp.where(is_odd, b, a)
            if k < n - (f >= 5):
                ghost[f, HALO + k] = jnp.where(is_odd, a, b)
        if f >= 5:
            ghost[f, 0] = rows[f, HEIGHT - 1]

    @pl.when(flags[1] == 1)
    def _():
        fold_rows(odd_msg, ghost)

    swap = flags[2] == 1
    for r in range(EXT // 2):
        parts = [east_own[r], west_own[r]]
        if r < HALO:
            parts = add_sides(parts, [ghost[f, r] for f in range(8)], 0)
        if r >= 2 * HALO:
            parts = add_sides(parts, [ghost[f, r - HALO] for f in range(8)], 1)
        even_strip[r] = jnp.where(swap, parts[1], parts[0])
        odd_strip[r] = jnp.where(swap, parts[0], parts[1])

    @pl.when(flags[4] == 1)
    def _():
        outer_part(flags, rows, ghost, cuts, mid, result, base, *scratch)


def minmod(p, t):
    return jnp.maximum(jnp.minimum(p, t), jnp.minimum(jnp.maximum(p, t), 0.0))


def vertical(q):
    level = lax.broadcasted_iota(jnp.int32, q.shape, 0)
    up = jnp.where(level == LEVELS - 1, q, pltpu.roll(q, LEVELS - 1, 0))
    down = jnp.where(level == 0, q, pltpu.roll(q, 1, 0))
    return up - down


def shifted(tiles, by):
    lane = lanes(128)
    rolled = [roll(t, by) for t in tiles]
    if len(tiles) == 1:
        return rolled
    seam = lane == (0 if by == 1 else 127)
    return [jnp.where(seam, rolled[1 - n], rolled[n]) for n in range(2)]


def coefficients(c, r, s):
    plus, minus = jnp.maximum(c, 0.0), jnp.minimum(c, 0.0)
    return (
        plus + r,
        0.5 * plus * (1.0 - plus),
        0.25 * r * s,
        minus - r,
        -0.5 * minus * (1.0 + minus),
    )


def store_x(cx, idx, c, r, s):
    p, lp, t, e, ln = coefficients(c, r, s)
    for n, x in enumerate((p, lp, t, roll(e, 1), roll(ln, 1), roll(t, 1))):
        cx[n, idx] = x


def store_y(cy, idx, c, r, s):
    for n, x in enumerate(coefficients(c, r, s)):
        cy[n, idx] = x


def rows_forward(src, dst, cx, cy, first, chunk, streams, tiles, seam=False, pad=0):
    def at(ref, n, idx, t):
        return ref[n, pad + idx, :, 128 * t : 128 * (t + 1)]

    def face(idx, t, q0, q1, m0, m1, g0, g1):
        c = [at(cy, n, idx, t) for n in range(5)]
        return (c[0] * q0 + c[3] * q1) + (c[1] * m0 + c[4] * m1) + c[2] * (g0 + g1)

    south = jnp.where(first == TOP + 1, 0, first - 1)
    carry = []
    for n in range(streams):
        for t in range(tiles):
            q = [at(src, n, first - 2 + k, t) for k in range(4)]
            d = [q[k + 1] - q[k] for k in range(3)]
            m0, m1 = minmod(d[0], d[1]), minmod(d[1], d[2])
            g0, g1 = vertical(q[1]), vertical(q[2])
            carry.append((q[2], q[3], d[2], m1, g1, face(south, t, q[1], q[2], m0, m1, g0, g1)))
    for k in range(chunk):
        idx = first + k
        out = []
        for n in range(streams):
            q0 = [carry[n * tiles + t][0] for t in range(tiles)]
            d = [x - y for x, y in zip(shifted(q0, -1), q0)]
            m = [minmod(x, y) for x, y in zip(d, shifted(d, 1))]
            a, b = [], []
            for t in range(tiles):
                g0 = carry[n * tiles + t][4]
                c = [at(cx, i, idx, t) for i in range(6)]
                a.append(c[0] * q0[t] + c[1] * m[t] + c[2] * g0)
                b.append(c[3] * q0[t] + c[4] * m[t] + c[5] * g0)
            x = [(b[t] - a[t]) + (p - r) for t, (p, r) in enumerate(zip(shifted(a, 1), shifted(b, -1)))]
            for t in range(tiles):
                q0, q1, d0, m0, g0, south = carry[n * tiles + t]
                q2 = at(src, n, idx + 2, t)
                d1 = q2 - q1
                m1 = minmod(d0, d1)
                g1 = vertical(q1)
                north = face(idx, t, q0, q1, m0, m1, g0, g1)
                dst[n, pad + idx, :, 128 * t : 128 * (t + 1)] = q0 + x[t] + (south - north)
                if isinstance(idx, int):
                    if idx == TOP and seam:
                        north = face(0, t, q0, q1, m0, m1, g0, g1)
                elif seam and k % 2 == 1 and k < chunk - 1:
                    at_seam = jnp.full((LEVELS, 128), idx, jnp.int32) == TOP
                    north = jnp.where(at_seam, face(0, t, q0, q1, m0, m1, g0, g1), north)
                out.append((q1, q2, d1, m1, g1, north))
        carry = out


def loop(count, body, unroll=1):
    def step(i, _):
        body(i)
        return 0

    lax.fori_loop(0, count, step, 0, unroll=unroll)


SALT = 24


def edges_of(x):
    return jnp.where(within(16, 32), roll(x[:, :128], 16), roll(x[:, 128:], 72))


def store_edges(base, k, x):
    x = [edges_of(y) for y in x]
    is_temp = within(8, 32) | within(56, 80)
    base[0, k] = jnp.where(is_temp, x[0], roll(x[1], SALT))
    for f in range(2, 8):
        base[f - 1, k] = jnp.where(is_temp, x[f], roll(x[f], SALT))


def inner_part(rows, cuts, mid, base, s0, s1, s2, s3, s4, cx, cy):
    def own(j):
        for n in TRACERS:
            s0[n, HALO + j] = rows[n, j]
        x = [rows[f, j] for f in range(8)]
        store_x(cx, HALO + j, *(x[f] for f in XF))
        store_y(cy, HALO + j, *(x[f] for f in YF))
        store_edges(base, j, x)

    loop(HEIGHT, own, 4)
    for src, dst, first, count in ((s0, s1, 0, 4), (s1, s2, 4, 3), (s2, s3, 4, 3), (s3, s4, 8, 2)):
        loop(count, lambda i: rows_forward(src, dst, cx, cy, HALO + first + 8 * i, 8, 2, 2))
    for n in TRACERS:
        for step, s in enumerate((s1, s2, s3), 1):
            low = HALO + 2 * step
            for k in range(4):
                cuts[step - 1, n, k] = s[n, low + k]
                cuts[step - 1, n, 4 + k] = s[n, EXT - 4 - low + k]

        def out(j, n=n):
            mid[n, j] = s4[n, 2 * HALO + j]

        loop(2 * HALO, out, 4)


def outer_part(flags, rows, ghost, cuts, mid, result, base, qa, qb, cx, cy):
    top = flags[1] == 1

    def near(k):
        for start in (0, HEIGHT - HALO):
            j = start + k
            for n in TRACERS:
                qa[n, HALO + j] = rows[n, j]
            store_x(cx, HALO + j, *(rows[f, j] for f in XF))
            store_y(cy, HALO + j, *(rows[f, j] for f in YF))

    loop(HALO, near, 4)
    store_y(cy, TOP - HALO, *(rows[f, HEIGHT - HALO - 1] for f in YF))

    def beyond(k, north):
        to = HEIGHT + k if north else k
        x = [ghost[f, k] for f in range(8)]
        store_edges(base, k, x)
        for n in TRACERS:
            qa[n, to] = x[n]
        store_x(cx, to, *(jnp.where(top, roll(x[f], -1), x[f]) if north else x[f] for f in XF))
        store_y(cy, to, *(x[f] for f in YF))

    loop(HALO, lambda k: beyond(k, False), 4)
    loop(HALO, lambda k: beyond(HALO + k, True), 4)

    def one(src, dst, step):
        low = HALO + 2 * step
        for n in TRACERS:
            for k in range(4):
                dst[n, low + k] = cuts[step - 1, n, k]
                dst[n, EXT - 4 - low + k] = cuts[step - 1, n, 4 + k]
        loop(2, lambda w: rows_forward(src, dst, cx, cy, 2 * step + w * (EXT - 8 - 4 * step), 8, 2, 2, seam=True))

    def two(i):
        one(qa, qb, 2 * i + 1)
        one(qb, qa, 2 * i + 2)

    loop(STEPS // 2, two)

    def out(j):
        for n in TRACERS:
            result[n, j] = qa[n, HALO + j]
            result[n, HEIGHT - HALO + j] = qa[n, HEIGHT + j]
            result[n, HALO + j] = mid[n, j]
            result[n, 2 * HALO + j] = mid[n, HALO + j]

    loop(HALO, out, 2)


def late_kernel(flags, rows, ghost, cuts, mid, result, base, beyond, my_cuts, my_mid, *scratch):
    states, (cx, cy) = scratch[:5], scratch[5:]

    @pl.when(flags[3] == 0)
    def _():
        inner_part(rows, my_cuts, my_mid, base, *states, cx, cy)

    @pl.when(flags[4] == 0)
    def _():
        @pl.when(flags[3] == 1)
        def _():
            def copy(k):
                for n in TRACERS:
                    for step in range(STEPS - 1):
                        my_cuts[step, n, k] = cuts[step, n, k]
                    my_mid[n, k] = mid[n, k]
                    my_mid[n, 8 + k] = mid[n, 8 + k]

            loop(8, copy, 4)

        outer_part(flags, rows, ghost, my_cuts, my_mid, result, beyond, *states[:2], cx, cy)


def edge_kernel(flags, base1, base2, beyond1, beyond2, odd_strip, even_strip, result1, result2, temp, salt, qa, qb, cx, cy, temp_out, salt_out, sems):
    top, inner_first, outer_first = flags[1] == 1, flags[3] == 1, flags[4] == 1
    lane = lanes(128)
    from_odd = (lane < 64).astype(jnp.int32) != flags[2]
    beside = within(8, 16) | within(72, 80) | within(32, 40) | within(96, 104)
    for_temp = within(8, 16) | within(72, 80)
    place = [within(8 * f, 8 * f + 8) | within(8 * f + 64, 8 * f + 72) for f in range(8)]

    def base(f, k):
        return jnp.where(inner_first, base1[f, k], base2[f, k])

    def beyond(f, k):
        return jnp.where(outer_first, beyond1[f, k], beyond2[f, k])

    def assemble(either, k, r, half, turn=None):
        a, b = odd_strip[r], even_strip[r]
        halo = jnp.where(from_odd, a, b) if half == 0 else jnp.where(from_odd, b, a)
        again = roll(halo, SALT)
        to = PAD + r + half * (EXT // 2)
        y = jnp.where(for_temp, roll(halo, 8 - 64 * half), roll(halo, SALT - 64 * half))
        qa[0, to] = jnp.where(beside, y, either(0, k))
        x = []
        for f in XF + YF:
            y = roll(jnp.where(place[f], halo, again), 8 - 8 * f - 64 * half)
            x.append(jnp.where(beside, y, either(f - 1, k)))
        if turn is not None:
            x[:3] = [jnp.where(turn, roll(z, -1), z) for z in x[:3]]
        store_x(cx, to, *x[:3])
        store_y(cy, to, *x[3:])

    def ghosts(k):
        assemble(beyond, k, k, 0)
        assemble(beyond, HALO + k, 2 * HALO + k, 1, top)

    loop(HALO, ghosts, 4)

    def own(k):
        assemble(base, k, HALO + k, 0)
        assemble(base, 2 * HALO + k, k, 1)

    loop(2 * HALO, own, 8)

    def two(_):
        for src, dst in ((qa, qb), (qb, qa)):
            loop(2, lambda i: rows_forward(src, dst, cx, cy, 2 + 22 * i, 22, 1, 1, seam=True, pad=PAD))

    loop(STEPS // 2, two)

    def patch(j):
        e = qa[0, PAD + HALO + j]
        for n, out in enumerate((temp_out, salt_out)):
            x = jnp.where(outer_first, result1[n, j], result2[n, j])
            w = jnp.where(lane < 8, roll(e, -16 - SALT * n), x[:, :128])
            z = jnp.where(lane >= 120, roll(e, 56 - SALT * n), x[:, 128:])
            for at, y in zip(places(j), (w, z)):
                out[at, :] = y

    copies = []
    for i in range(HEIGHT // 8):
        loop(8, lambda j: patch(8 * i + j), 8)
        for n, (x, y) in enumerate(((temp_out, temp), (salt_out, salt))):
            x = x.reshape(LEVELS, 2 * HEIGHT, 128)
            part = pl.ds(16 * i, 16)
            copies.append(pltpu.make_async_copy(x.at[:, part, :], y.at[:, part, :], sems.at[n, i]))
            copies[-1].start()
    for copy in copies:
        copy.wait()


def call(kernel, outs, args, scratch=(), args_in=None, flags=None, outs_in=VMEM):
    first = [] if flags is None else [flags]
    return pl.pallas_call(
        kernel,
        out_shape=[jax.ShapeDtypeStruct(s, F32) for s in outs],
        in_specs=[SMEM] * len(first) + (args_in or [VMEM] * len(args)),
        out_specs=[outs_in] * len(outs),
        scratch_shapes=[pltpu.VMEM(s, F32) if isinstance(s, tuple) else s for s in scratch],
        compiler_params=PARAMS,
        cost_estimate=COST,
    )(*first, *args)


ROW = (LEVELS, WIDTH)
TILE = (LEVELS, 128)
STRIP = (EXT // 2, *TILE)
STATE = (2, EXT, *ROW)
FLAT = (2 * LEVELS * HEIGHT, 128)


STATES = [STATE] * 5 + [(6, EXT, *ROW), (5, EXT, *ROW)]
OUTER = [STATE] * 2 + [(6, EXT, *ROW), (5, EXT, *ROW)]
RESULT = (2, HEIGHT, *ROW)
CUTS, MID, BASE, BEYOND = (STEPS, 2, 8, *ROW), (2, 2 * HALO, *ROW), (7, HEIGHT, *TILE), (7, 2 * HALO, *TILE)
GHOST = (8, 2 * HALO, *ROW)
IN_HBM = pl.BlockSpec(memory_space=pltpu.HBM)


def pack(flags, args):
    held = [pltpu.VMEM((2, LEVELS, 16, 128), x.dtype) for x in args]
    args = [pltpu.with_memory_space_constraint(x.reshape(LEVELS, -1, 128), pltpu.HBM) for x in args]
    return call(
        pack_kernel,
        [(MESSAGE, *ROW)] * 2 + [TILE],
        args,
        [*held, pltpu.SemaphoreType.DMA((9, 2))],
        [IN_HBM] * 9,
        flags,
    )


def transpose(flags, args, after):
    held = [pltpu.VMEM(FLAT, x.dtype) for x in args]
    args = [pltpu.with_memory_space_constraint(x, pltpu.HBM) for x in args]
    return call(
        rows_kernel,
        [(8, HEIGHT, *ROW), STRIP, STRIP, CUTS, MID, BASE],
        [*args, after],
        [*held, pltpu.SemaphoreType.DMA((9,)), *STATES],
        [IN_HBM] * 9 + [VMEM],
        flags,
    )


def fill_ghost(flags, *args):
    return call(
        ghost_kernel,
        [GHOST, STRIP, STRIP, RESULT, BEYOND],
        args,
        OUTER,
        flags=flags,
    )


def late(flags, rows, ghost, cuts, mid):
    return call(
        late_kernel,
        [RESULT, BASE, BEYOND],
        [rows, ghost, cuts, mid],
        [CUTS, MID, *STATES],
        flags=flags,
    )


def edge(flags, *args):
    return call(
        edge_kernel,
        [(LEVELS, 2 * HEIGHT, 128)] * 2,
        args,
        [(1, EDGE_DEPTH, *TILE)] * 2
        + [(6, EDGE_DEPTH, *TILE), (5, EDGE_DEPTH, *TILE), FLAT, FLAT, pltpu.SemaphoreType.DMA((2, HEIGHT // 8))],
        flags=flags,
        outs_in=IN_HBM,
    )


def on_device(lon_count, lat_count, *args):
    lon, lat = lax.axis_index("lon"), lax.axis_index("lat")
    top = (lat == lat_count - 1).astype(jnp.int32)
    place = lon % 8
    waits = (lat == lat_count - 2) & (place >= WAITS_FROM)
    inner_first = ((place < INNER_FIRST) | waits | (lat == lat_count - 1)).astype(jnp.int32)
    outer_first = (((place < OUTER_FIRST) & (lat < lat_count - 2)) | waits).astype(jnp.int32)
    flags = jnp.stack([lat % 2, top, lon % 2, inner_first, outer_first])
    flat = [level_major(x) for x in args]

    def index(i, j):
        return i * lat_count + j

    lons, lats = range(lon_count), range(lat_count)
    lat_even = [(index(i, j), index(i, j ^ 1)) for i in lons for j in lats]
    lat_odd = [
        (index(i, j), index(lon_count - 1 - i, j) if j == lat_count - 1 else index(i, j + 1 if j % 2 else j - 1))
        for i in lons
        for j in lats
        if j > 0
    ]
    lon_even = [(i, i ^ 1) for i in lons]
    lon_odd = [(i, (i + 1 if i % 2 else i - 1) % lon_count) for i in lons]
    both = ("lon", "lat")
    odd_msg, even_msg, packed = pack(flags, flat)
    odd_in = lax.ppermute(odd_msg, both, lat_odd)
    even_in = lax.ppermute(even_msg, both, lat_even)
    rows, east, west, cuts, mid, base1 = transpose(flags, flat, packed)
    ghost, odd_strip, even_strip, result1, beyond1 = fill_ghost(
        flags, rows, odd_in, even_in, east, west, cuts, mid
    )
    odd_strip = lax.ppermute(odd_strip, "lon", lon_odd)
    even_strip = lax.ppermute(even_strip, "lon", lon_even)
    result2, base2, beyond2 = late(flags, rows, ghost, cuts, mid)
    temp, salt = edge(flags, base1, base2, beyond1, beyond2, odd_strip, even_strip, result1, result2)
    return from_level_major(temp), from_level_major(salt)


def solution(mesh):
    spec = P(None, "lat", "lon")
    return jax.shard_map(
        functools.partial(on_device, mesh.shape["lon"], mesh.shape["lat"]),
        mesh=mesh,
        in_specs=(spec,) * 9,
        out_specs=(spec, spec),
        check_vma=False,
    )
```

```python
import functools

import jax
import jax.numpy as jnp
from jax import lax
from jax.experimental import pallas as pl
from jax.experimental.pallas import tpu as pltpu
from jax.sharding import PartitionSpec as P

STEPS = 4
HALO = 2 * STEPS
PAD = 4
INNER_FIRST = 4
OUTER_FIRST = 3
LEVELS = 8
HEIGHT = 32
WIDTH = 256
EXT = HEIGHT + 2 * HALO
TOP = HALO + HEIGHT - 1
EDGE_DEPTH = EXT + 2 * PAD
F32 = jnp.float32
VMEM = pl.BlockSpec(memory_space=pltpu.VMEM)
SMEM = pl.BlockSpec(memory_space=pltpu.SMEM)
PARAMS = pltpu.CompilerParams(vmem_limit_bytes=24 * 2**20)
COST = pl.CostEstimate(flops=50_000_000, bytes_accessed=8_000_000, transcendentals=0)

TRACERS, XF, YF = (0, 1), (2, 3, 4), (5, 6, 7)
FLIPPED = (2, 4, 5, 7)
MESSAGE = 2 * 8 + 3 * 6 + 3 * 7


def slot(field, k):
    if field < 2:
        return field * 8 + k
    if field < 5:
        return 16 + (field - 2) * 6 + k
    return 34 + (field - 5) * 7 + k


def rows_of(field):
    return 8 if field < 2 else 6 if field < 5 else 7


def level_major(x):
    x = x.reshape(LEVELS, HEIGHT // 8, 8, WIDTH // 128, 128)
    return x.transpose(0, 1, 3, 2, 4).reshape(-1, 128)


def from_level_major(x):
    x = x.reshape(LEVELS, HEIGHT // 8, WIDTH // 128, 8, 128)
    return x.transpose(0, 1, 3, 2, 4).reshape(LEVELS, HEIGHT, WIDTH)


def places(j):
    start = (j // 8) * 16 + j % 8
    return [pl.ds(start + 8 * c, LEVELS, stride=2 * HEIGHT) for c in range(2)]


def load_row(ref, j):
    return jnp.concatenate([ref[at, :] for at in places(j)], axis=1)


def lanes(width):
    return lax.broadcasted_iota(jnp.int32, (LEVELS, width), 1)


def within(lo, hi):
    lane = lanes(128)
    return (lane >= lo) & (lane < hi)


def roll(x, by):
    return pltpu.roll(x, by % x.shape[-1], 1)


def fields(held, at):
    temp, salt, u, v, diff, sx, sy, mu, mv = (at(ref) for ref in held)
    wet_u, wet_v = mu.astype(F32), mv.astype(F32)
    return temp, salt, u * wet_u, diff * wet_u, sx, v * wet_v, diff * wet_v, sy


def pack_kernel(flags, *refs):
    args, (odd_msg, even_msg, done), held, sems = refs[:9], refs[9:12], refs[12:21], refs[21]
    done[...] = jnp.zeros((LEVELS, 128), F32)
    copies = []
    for n, (x, y) in enumerate(zip(args, held)):
        for part, start in enumerate((0, 2 * HEIGHT - 16)):
            copies.append(pltpu.make_async_copy(x.at[:, pl.ds(start, 16), :], y.at[part], sems.at[n, part]))
    for copy in copies:
        copy.start()
    for copy in copies:
        copy.wait()

    odd = flags[0]

    def row(i):
        for msg, part in ((odd_msg, odd), (even_msg, 1 - odd)):
            k = jnp.where(part == 1, i, 7 - i)

            def at(ref):
                flat = ref.at[part].reshape(LEVELS * 16, 128)
                return jnp.concatenate([flat[pl.ds(8 * c + k, LEVELS, stride=16), :] for c in range(2)], axis=1)

            for f, x in enumerate(fields(held, at)):
                n = rows_of(f)
                msg[slot(f, 0) + jnp.clip(k - (8 - n) * part, 0, n - 1)] = x

    loop(8, row, 4)


def add_sides(parts, x, half):
    east, west = parts
    for f in range(8):
        to = 8 * f + 64 * half
        east = jnp.where(within(to, to + 8), roll(x[f][:, 128:], to + 8), east)
        to = 8 * f + 64 * (1 - half)
        west = jnp.where(within(to, to + 8), roll(x[f][:, :128], to), west)
    return east, west


def rows_kernel(flags, *refs):
    args, _, outs, held, sems = refs[:9], refs[9], refs[10:16], refs[16:25], refs[25]
    rows, east_own, west_own, cuts, mid, base = outs
    copies = [pltpu.make_async_copy(x, y, sems.at[n]) for n, (x, y) in enumerate(zip(args, held))]
    for copy in copies:
        copy.start()
    for copy in copies:
        copy.wait()

    def one(j):
        for f, x in enumerate(fields(held, lambda ref: load_row(ref, j))):
            rows[f, j] = x

    loop(HEIGHT, one, 4)

    def sides(r):
        parts = [jnp.zeros((LEVELS, 128), F32)] * 2
        for half in range(2):
            idx = r + half * (EXT // 2)
            j = jnp.clip(idx - HALO, 0, HEIGHT - 1)
            parts = add_sides(parts, [rows[f, j] for f in range(8)], half)
        east_own[r], west_own[r] = parts

    loop(EXT // 2, sides, 4)

    @pl.when(flags[3] == 1)
    def _():
        inner_part(rows, cuts, mid, base, *refs[26:])


def mirrored(x):
    n = x.shape[-1] // 128
    back = 127 - lanes(128)
    parts = [x[:, 128 * i : 128 * (i + 1)] for i in range(n)]
    return jnp.concatenate([jnp.take_along_axis(p, back, axis=1) for p in reversed(parts)], axis=1)


def fold_rows(msg, ghost):
    for f in range(8):
        n = rows_of(f)
        sign = -1.0 if f in FLIPPED else 1.0
        for k in range(n):
            x = mirrored(msg[slot(f, n - 1 - k)]) * sign
            if f < 5:
                ghost[f, HALO + k] = x
            elif k == 0:
                ghost[f, 0] = x
            else:
                ghost[f, HALO + k - 1] = x


def ghost_kernel(flags, rows, odd_msg, even_msg, east_own, west_own, cuts, mid, ghost, odd_strip, even_strip, result, base, *scratch):
    is_odd = flags[0] == 1
    for f in range(8):
        n = rows_of(f)
        for k in range(n):
            a, b = odd_msg[slot(f, k)], even_msg[slot(f, k)]
            ghost[f, HALO - n + k] = jnp.where(is_odd, b, a)
            if k < n - (f >= 5):
                ghost[f, HALO + k] = jnp.where(is_odd, a, b)
        if f >= 5:
            ghost[f, 0] = rows[f, HEIGHT - 1]

    @pl.when(flags[1] == 1)
    def _():
        fold_rows(odd_msg, ghost)

    swap = flags[2] == 1
    for r in range(EXT // 2):
        parts = [east_own[r], west_own[r]]
        if r < HALO:
            parts = add_sides(parts, [ghost[f, r] for f in range(8)], 0)
        if r >= 2 * HALO:
            parts = add_sides(parts, [ghost[f, r - HALO] for f in range(8)], 1)
        even_strip[r] = jnp.where(swap, parts[1], parts[0])
        odd_strip[r] = jnp.where(swap, parts[0], parts[1])

    @pl.when(flags[4] == 1)
    def _():
        outer_part(flags, rows, ghost, cuts, mid, result, *scratch)

    @pl.when(flags[5] == 1)
    def _():
        sides_beyond(ghost, base)


def minmod(p, t):
    return jnp.maximum(jnp.minimum(p, t), jnp.minimum(jnp.maximum(p, t), 0.0))


def vertical(q):
    level = lax.broadcasted_iota(jnp.int32, q.shape, 0)
    up = jnp.where(level == LEVELS - 1, q, pltpu.roll(q, LEVELS - 1, 0))
    down = jnp.where(level == 0, q, pltpu.roll(q, 1, 0))
    return up - down


def shifted(tiles, by):
    lane = lanes(128)
    rolled = [roll(t, by) for t in tiles]
    if len(tiles) == 1:
        return rolled
    seam = lane == (0 if by == 1 else 127)
    return [jnp.where(seam, rolled[1 - n], rolled[n]) for n in range(2)]


def coefficients(c, r, s):
    plus, minus = jnp.maximum(c, 0.0), jnp.minimum(c, 0.0)
    return (
        plus + r,
        0.5 * plus * (1.0 - plus),
        0.25 * r * s,
        minus - r,
        -0.5 * minus * (1.0 + minus),
    )


def store_x(cx, idx, c, r, s):
    p, lp, t, e, ln = coefficients(c, r, s)
    for n, x in enumerate((p, lp, t, roll(e, 1), roll(ln, 1), roll(t, 1))):
        cx[n, idx] = x


def store_y(cy, idx, c, r, s):
    for n, x in enumerate(coefficients(c, r, s)):
        cy[n, idx] = x


def rows_forward(src, dst, cx, cy, first, chunk, streams, tiles, seam=False, pad=0):
    def at(ref, n, idx, t):
        return ref[n, pad + idx, :, 128 * t : 128 * (t + 1)]

    def face(idx, t, q0, q1, m0, m1, g0, g1):
        c = [at(cy, n, idx, t) for n in range(5)]
        return (c[0] * q0 + c[3] * q1) + (c[1] * m0 + c[4] * m1) + c[2] * (g0 + g1)

    south = jnp.where(first == TOP + 1, 0, first - 1)
    carry = []
    for n in range(streams):
        for t in range(tiles):
            q = [at(src, n, first - 2 + k, t) for k in range(4)]
            d = [q[k + 1] - q[k] for k in range(3)]
            m0, m1 = minmod(d[0], d[1]), minmod(d[1], d[2])
            g0, g1 = vertical(q[1]), vertical(q[2])
            carry.append((q[2], q[3], d[2], m1, g1, face(south, t, q[1], q[2], m0, m1, g0, g1)))
    for k in range(chunk):
        idx = first + k
        out = []
        for n in range(streams):
            q0 = [carry[n * tiles + t][0] for t in range(tiles)]
            d = [x - y for x, y in zip(shifted(q0, -1), q0)]
            m = [minmod(x, y) for x, y in zip(d, shifted(d, 1))]
            a, b = [], []
            for t in range(tiles):
                g0 = carry[n * tiles + t][4]
                c = [at(cx, i, idx, t) for i in range(6)]
                a.append(c[0] * q0[t] + c[1] * m[t] + c[2] * g0)
                b.append(c[3] * q0[t] + c[4] * m[t] + c[5] * g0)
            x = [(b[t] - a[t]) + (p - r) for t, (p, r) in enumerate(zip(shifted(a, 1), shifted(b, -1)))]
            for t in range(tiles):
                q0, q1, d0, m0, g0, south = carry[n * tiles + t]
                q2 = at(src, n, idx + 2, t)
                d1 = q2 - q1
                m1 = minmod(d0, d1)
                g1 = vertical(q1)
                north = face(idx, t, q0, q1, m0, m1, g0, g1)
                dst[n, pad + idx, :, 128 * t : 128 * (t + 1)] = q0 + x[t] + (south - north)
                if isinstance(idx, int):
                    if idx == TOP and seam:
                        north = face(0, t, q0, q1, m0, m1, g0, g1)
                elif seam and k % 2 == 1 and k < chunk - 1:
                    at_seam = jnp.full((LEVELS, 128), idx, jnp.int32) == TOP
                    north = jnp.where(at_seam, face(0, t, q0, q1, m0, m1, g0, g1), north)
                out.append((q1, q2, d1, m1, g1, north))
        carry = out


def loop(count, body, unroll=1):
    def step(i, _):
        body(i)
        return 0

    lax.fori_loop(0, count, step, 0, unroll=unroll)


SALT = 24


def edges_of(x):
    return jnp.where(within(16, 32), roll(x[:, :128], 16), roll(x[:, 128:], 72))


def store_edges(base, k, x):
    x = [edges_of(y) for y in x]
    is_temp = within(8, 32) | within(56, 80)
    base[0, k] = jnp.where(is_temp, x[0], roll(x[1], SALT))
    for f in range(2, 8):
        base[f - 1, k] = jnp.where(is_temp, x[f], roll(x[f], SALT))


def inner_part(rows, cuts, mid, base, s0, s1, s2, s3, s4, cx, cy):
    def own(j):
        for n in TRACERS:
            s0[n, HALO + j] = rows[n, j]
        x = [rows[f, j] for f in range(8)]
        store_x(cx, HALO + j, *(x[f] for f in XF))
        store_y(cy, HALO + j, *(x[f] for f in YF))
        store_edges(base, j, x)

    loop(HEIGHT, own, 4)
    for src, dst, first, count in ((s0, s1, 0, 4), (s1, s2, 4, 3), (s2, s3, 4, 3), (s3, s4, 8, 2)):
        loop(count, lambda i: rows_forward(src, dst, cx, cy, HALO + first + 8 * i, 8, 2, 2))
    for n in TRACERS:
        for step, s in enumerate((s1, s2, s3), 1):
            low = HALO + 2 * step
            for k in range(4):
                cuts[step - 1, n, k] = s[n, low + k]
                cuts[step - 1, n, 4 + k] = s[n, EXT - 4 - low + k]

        def out(j, n=n):
            mid[n, j] = s4[n, 2 * HALO + j]

        loop(2 * HALO, out, 4)


def sides_beyond(ghost, base):
    loop(2 * HALO, lambda k: store_edges(base, k, [ghost[f, k] for f in range(8)]), 4)


def outer_part(flags, rows, ghost, cuts, mid, result, qa, qb, cx, cy):
    top = flags[1] == 1

    def near(k):
        for start in (0, HEIGHT - HALO):
            j = start + k
            for n in TRACERS:
                qa[n, HALO + j] = rows[n, j]
            store_x(cx, HALO + j, *(rows[f, j] for f in XF))
            store_y(cy, HALO + j, *(rows[f, j] for f in YF))

    loop(HALO, near, 4)
    store_y(cy, TOP - HALO, *(rows[f, HEIGHT - HALO - 1] for f in YF))

    def beyond(k, north):
        to = HEIGHT + k if north else k
        x = [ghost[f, k] for f in range(8)]
        for n in TRACERS:
            qa[n, to] = x[n]
        store_x(cx, to, *(jnp.where(top, roll(x[f], -1), x[f]) if north else x[f] for f in XF))
        store_y(cy, to, *(x[f] for f in YF))

    loop(HALO, lambda k: beyond(k, False), 4)
    loop(HALO, lambda k: beyond(HALO + k, True), 4)

    def one(src, dst, step):
        low = HALO + 2 * step
        for n in TRACERS:
            for k in range(4):
                dst[n, low + k] = cuts[step - 1, n, k]
                dst[n, EXT - 4 - low + k] = cuts[step - 1, n, 4 + k]
        loop(2, lambda w: rows_forward(src, dst, cx, cy, 2 * step + w * (EXT - 8 - 4 * step), 8, 2, 2, seam=True))

    def two(i):
        one(qa, qb, 2 * i + 1)
        one(qb, qa, 2 * i + 2)

    loop(STEPS // 2, two)

    def out(j):
        for n in TRACERS:
            result[n, j] = qa[n, HALO + j]
            result[n, HEIGHT - HALO + j] = qa[n, HEIGHT + j]
            result[n, HALO + j] = mid[n, j]
            result[n, 2 * HALO + j] = mid[n, HALO + j]

    loop(HALO, out, 2)


def late_kernel(flags, rows, ghost, cuts, mid, result, base, beyond, my_cuts, my_mid, *scratch):
    states, (cx, cy) = scratch[:5], scratch[5:]

    @pl.when(flags[3] == 0)
    def _():
        inner_part(rows, my_cuts, my_mid, base, *states, cx, cy)

    @pl.when(flags[4] == 0)
    def _():
        @pl.when(flags[3] == 1)
        def _():
            def copy(k):
                for n in TRACERS:
                    for step in range(STEPS - 1):
                        my_cuts[step, n, k] = cuts[step, n, k]
                    my_mid[n, k] = mid[n, k]
                    my_mid[n, 8 + k] = mid[n, 8 + k]

            loop(8, copy, 4)

        outer_part(flags, rows, ghost, my_cuts, my_mid, result, *states[:2], cx, cy)

    @pl.when(flags[5] == 0)
    def _():
        sides_beyond(ghost, beyond)


def edge_kernel(flags, base1, base2, beyond1, beyond2, odd_strip, even_strip, result1, result2, temp, salt, qa, qb, cx, cy, temp_out, salt_out, sems):
    top, inner_first, outer_first, sides_first = (flags[n] == 1 for n in (1, 3, 4, 5))
    lane = lanes(128)
    from_odd = (lane < 64).astype(jnp.int32) != flags[2]
    beside = within(8, 16) | within(72, 80) | within(32, 40) | within(96, 104)
    for_temp = within(8, 16) | within(72, 80)
    place = [within(8 * f, 8 * f + 8) | within(8 * f + 64, 8 * f + 72) for f in range(8)]

    def base(f, k):
        return jnp.where(inner_first, base1[f, k], base2[f, k])

    def beyond(f, k):
        return jnp.where(sides_first, beyond1[f, k], beyond2[f, k])

    def assemble(either, k, r, half, turn=None):
        a, b = odd_strip[r], even_strip[r]
        halo = jnp.where(from_odd, a, b) if half == 0 else jnp.where(from_odd, b, a)
        again = roll(halo, SALT)
        to = PAD + r + half * (EXT // 2)
        y = jnp.where(for_temp, roll(halo, 8 - 64 * half), roll(halo, SALT - 64 * half))
        qa[0, to] = jnp.where(beside, y, either(0, k))
        x = []
        for f in XF + YF:
            y = roll(jnp.where(place[f], halo, again), 8 - 8 * f - 64 * half)
            x.append(jnp.where(beside, y, either(f - 1, k)))
        if turn is not None:
            x[:3] = [jnp.where(turn, roll(z, -1), z) for z in x[:3]]
        store_x(cx, to, *x[:3])
        store_y(cy, to, *x[3:])

    def ghosts(k):
        assemble(beyond, k, k, 0)
        assemble(beyond, HALO + k, 2 * HALO + k, 1, top)

    loop(HALO, ghosts, 4)

    def own(k):
        assemble(base, k, HALO + k, 0)
        assemble(base, 2 * HALO + k, k, 1)

    loop(2 * HALO, own, 8)

    def two(_):
        for src, dst in ((qa, qb), (qb, qa)):
            loop(2, lambda i: rows_forward(src, dst, cx, cy, 2 + 22 * i, 22, 1, 1, seam=True, pad=PAD))

    loop(STEPS // 2, two)

    def patch(j):
        e = qa[0, PAD + HALO + j]
        for n, out in enumerate((temp_out, salt_out)):
            x = jnp.where(outer_first, result1[n, j], result2[n, j])
            w = jnp.where(lane < 8, roll(e, -16 - SALT * n), x[:, :128])
            z = jnp.where(lane >= 120, roll(e, 56 - SALT * n), x[:, 128:])
            for at, y in zip(places(j), (w, z)):
                out[at, :] = y

    copies = []
    for i in range(HEIGHT // 8):
        loop(8, lambda j: patch(8 * i + j), 8)
        for n, (x, y) in enumerate(((temp_out, temp), (salt_out, salt))):
            x = x.reshape(LEVELS, 2 * HEIGHT, 128)
            part = pl.ds(16 * i, 16)
            copies.append(pltpu.make_async_copy(x.at[:, part, :], y.at[:, part, :], sems.at[n, i]))
            copies[-1].start()
    for copy in copies:
        copy.wait()


def call(kernel, outs, args, scratch=(), args_in=None, flags=None, outs_in=VMEM):
    first = [] if flags is None else [flags]
    return pl.pallas_call(
        kernel,
        out_shape=[jax.ShapeDtypeStruct(s, F32) for s in outs],
        in_specs=[SMEM] * len(first) + (args_in or [VMEM] * len(args)),
        out_specs=[outs_in] * len(outs),
        scratch_shapes=[pltpu.VMEM(s, F32) if isinstance(s, tuple) else s for s in scratch],
        compiler_params=PARAMS,
        cost_estimate=COST,
    )(*first, *args)


ROW = (LEVELS, WIDTH)
TILE = (LEVELS, 128)
STRIP = (EXT // 2, *TILE)
STATE = (2, EXT, *ROW)
FLAT = (2 * LEVELS * HEIGHT, 128)


STATES = [STATE] * 5 + [(6, EXT, *ROW), (5, EXT, *ROW)]
OUTER = [STATE] * 2 + [(6, EXT, *ROW), (5, EXT, *ROW)]
RESULT = (2, HEIGHT, *ROW)
CUTS, MID, BASE, BEYOND = (STEPS, 2, 8, *ROW), (2, 2 * HALO, *ROW), (7, HEIGHT, *TILE), (7, 2 * HALO, *TILE)
GHOST = (8, 2 * HALO, *ROW)
IN_HBM = pl.BlockSpec(memory_space=pltpu.HBM)


def pack(flags, args):
    held = [pltpu.VMEM((2, LEVELS, 16, 128), x.dtype) for x in args]
    args = [pltpu.with_memory_space_constraint(x.reshape(LEVELS, -1, 128), pltpu.HBM) for x in args]
    return call(
        pack_kernel,
        [(MESSAGE, *ROW)] * 2 + [TILE],
        args,
        [*held, pltpu.SemaphoreType.DMA((9, 2))],
        [IN_HBM] * 9,
        flags,
    )


def transpose(flags, args, after):
    held = [pltpu.VMEM(FLAT, x.dtype) for x in args]
    args = [pltpu.with_memory_space_constraint(x, pltpu.HBM) for x in args]
    return call(
        rows_kernel,
        [(8, HEIGHT, *ROW), STRIP, STRIP, CUTS, MID, BASE],
        [*args, after],
        [*held, pltpu.SemaphoreType.DMA((9,)), *STATES],
        [IN_HBM] * 9 + [VMEM],
        flags,
    )


def fill_ghost(flags, *args):
    return call(
        ghost_kernel,
        [GHOST, STRIP, STRIP, RESULT, BEYOND],
        args,
        OUTER,
        flags=flags,
    )


def late(flags, rows, ghost, cuts, mid):
    return call(
        late_kernel,
        [RESULT, BASE, BEYOND],
        [rows, ghost, cuts, mid],
        [CUTS, MID, *STATES],
        flags=flags,
    )


def edge(flags, *args):
    return call(
        edge_kernel,
        [(LEVELS, 2 * HEIGHT, 128)] * 2,
        args,
        [(1, EDGE_DEPTH, *TILE)] * 2
        + [(6, EDGE_DEPTH, *TILE), (5, EDGE_DEPTH, *TILE), FLAT, FLAT, pltpu.SemaphoreType.DMA((2, HEIGHT // 8))],
        flags=flags,
        outs_in=IN_HBM,
    )


def on_device(lon_count, lat_count, *args):
    lon, lat = lax.axis_index("lon"), lax.axis_index("lat")
    top = (lat == lat_count - 1).astype(jnp.int32)
    place = lon % 8
    inner_first = ((place < INNER_FIRST) | (lat >= lat_count - 2)).astype(jnp.int32)
    outer_first = ((place < OUTER_FIRST) & (lat < lat_count - 2)).astype(jnp.int32)
    sides_first = (place < INNER_FIRST).astype(jnp.int32)
    flags = jnp.stack([lat % 2, top, lon % 2, inner_first, outer_first, sides_first])
    flat = [level_major(x) for x in args]

    def index(i, j):
        return i * lat_count + j

    lons, lats = range(lon_count), range(lat_count)
    lat_even = [(index(i, j), index(i, j ^ 1)) for i in lons for j in lats]
    lat_odd = [
        (index(i, j), index(lon_count - 1 - i, j) if j == lat_count - 1 else index(i, j + 1 if j % 2 else j - 1))
        for i in lons
        for j in lats
        if j > 0
    ]
    lon_even = [(i, i ^ 1) for i in lons]
    lon_odd = [(i, (i + 1 if i % 2 else i - 1) % lon_count) for i in lons]
    both = ("lon", "lat")
    odd_msg, even_msg, packed = pack(flags, flat)
    odd_in = lax.ppermute(odd_msg, both, lat_odd)
    even_in = lax.ppermute(even_msg, both, lat_even)
    rows, east, west, cuts, mid, base1 = transpose(flags, flat, packed)
    ghost, odd_strip, even_strip, result1, beyond1 = fill_ghost(
        flags, rows, odd_in, even_in, east, west, cuts, mid
    )
    odd_strip = lax.ppermute(odd_strip, "lon", lon_odd)
    even_strip = lax.ppermute(even_strip, "lon", lon_even)
    result2, base2, beyond2 = late(flags, rows, ghost, cuts, mid)
    temp, salt = edge(flags, base1, base2, beyond1, beyond2, odd_strip, even_strip, result1, result2)
    return from_level_major(temp), from_level_major(salt)


def solution(mesh):
    spec = P(None, "lat", "lon")
    return jax.shard_map(
        functools.partial(on_device, mesh.shape["lon"], mesh.shape["lat"]),
        mesh=mesh,
        in_specs=(spec,) * 9,
        out_specs=(spec, spec),
        check_vma=False,
    )
```

```python
import functools

import jax
import jax.numpy as jnp
from jax import lax
from jax.experimental import pallas as pl
from jax.experimental.pallas import tpu as pltpu
from jax.sharding import PartitionSpec as P

STEPS = 4
HALO = 2 * STEPS
PAD = 4
INNER_FIRST = 4
OUTER_FIRST = 3
LEVELS = 8
HEIGHT = 32
WIDTH = 256
EXT = HEIGHT + 2 * HALO
TOP = HALO + HEIGHT - 1
EDGE_DEPTH = EXT + 2 * PAD
F32 = jnp.float32
VMEM = pl.BlockSpec(memory_space=pltpu.VMEM)
SMEM = pl.BlockSpec(memory_space=pltpu.SMEM)
PARAMS = pltpu.CompilerParams(vmem_limit_bytes=24 * 2**20)
COST = pl.CostEstimate(flops=50_000_000, bytes_accessed=8_000_000, transcendentals=0)

TRACERS, XF, YF = (0, 1), (2, 3, 4), (5, 6, 7)
FLIPPED = (2, 4, 5, 7)
MESSAGE = 2 * 8 + 3 * 6 + 3 * 7


def slot(field, k):
    if field < 2:
        return field * 8 + k
    if field < 5:
        return 16 + (field - 2) * 6 + k
    return 34 + (field - 5) * 7 + k


def rows_of(field):
    return 8 if field < 2 else 6 if field < 5 else 7


def level_major(x):
    x = x.reshape(LEVELS, HEIGHT // 8, 8, WIDTH // 128, 128)
    return x.transpose(0, 1, 3, 2, 4).reshape(-1, 128)


def from_level_major(x):
    x = x.reshape(LEVELS, HEIGHT // 8, WIDTH // 128, 8, 128)
    return x.transpose(0, 1, 3, 2, 4).reshape(LEVELS, HEIGHT, WIDTH)


def places(j):
    start = (j // 8) * 16 + j % 8
    return [pl.ds(start + 8 * c, LEVELS, stride=2 * HEIGHT) for c in range(2)]


def load_row(ref, j):
    return jnp.concatenate([ref[at, :] for at in places(j)], axis=1)


def lanes(width):
    return lax.broadcasted_iota(jnp.int32, (LEVELS, width), 1)


def within(lo, hi):
    lane = lanes(128)
    return (lane >= lo) & (lane < hi)


def roll(x, by):
    return pltpu.roll(x, by % x.shape[-1], 1)


def fields(held, at):
    temp, salt, u, v, diff, sx, sy, mu, mv = (at(ref) for ref in held)
    wet_u, wet_v = mu.astype(F32), mv.astype(F32)
    return temp, salt, u * wet_u, diff * wet_u, sx, v * wet_v, diff * wet_v, sy


def pack_kernel(flags, *refs):
    args, (odd_msg, even_msg, done), held, sems = refs[:9], refs[9:12], refs[12:21], refs[21]
    done[...] = jnp.zeros((LEVELS, 128), F32)
    copies = []
    for n, (x, y) in enumerate(zip(args, held)):
        for part, start in enumerate((0, 2 * HEIGHT - 16)):
            copies.append(pltpu.make_async_copy(x.at[:, pl.ds(start, 16), :], y.at[part], sems.at[n, part]))
    for n in (0, 1, 2, 4, 5, 7, 3, 6, 8):
        copies[2 * n].start()
        copies[2 * n + 1].start()
    odd = flags[0]

    def put(group, make):
        def row(i):
            for msg, part in ((odd_msg, odd), (even_msg, 1 - odd)):
                k = jnp.where(part == 1, i, 7 - i)

                def at(n):
                    flat = held[n].at[part].reshape(LEVELS * 16, 128)
                    return jnp.concatenate([flat[pl.ds(8 * c + k, LEVELS, stride=16), :] for c in range(2)], axis=1)

                for f, x in zip(group, make(at)):
                    n = rows_of(f)
                    msg[slot(f, 0) + jnp.clip(k - (8 - n) * part, 0, n - 1)] = x

        loop(8, row, 4)

    def face(at, c, slope, mask):
        wet = at(mask).astype(F32)
        return at(c) * wet, at(4) * wet, at(slope)

    for group, needs, make in (
        (TRACERS, (0, 1), lambda at: (at(0), at(1))),
        (XF, (2, 4, 5, 7), lambda at: face(at, 2, 5, 7)),
        (YF, (3, 6, 8), lambda at: face(at, 3, 6, 8)),
    ):
        for n in needs:
            copies[2 * n].wait()
            copies[2 * n + 1].wait()
        put(group, make)


def add_sides(parts, x, half):
    east, west = parts
    for f in range(8):
        to = 8 * f + 64 * half
        east = jnp.where(within(to, to + 8), roll(x[f][:, 128:], to + 8), east)
        to = 8 * f + 64 * (1 - half)
        west = jnp.where(within(to, to + 8), roll(x[f][:, :128], to), west)
    return east, west


def rows_kernel(flags, *refs):
    args, _, outs, held, sems = refs[:9], refs[9], refs[10:16], refs[16:25], refs[25]
    rows, east_own, west_own, cuts, mid, base = outs
    copies = [pltpu.make_async_copy(x, y, sems.at[n]) for n, (x, y) in enumerate(zip(args, held))]
    for copy in copies:
        copy.start()
    for copy in copies:
        copy.wait()

    def one(j):
        for f, x in enumerate(fields(held, lambda ref: load_row(ref, j))):
            rows[f, j] = x

    loop(HEIGHT, one, 4)

    def sides(r):
        parts = [jnp.zeros((LEVELS, 128), F32)] * 2
        for half in range(2):
            idx = r + half * (EXT // 2)
            j = jnp.clip(idx - HALO, 0, HEIGHT - 1)
            parts = add_sides(parts, [rows[f, j] for f in range(8)], half)
        east_own[r], west_own[r] = parts

    loop(EXT // 2, sides, 4)

    @pl.when(flags[3] == 1)
    def _():
        inner_part(rows, cuts, mid, base, *refs[26:])


def mirrored(x):
    n = x.shape[-1] // 128
    back = 127 - lanes(128)
    parts = [x[:, 128 * i : 128 * (i + 1)] for i in range(n)]
    return jnp.concatenate([jnp.take_along_axis(p, back, axis=1) for p in reversed(parts)], axis=1)


def fold_rows(msg, ghost):
    for f in range(8):
        n = rows_of(f)
        sign = -1.0 if f in FLIPPED else 1.0
        for k in range(n):
            x = mirrored(msg[slot(f, n - 1 - k)]) * sign
            if f < 5:
                ghost[f, HALO + k] = x
            elif k == 0:
                ghost[f, 0] = x
            else:
                ghost[f, HALO + k - 1] = x


def ghost_kernel(flags, rows, odd_msg, even_msg, east_own, west_own, cuts, mid, ghost, odd_strip, even_strip, result, base, q, cx, cy, qa, qb):
    is_odd = flags[0] == 1
    for f in range(8):
        n = rows_of(f)
        for k in range(n):
            a, b = odd_msg[slot(f, k)], even_msg[slot(f, k)]
            ghost[f, HALO - n + k] = jnp.where(is_odd, b, a)
            if k < n - (f >= 5):
                ghost[f, HALO + k] = jnp.where(is_odd, a, b)
        if f >= 5:
            ghost[f, 0] = rows[f, HEIGHT - 1]

    @pl.when(flags[1] == 1)
    def _():
        fold_rows(odd_msg, ghost)

    swap = flags[2] == 1
    for r in range(EXT // 2):
        parts = [east_own[r], west_own[r]]
        if r < HALO:
            parts = add_sides(parts, [ghost[f, r] for f in range(8)], 0)
        if r >= 2 * HALO:
            parts = add_sides(parts, [ghost[f, r - HALO] for f in range(8)], 1)
        even_strip[r] = jnp.where(swap, parts[1], parts[0])
        odd_strip[r] = jnp.where(swap, parts[0], parts[1])

    @pl.when(flags[5] == 1)
    def _():
        sides_beyond(ghost, base)
        outer_prepare(flags, rows, ghost, q, cx, cy)

    @pl.when(flags[4] == 1)
    def _():
        start_from(q, qa)
        outer_steps(cuts, mid, result, qa, qb, cx, cy)


def start_from(q, qa):
    def copy(k):
        for n in TRACERS:
            qa[n, k] = q[n, k]
            qa[n, EXT - 12 + k] = q[n, EXT - 12 + k]

    loop(12, copy, 4)


def minmod(p, t):
    return jnp.maximum(jnp.minimum(p, t), jnp.minimum(jnp.maximum(p, t), 0.0))


def vertical(q):
    level = lax.broadcasted_iota(jnp.int32, q.shape, 0)
    up = jnp.where(level == LEVELS - 1, q, pltpu.roll(q, LEVELS - 1, 0))
    down = jnp.where(level == 0, q, pltpu.roll(q, 1, 0))
    return up - down


def shifted(tiles, by):
    lane = lanes(128)
    rolled = [roll(t, by) for t in tiles]
    if len(tiles) == 1:
        return rolled
    seam = lane == (0 if by == 1 else 127)
    return [jnp.where(seam, rolled[1 - n], rolled[n]) for n in range(2)]


def coefficients(c, r, s):
    plus, minus = jnp.maximum(c, 0.0), jnp.minimum(c, 0.0)
    return (
        plus + r,
        0.5 * plus * (1.0 - plus),
        0.25 * r * s,
        minus - r,
        -0.5 * minus * (1.0 + minus),
    )


def store_x(cx, idx, c, r, s):
    p, lp, t, e, ln = coefficients(c, r, s)
    for n, x in enumerate((p, lp, t, roll(e, 1), roll(ln, 1), roll(t, 1))):
        cx[n, idx] = x


def store_y(cy, idx, c, r, s):
    for n, x in enumerate(coefficients(c, r, s)):
        cy[n, idx] = x


def rows_forward(src, dst, cx, cy, first, chunk, streams, tiles, seam=False, pad=0):
    def at(ref, n, idx, t):
        return ref[n, pad + idx, :, 128 * t : 128 * (t + 1)]

    def face(idx, t, q0, q1, m0, m1, g0, g1):
        c = [at(cy, n, idx, t) for n in range(5)]
        return (c[0] * q0 + c[3] * q1) + (c[1] * m0 + c[4] * m1) + c[2] * (g0 + g1)

    south = jnp.where(first == TOP + 1, 0, first - 1)
    carry = []
    for n in range(streams):
        for t in range(tiles):
            q = [at(src, n, first - 2 + k, t) for k in range(4)]
            d = [q[k + 1] - q[k] for k in range(3)]
            m0, m1 = minmod(d[0], d[1]), minmod(d[1], d[2])
            g0, g1 = vertical(q[1]), vertical(q[2])
            carry.append((q[2], q[3], d[2], m1, g1, face(south, t, q[1], q[2], m0, m1, g0, g1)))
    for k in range(chunk):
        idx = first + k
        out = []
        for n in range(streams):
            q0 = [carry[n * tiles + t][0] for t in range(tiles)]
            d = [x - y for x, y in zip(shifted(q0, -1), q0)]
            m = [minmod(x, y) for x, y in zip(d, shifted(d, 1))]
            a, b = [], []
            for t in range(tiles):
                g0 = carry[n * tiles + t][4]
                c = [at(cx, i, idx, t) for i in range(6)]
                a.append(c[0] * q0[t] + c[1] * m[t] + c[2] * g0)
                b.append(c[3] * q0[t] + c[4] * m[t] + c[5] * g0)
            x = [(b[t] - a[t]) + (p - r) for t, (p, r) in enumerate(zip(shifted(a, 1), shifted(b, -1)))]
            for t in range(tiles):
                q0, q1, d0, m0, g0, south = carry[n * tiles + t]
                q2 = at(src, n, idx + 2, t)
                d1 = q2 - q1
                m1 = minmod(d0, d1)
                g1 = vertical(q1)
                north = face(idx, t, q0, q1, m0, m1, g0, g1)
                dst[n, pad + idx, :, 128 * t : 128 * (t + 1)] = q0 + x[t] + (south - north)
                if isinstance(idx, int):
                    if idx == TOP and seam:
                        north = face(0, t, q0, q1, m0, m1, g0, g1)
                elif seam and k % 2 == 1 and k < chunk - 1:
                    at_seam = jnp.full((LEVELS, 128), idx, jnp.int32) == TOP
                    north = jnp.where(at_seam, face(0, t, q0, q1, m0, m1, g0, g1), north)
                out.append((q1, q2, d1, m1, g1, north))
        carry = out


def loop(count, body, unroll=1):
    def step(i, _):
        body(i)
        return 0

    lax.fori_loop(0, count, step, 0, unroll=unroll)


SALT = 24


def edges_of(x):
    return jnp.where(within(16, 32), roll(x[:, :128], 16), roll(x[:, 128:], 72))


def store_edges(base, k, x):
    x = [edges_of(y) for y in x]
    is_temp = within(8, 32) | within(56, 80)
    base[0, k] = jnp.where(is_temp, x[0], roll(x[1], SALT))
    for f in range(2, 8):
        base[f - 1, k] = jnp.where(is_temp, x[f], roll(x[f], SALT))


def inner_part(rows, cuts, mid, base, s0, s1, s2, s3, s4, cx, cy):
    def own(j):
        for n in TRACERS:
            s0[n, HALO + j] = rows[n, j]
        x = [rows[f, j] for f in range(8)]
        store_x(cx, HALO + j, *(x[f] for f in XF))
        store_y(cy, HALO + j, *(x[f] for f in YF))
        store_edges(base, j, x)

    loop(HEIGHT, own, 4)
    for src, dst, first, count in ((s0, s1, 0, 4), (s1, s2, 4, 3), (s2, s3, 4, 3), (s3, s4, 8, 2)):
        loop(count, lambda i: rows_forward(src, dst, cx, cy, HALO + first + 8 * i, 8, 2, 2))
    for n in TRACERS:
        for step, s in enumerate((s1, s2, s3), 1):
            low = HALO + 2 * step
            for k in range(4):
                cuts[step - 1, n, k] = s[n, low + k]
                cuts[step - 1, n, 4 + k] = s[n, EXT - 4 - low + k]

        def out(j, n=n):
            mid[n, j] = s4[n, 2 * HALO + j]

        loop(2 * HALO, out, 4)


def sides_beyond(ghost, base):
    loop(2 * HALO, lambda k: store_edges(base, k, [ghost[f, k] for f in range(8)]), 4)


def outer_prepare(flags, rows, ghost, q, cx, cy):
    top = flags[1] == 1

    def near(k):
        for start in (0, HEIGHT - HALO):
            j = start + k
            for n in TRACERS:
                q[n, HALO + j] = rows[n, j]
            store_x(cx, HALO + j, *(rows[f, j] for f in XF))
            store_y(cy, HALO + j, *(rows[f, j] for f in YF))

    loop(HALO, near, 4)
    store_y(cy, TOP - HALO, *(rows[f, HEIGHT - HALO - 1] for f in YF))

    def beyond(k, north):
        to = HEIGHT + k if north else k
        x = [ghost[f, k] for f in range(8)]
        for n in TRACERS:
            q[n, to] = x[n]
        store_x(cx, to, *(jnp.where(top, roll(x[f], -1), x[f]) if north else x[f] for f in XF))
        store_y(cy, to, *(x[f] for f in YF))

    loop(HALO, lambda k: beyond(k, False), 4)
    loop(HALO, lambda k: beyond(HALO + k, True), 4)


def outer_steps(cuts, mid, result, qa, qb, cx, cy):
    def one(src, dst, step):
        low = HALO + 2 * step
        for n in TRACERS:
            for k in range(4):
                dst[n, low + k] = cuts[step - 1, n, k]
                dst[n, EXT - 4 - low + k] = cuts[step - 1, n, 4 + k]
        loop(2, lambda w: rows_forward(src, dst, cx, cy, 2 * step + w * (EXT - 8 - 4 * step), 8, 2, 2, seam=True))

    def two(i):
        one(qa, qb, 2 * i + 1)
        one(qb, qa, 2 * i + 2)

    loop(STEPS // 2, two)

    def out(j):
        for n in TRACERS:
            result[n, j] = qa[n, HALO + j]
            result[n, HEIGHT - HALO + j] = qa[n, HEIGHT + j]
            result[n, HALO + j] = mid[n, j]
            result[n, 2 * HALO + j] = mid[n, HALO + j]

    loop(HALO, out, 2)


def late_kernel(flags, rows, ghost, cuts, mid, q, cx, cy, result, base, beyond, my_cuts, my_mid, *scratch):
    states, (my_cx, my_cy) = scratch[:5], scratch[5:]
    qa, qb = states[:2]

    @pl.when(flags[3] == 0)
    def _():
        inner_part(rows, my_cuts, my_mid, base, *states, my_cx, my_cy)

    @pl.when((flags[5] == 1) & (flags[4] == 0))
    def _():
        start_from(q, qa)
        outer_steps(cuts, mid, result, qa, qb, cx, cy)

    @pl.when(flags[5] == 0)
    def _():
        sides_beyond(ghost, beyond)

        @pl.when(flags[3] == 1)
        def _():
            def copy(k):
                for n in TRACERS:
                    for step in range(STEPS - 1):
                        my_cuts[step, n, k] = cuts[step, n, k]
                    my_mid[n, k] = mid[n, k]
                    my_mid[n, 8 + k] = mid[n, 8 + k]

            loop(8, copy, 4)

        outer_prepare(flags, rows, ghost, qa, my_cx, my_cy)
        outer_steps(my_cuts, my_mid, result, qa, qb, my_cx, my_cy)


def edge_kernel(flags, base1, base2, beyond1, beyond2, odd_strip, even_strip, result1, result2, temp, salt, qa, qb, cx, cy, temp_out, salt_out, sems):
    top, inner_first, outer_first, sides_first = (flags[n] == 1 for n in (1, 3, 4, 5))
    lane = lanes(128)
    from_odd = (lane < 64).astype(jnp.int32) != flags[2]
    beside = within(8, 16) | within(72, 80) | within(32, 40) | within(96, 104)
    for_temp = within(8, 16) | within(72, 80)
    place = [within(8 * f, 8 * f + 8) | within(8 * f + 64, 8 * f + 72) for f in range(8)]

    def base(f, k):
        return jnp.where(inner_first, base1[f, k], base2[f, k])

    def beyond(f, k):
        return jnp.where(sides_first, beyond1[f, k], beyond2[f, k])

    def assemble(either, k, r, half, turn=None):
        a, b = odd_strip[r], even_strip[r]
        halo = jnp.where(from_odd, a, b) if half == 0 else jnp.where(from_odd, b, a)
        again = roll(halo, SALT)
        to = PAD + r + half * (EXT // 2)
        y = jnp.where(for_temp, roll(halo, 8 - 64 * half), roll(halo, SALT - 64 * half))
        qa[0, to] = jnp.where(beside, y, either(0, k))
        x = []
        for f in XF + YF:
            y = roll(jnp.where(place[f], halo, again), 8 - 8 * f - 64 * half)
            x.append(jnp.where(beside, y, either(f - 1, k)))
        if turn is not None:
            x[:3] = [jnp.where(turn, roll(z, -1), z) for z in x[:3]]
        store_x(cx, to, *x[:3])
        store_y(cy, to, *x[3:])

    def ghosts(k):
        assemble(beyond, k, k, 0)
        assemble(beyond, HALO + k, 2 * HALO + k, 1, top)

    loop(HALO, ghosts, 4)

    def own(k):
        assemble(base, k, HALO + k, 0)
        assemble(base, 2 * HALO + k, k, 1)

    loop(2 * HALO, own, 8)

    def two(_):
        for src, dst in ((qa, qb), (qb, qa)):
            loop(2, lambda i: rows_forward(src, dst, cx, cy, 2 + 22 * i, 22, 1, 1, seam=True, pad=PAD))

    loop(STEPS // 2, two)

    def patch(j):
        e = qa[0, PAD + HALO + j]
        for n, out in enumerate((temp_out, salt_out)):
            x = jnp.where(outer_first, result1[n, j], result2[n, j])
            w = jnp.where(lane < 8, roll(e, -16 - SALT * n), x[:, :128])
            z = jnp.where(lane >= 120, roll(e, 56 - SALT * n), x[:, 128:])
            for at, y in zip(places(j), (w, z)):
                out[at, :] = y

    copies = []
    for i in range(HEIGHT // 8):
        loop(8, lambda j: patch(8 * i + j), 8)
        for n, (x, y) in enumerate(((temp_out, temp), (salt_out, salt))):
            x = x.reshape(LEVELS, 2 * HEIGHT, 128)
            part = pl.ds(16 * i, 16)
            copies.append(pltpu.make_async_copy(x.at[:, part, :], y.at[:, part, :], sems.at[n, i]))
            copies[-1].start()
    for copy in copies:
        copy.wait()


def call(kernel, outs, args, scratch=(), args_in=None, flags=None, outs_in=VMEM):
    first = [] if flags is None else [flags]
    return pl.pallas_call(
        kernel,
        out_shape=[jax.ShapeDtypeStruct(s, F32) for s in outs],
        in_specs=[SMEM] * len(first) + (args_in or [VMEM] * len(args)),
        out_specs=[outs_in] * len(outs),
        scratch_shapes=[pltpu.VMEM(s, F32) if isinstance(s, tuple) else s for s in scratch],
        compiler_params=PARAMS,
        cost_estimate=COST,
    )(*first, *args)


ROW = (LEVELS, WIDTH)
TILE = (LEVELS, 128)
STRIP = (EXT // 2, *TILE)
STATE = (2, EXT, *ROW)
FLAT = (2 * LEVELS * HEIGHT, 128)


STATES = [STATE] * 5 + [(6, EXT, *ROW), (5, EXT, *ROW)]
OUTER = [STATE, (6, EXT, *ROW), (5, EXT, *ROW)]
RESULT = (2, HEIGHT, *ROW)
CUTS, MID, BASE, BEYOND = (STEPS, 2, 8, *ROW), (2, 2 * HALO, *ROW), (7, HEIGHT, *TILE), (7, 2 * HALO, *TILE)
GHOST = (8, 2 * HALO, *ROW)
IN_HBM = pl.BlockSpec(memory_space=pltpu.HBM)


def pack(flags, args):
    held = [pltpu.VMEM((2, LEVELS, 16, 128), x.dtype) for x in args]
    args = [pltpu.with_memory_space_constraint(x.reshape(LEVELS, -1, 128), pltpu.HBM) for x in args]
    return call(
        pack_kernel,
        [(MESSAGE, *ROW)] * 2 + [TILE],
        args,
        [*held, pltpu.SemaphoreType.DMA((9, 2))],
        [IN_HBM] * 9,
        flags,
    )


def transpose(flags, args, after):
    held = [pltpu.VMEM(FLAT, x.dtype) for x in args]
    args = [pltpu.with_memory_space_constraint(x, pltpu.HBM) for x in args]
    return call(
        rows_kernel,
        [(8, HEIGHT, *ROW), STRIP, STRIP, CUTS, MID, BASE],
        [*args, after],
        [*held, pltpu.SemaphoreType.DMA((9,)), *STATES],
        [IN_HBM] * 9 + [VMEM],
        flags,
    )


def fill_ghost(flags, *args):
    return call(
        ghost_kernel,
        [GHOST, STRIP, STRIP, RESULT, BEYOND, *OUTER],
        args,
        [STATE] * 2,
        flags=flags,
    )


def late(flags, *args):
    return call(
        late_kernel,
        [RESULT, BASE, BEYOND],
        args,
        [CUTS, MID, *STATES],
        flags=flags,
    )


def edge(flags, *args):
    return call(
        edge_kernel,
        [(LEVELS, 2 * HEIGHT, 128)] * 2,
        args,
        [(1, EDGE_DEPTH, *TILE)] * 2
        + [(6, EDGE_DEPTH, *TILE), (5, EDGE_DEPTH, *TILE), FLAT, FLAT, pltpu.SemaphoreType.DMA((2, HEIGHT // 8))],
        flags=flags,
        outs_in=IN_HBM,
    )


def on_device(lon_count, lat_count, *args):
    lon, lat = lax.axis_index("lon"), lax.axis_index("lat")
    top = (lat == lat_count - 1).astype(jnp.int32)
    place = lon % 8
    inner_first = ((place < INNER_FIRST) | (lat >= lat_count - 2)).astype(jnp.int32)
    outer_first = ((place < OUTER_FIRST) & (lat < lat_count - 2)).astype(jnp.int32)
    sides_first = ((place < INNER_FIRST) & (lat != lat_count - 2)).astype(jnp.int32)
    flags = jnp.stack([lat % 2, top, lon % 2, inner_first, outer_first, sides_first])
    flat = [level_major(x) for x in args]

    def index(i, j):
        return i * lat_count + j

    lons, lats = range(lon_count), range(lat_count)
    lat_even = [(index(i, j), index(i, j ^ 1)) for i in lons for j in lats]
    lat_odd = [
        (index(i, j), index(lon_count - 1 - i, j) if j == lat_count - 1 else index(i, j + 1 if j % 2 else j - 1))
        for i in lons
        for j in lats
        if j > 0
    ]
    lon_even = [(i, i ^ 1) for i in lons]
    lon_odd = [(i, (i + 1 if i % 2 else i - 1) % lon_count) for i in lons]
    both = ("lon", "lat")
    odd_msg, even_msg, packed = pack(flags, flat)
    odd_in = lax.ppermute(odd_msg, both, lat_odd)
    even_in = lax.ppermute(even_msg, both, lat_even)
    rows, east, west, cuts, mid, base1 = transpose(flags, flat, packed)
    ghost, odd_strip, even_strip, result1, beyond1, *prepared = fill_ghost(
        flags, rows, odd_in, even_in, east, west, cuts, mid
    )
    odd_strip = lax.ppermute(odd_strip, "lon", lon_odd)
    even_strip = lax.ppermute(even_strip, "lon", lon_even)
    result2, base2, beyond2 = late(flags, rows, ghost, cuts, mid, *prepared)
    temp, salt = edge(flags, base1, base2, beyond1, beyond2, odd_strip, even_strip, result1, result2)
    return from_level_major(temp), from_level_major(salt)


def solution(mesh):
    spec = P(None, "lat", "lon")
    return jax.shard_map(
        functools.partial(on_device, mesh.shape["lon"], mesh.shape["lat"]),
        mesh=mesh,
        in_specs=(spec,) * 9,
        out_specs=(spec, spec),
        check_vma=False,
    )
```

```python
import functools

import jax
import jax.numpy as jnp
from jax import lax
from jax.experimental import pallas as pl
from jax.experimental.pallas import tpu as pltpu
from jax.sharding import PartitionSpec as P

STEPS = 4
HALO = 2 * STEPS
PAD = 4
INNER_FIRST = 7
SIDES_FIRST = 4
OUTER_FIRST = 3
LEVELS = 8
HEIGHT = 32
WIDTH = 256
EXT = HEIGHT + 2 * HALO
TOP = HALO + HEIGHT - 1
EDGE_DEPTH = EXT + 2 * PAD
F32 = jnp.float32
VMEM = pl.BlockSpec(memory_space=pltpu.VMEM)
SMEM = pl.BlockSpec(memory_space=pltpu.SMEM)
PARAMS = pltpu.CompilerParams(vmem_limit_bytes=24 * 2**20)
COST = pl.CostEstimate(flops=50_000_000, bytes_accessed=8_000_000, transcendentals=0)

TRACERS, XF, YF = (0, 1), (2, 3, 4), (5, 6, 7)
FLIPPED = (2, 4, 5, 7)
MESSAGE = 2 * 8 + 3 * 6 + 3 * 7


def slot(field, k):
    if field < 2:
        return field * 8 + k
    if field < 5:
        return 16 + (field - 2) * 6 + k
    return 34 + (field - 5) * 7 + k


def rows_of(field):
    return 8 if field < 2 else 6 if field < 5 else 7


def level_major(x):
    x = x.reshape(LEVELS, HEIGHT // 8, 8, WIDTH // 128, 128)
    return x.transpose(0, 1, 3, 2, 4).reshape(-1, 128)


def from_level_major(x):
    x = x.reshape(LEVELS, HEIGHT // 8, WIDTH // 128, 8, 128)
    return x.transpose(0, 1, 3, 2, 4).reshape(LEVELS, HEIGHT, WIDTH)


def places(j):
    start = (j // 8) * 16 + j % 8
    return [pl.ds(start + 8 * c, LEVELS, stride=2 * HEIGHT) for c in range(2)]


def load_row(ref, j):
    return jnp.concatenate([ref[at, :] for at in places(j)], axis=1)


def lanes(width):
    return lax.broadcasted_iota(jnp.int32, (LEVELS, width), 1)


def within(lo, hi):
    lane = lanes(128)
    return (lane >= lo) & (lane < hi)


def roll(x, by):
    return pltpu.roll(x, by % x.shape[-1], 1)


def fields(held, at):
    temp, salt, u, v, diff, sx, sy, mu, mv = (at(ref) for ref in held)
    wet_u, wet_v = mu.astype(F32), mv.astype(F32)
    return temp, salt, u * wet_u, diff * wet_u, sx, v * wet_v, diff * wet_v, sy


def pack_kernel(flags, *refs):
    args, (odd_msg, even_msg, done), held, sems = refs[:9], refs[9:12], refs[12:21], refs[21]
    done[...] = jnp.zeros((LEVELS, 128), F32)
    copies = []
    for n, (x, y) in enumerate(zip(args, held)):
        for part, start in enumerate((0, 2 * HEIGHT - 16)):
            copies.append(pltpu.make_async_copy(x.at[:, pl.ds(start, 16), :], y.at[part], sems.at[n, part]))
    for n in (0, 1, 2, 4, 5, 7, 3, 6, 8):
        copies[2 * n].start()
        copies[2 * n + 1].start()
    odd = flags[0]

    def put(group, make):
        def row(i):
            for msg, part in ((odd_msg, odd), (even_msg, 1 - odd)):
                k = jnp.where(part == 1, i, 7 - i)

                def at(n):
                    flat = held[n].at[part].reshape(LEVELS * 16, 128)
                    return jnp.concatenate([flat[pl.ds(8 * c + k, LEVELS, stride=16), :] for c in range(2)], axis=1)

                for f, x in zip(group, make(at)):
                    n = rows_of(f)
                    msg[slot(f, 0) + jnp.clip(k - (8 - n) * part, 0, n - 1)] = x

        loop(8, row, 4)

    def face(at, c, slope, mask):
        wet = at(mask).astype(F32)
        return at(c) * wet, at(4) * wet, at(slope)

    for group, needs, make in (
        (TRACERS, (0, 1), lambda at: (at(0), at(1))),
        (XF, (2, 4, 5, 7), lambda at: face(at, 2, 5, 7)),
        (YF, (3, 6, 8), lambda at: face(at, 3, 6, 8)),
    ):
        for n in needs:
            copies[2 * n].wait()
            copies[2 * n + 1].wait()
        put(group, make)


def add_sides(parts, x, half):
    east, west = parts
    for f in range(8):
        to = 8 * f + 64 * half
        east = jnp.where(within(to, to + 8), roll(x[f][:, 128:], to + 8), east)
        to = 8 * f + 64 * (1 - half)
        west = jnp.where(within(to, to + 8), roll(x[f][:, :128], to), west)
    return east, west


def rows_kernel(flags, *refs):
    args, _, outs, held, sems = refs[:9], refs[9], refs[10:16], refs[16:25], refs[25]
    rows, east_own, west_own, cuts, mid, base = outs
    copies = [pltpu.make_async_copy(x, y, sems.at[n]) for n, (x, y) in enumerate(zip(args, held))]
    for copy in copies:
        copy.start()
    for copy in copies:
        copy.wait()

    def one(j):
        for f, x in enumerate(fields(held, lambda ref: load_row(ref, j))):
            rows[f, j] = x

    loop(HEIGHT, one, 4)

    def sides(r):
        parts = [jnp.zeros((LEVELS, 128), F32)] * 2
        for half in range(2):
            idx = r + half * (EXT // 2)
            j = jnp.clip(idx - HALO, 0, HEIGHT - 1)
            parts = add_sides(parts, [rows[f, j] for f in range(8)], half)
        east_own[r], west_own[r] = parts

    loop(EXT // 2, sides, 4)

    @pl.when(flags[3] == 1)
    def _():
        inner_part(rows, cuts, mid, base, *refs[26:])


def mirrored(x):
    n = x.shape[-1] // 128
    back = 127 - lanes(128)
    parts = [x[:, 128 * i : 128 * (i + 1)] for i in range(n)]
    return jnp.concatenate([jnp.take_along_axis(p, back, axis=1) for p in reversed(parts)], axis=1)


def fold_rows(msg, ghost):
    for f in range(8):
        n = rows_of(f)
        sign = -1.0 if f in FLIPPED else 1.0
        for k in range(n):
            x = mirrored(msg[slot(f, n - 1 - k)]) * sign
            if f < 5:
                ghost[f, HALO + k] = x
            elif k == 0:
                ghost[f, 0] = x
            else:
                ghost[f, HALO + k - 1] = x


def ghost_kernel(flags, rows, odd_msg, even_msg, east_own, west_own, cuts, mid, ghost, odd_strip, even_strip, result, base, q, cx, cy, qa, qb):
    is_odd = flags[0] == 1
    for f in range(8):
        n = rows_of(f)
        for k in range(n):
            a, b = odd_msg[slot(f, k)], even_msg[slot(f, k)]
            ghost[f, HALO - n + k] = jnp.where(is_odd, b, a)
            if k < n - (f >= 5):
                ghost[f, HALO + k] = jnp.where(is_odd, a, b)
        if f >= 5:
            ghost[f, 0] = rows[f, HEIGHT - 1]

    @pl.when(flags[1] == 1)
    def _():
        fold_rows(odd_msg, ghost)

    swap = flags[2] == 1
    for r in range(EXT // 2):
        parts = [east_own[r], west_own[r]]
        if r < HALO:
            parts = add_sides(parts, [ghost[f, r] for f in range(8)], 0)
        if r >= 2 * HALO:
            parts = add_sides(parts, [ghost[f, r - HALO] for f in range(8)], 1)
        even_strip[r] = jnp.where(swap, parts[1], parts[0])
        odd_strip[r] = jnp.where(swap, parts[0], parts[1])

    @pl.when(flags[5] == 1)
    def _():
        sides_beyond(ghost, base)
        outer_prepare(flags, rows, ghost, q, cx, cy)

    @pl.when(flags[4] == 1)
    def _():
        start_from(q, qa)
        outer_steps(cuts, mid, result, qa, qb, cx, cy)


def start_from(q, qa):
    def copy(k):
        for n in TRACERS:
            qa[n, k] = q[n, k]
            qa[n, EXT - 12 + k] = q[n, EXT - 12 + k]

    loop(12, copy, 4)


def minmod(p, t):
    return jnp.maximum(jnp.minimum(p, t), jnp.minimum(jnp.maximum(p, t), 0.0))


def vertical(q):
    level = lax.broadcasted_iota(jnp.int32, q.shape, 0)
    up = jnp.where(level == LEVELS - 1, q, pltpu.roll(q, LEVELS - 1, 0))
    down = jnp.where(level == 0, q, pltpu.roll(q, 1, 0))
    return up - down


def shifted(tiles, by):
    lane = lanes(128)
    rolled = [roll(t, by) for t in tiles]
    if len(tiles) == 1:
        return rolled
    seam = lane == (0 if by == 1 else 127)
    return [jnp.where(seam, rolled[1 - n], rolled[n]) for n in range(2)]


def coefficients(c, r, s):
    plus, minus = jnp.maximum(c, 0.0), jnp.minimum(c, 0.0)
    return (
        plus + r,
        0.5 * plus * (1.0 - plus),
        0.25 * r * s,
        minus - r,
        -0.5 * minus * (1.0 + minus),
    )


def store_x(cx, idx, c, r, s):
    p, lp, t, e, ln = coefficients(c, r, s)
    for n, x in enumerate((p, lp, t, roll(e, 1), roll(ln, 1), roll(t, 1))):
        cx[n, idx] = x


def store_y(cy, idx, c, r, s):
    for n, x in enumerate(coefficients(c, r, s)):
        cy[n, idx] = x


def rows_forward(src, dst, cx, cy, first, chunk, streams, tiles, seam=False, pad=0):
    def at(ref, n, idx, t):
        return ref[n, pad + idx, :, 128 * t : 128 * (t + 1)]

    def face(idx, t, q0, q1, m0, m1, g0, g1):
        c = [at(cy, n, idx, t) for n in range(5)]
        return (c[0] * q0 + c[3] * q1) + (c[1] * m0 + c[4] * m1) + c[2] * (g0 + g1)

    south = jnp.where(first == TOP + 1, 0, first - 1)
    carry = []
    for n in range(streams):
        for t in range(tiles):
            q = [at(src, n, first - 2 + k, t) for k in range(4)]
            d = [q[k + 1] - q[k] for k in range(3)]
            m0, m1 = minmod(d[0], d[1]), minmod(d[1], d[2])
            g0, g1 = vertical(q[1]), vertical(q[2])
            carry.append((q[2], q[3], d[2], m1, g1, face(south, t, q[1], q[2], m0, m1, g0, g1)))
    for k in range(chunk):
        idx = first + k
        out = []
        for n in range(streams):
            q0 = [carry[n * tiles + t][0] for t in range(tiles)]
            d = [x - y for x, y in zip(shifted(q0, -1), q0)]
            m = [minmod(x, y) for x, y in zip(d, shifted(d, 1))]
            a, b = [], []
            for t in range(tiles):
                g0 = carry[n * tiles + t][4]
                c = [at(cx, i, idx, t) for i in range(6)]
                a.append(c[0] * q0[t] + c[1] * m[t] + c[2] * g0)
                b.append(c[3] * q0[t] + c[4] * m[t] + c[5] * g0)
            x = [(b[t] - a[t]) + (p - r) for t, (p, r) in enumerate(zip(shifted(a, 1), shifted(b, -1)))]
            for t in range(tiles):
                q0, q1, d0, m0, g0, south = carry[n * tiles + t]
                q2 = at(src, n, idx + 2, t)
                d1 = q2 - q1
                m1 = minmod(d0, d1)
                g1 = vertical(q1)
                north = face(idx, t, q0, q1, m0, m1, g0, g1)
                dst[n, pad + idx, :, 128 * t : 128 * (t + 1)] = q0 + x[t] + (south - north)
                if isinstance(idx, int):
                    if idx == TOP and seam:
                        north = face(0, t, q0, q1, m0, m1, g0, g1)
                elif seam and k % 2 == 1 and k < chunk - 1:
                    at_seam = jnp.full((LEVELS, 128), idx, jnp.int32) == TOP
                    north = jnp.where(at_seam, face(0, t, q0, q1, m0, m1, g0, g1), north)
                out.append((q1, q2, d1, m1, g1, north))
        carry = out


def loop(count, body, unroll=1):
    def step(i, _):
        body(i)
        return 0

    lax.fori_loop(0, count, step, 0, unroll=unroll)


SALT = 24


def edges_of(x):
    return jnp.where(within(16, 32), roll(x[:, :128], 16), roll(x[:, 128:], 72))


def store_edges(base, k, x):
    x = [edges_of(y) for y in x]
    is_temp = within(8, 32) | within(56, 80)
    base[0, k] = jnp.where(is_temp, x[0], roll(x[1], SALT))
    for f in range(2, 8):
        base[f - 1, k] = jnp.where(is_temp, x[f], roll(x[f], SALT))


def inner_part(rows, cuts, mid, base, s0, s1, s2, s3, s4, cx, cy):
    def own(j):
        for n in TRACERS:
            s0[n, HALO + j] = rows[n, j]
        x = [rows[f, j] for f in range(8)]
        store_x(cx, HALO + j, *(x[f] for f in XF))
        store_y(cy, HALO + j, *(x[f] for f in YF))
        store_edges(base, j, x)

    loop(HEIGHT, own, 4)
    for src, dst, first, count in ((s0, s1, 0, 4), (s1, s2, 4, 3), (s2, s3, 4, 3), (s3, s4, 8, 2)):
        loop(count, lambda i: rows_forward(src, dst, cx, cy, HALO + first + 8 * i, 8, 2, 2))
    for n in TRACERS:
        for step, s in enumerate((s1, s2, s3), 1):
            low = HALO + 2 * step
            for k in range(4):
                cuts[step - 1, n, k] = s[n, low + k]
                cuts[step - 1, n, 4 + k] = s[n, EXT - 4 - low + k]

        def out(j, n=n):
            mid[n, j] = s4[n, 2 * HALO + j]

        loop(2 * HALO, out, 4)


def sides_beyond(ghost, base):
    loop(2 * HALO, lambda k: store_edges(base, k, [ghost[f, k] for f in range(8)]), 4)


def outer_prepare(flags, rows, ghost, q, cx, cy):
    top = flags[1] == 1

    def near(k):
        for start in (0, HEIGHT - HALO):
            j = start + k
            for n in TRACERS:
                q[n, HALO + j] = rows[n, j]
            store_x(cx, HALO + j, *(rows[f, j] for f in XF))
            store_y(cy, HALO + j, *(rows[f, j] for f in YF))

    loop(HALO, near, 4)
    store_y(cy, TOP - HALO, *(rows[f, HEIGHT - HALO - 1] for f in YF))

    def beyond(k, north):
        to = HEIGHT + k if north else k
        x = [ghost[f, k] for f in range(8)]
        for n in TRACERS:
            q[n, to] = x[n]
        store_x(cx, to, *(jnp.where(top, roll(x[f], -1), x[f]) if north else x[f] for f in XF))
        store_y(cy, to, *(x[f] for f in YF))

    loop(HALO, lambda k: beyond(k, False), 4)
    loop(HALO, lambda k: beyond(HALO + k, True), 4)


def outer_steps(cuts, mid, result, qa, qb, cx, cy):
    def one(src, dst, step):
        low = HALO + 2 * step
        for n in TRACERS:
            for k in range(4):
                dst[n, low + k] = cuts[step - 1, n, k]
                dst[n, EXT - 4 - low + k] = cuts[step - 1, n, 4 + k]
        loop(2, lambda w: rows_forward(src, dst, cx, cy, 2 * step + w * (EXT - 8 - 4 * step), 8, 2, 2, seam=True))

    def two(i):
        one(qa, qb, 2 * i + 1)
        one(qb, qa, 2 * i + 2)

    loop(STEPS // 2, two)

    def out(j):
        for n in TRACERS:
            result[n, j] = qa[n, HALO + j]
            result[n, HEIGHT - HALO + j] = qa[n, HEIGHT + j]
            result[n, HALO + j] = mid[n, j]
            result[n, 2 * HALO + j] = mid[n, HALO + j]

    loop(HALO, out, 2)


def late_kernel(flags, rows, ghost, cuts, mid, q, cx, cy, result, base, beyond, my_cuts, my_mid, *scratch):
    states, (my_cx, my_cy) = scratch[:5], scratch[5:]
    qa, qb = states[:2]

    @pl.when(flags[3] == 0)
    def _():
        inner_part(rows, my_cuts, my_mid, base, *states, my_cx, my_cy)

    @pl.when((flags[5] == 1) & (flags[4] == 0))
    def _():
        start_from(q, qa)
        outer_steps(cuts, mid, result, qa, qb, cx, cy)

    @pl.when(flags[5] == 0)
    def _():
        sides_beyond(ghost, beyond)

        @pl.when(flags[3] == 1)
        def _():
            def copy(k):
                for n in TRACERS:
                    for step in range(STEPS - 1):
                        my_cuts[step, n, k] = cuts[step, n, k]
                    my_mid[n, k] = mid[n, k]
                    my_mid[n, 8 + k] = mid[n, 8 + k]

            loop(8, copy, 4)

        outer_prepare(flags, rows, ghost, qa, my_cx, my_cy)
        outer_steps(my_cuts, my_mid, result, qa, qb, my_cx, my_cy)


def edge_kernel(flags, base1, base2, beyond1, beyond2, odd_strip, even_strip, result1, result2, temp, salt, qa, qb, cx, cy, temp_out, salt_out, sems):
    top, inner_first, outer_first, sides_first = (flags[n] == 1 for n in (1, 3, 4, 5))
    lane = lanes(128)
    from_odd = (lane < 64).astype(jnp.int32) != flags[2]
    beside = within(8, 16) | within(72, 80) | within(32, 40) | within(96, 104)
    for_temp = within(8, 16) | within(72, 80)
    place = [within(8 * f, 8 * f + 8) | within(8 * f + 64, 8 * f + 72) for f in range(8)]

    def base(f, k):
        return jnp.where(inner_first, base1[f, k], base2[f, k])

    def beyond(f, k):
        return jnp.where(sides_first, beyond1[f, k], beyond2[f, k])

    def assemble(either, k, r, half, turn=None):
        a, b = odd_strip[r], even_strip[r]
        halo = jnp.where(from_odd, a, b) if half == 0 else jnp.where(from_odd, b, a)
        again = roll(halo, SALT)
        to = PAD + r + half * (EXT // 2)
        y = jnp.where(for_temp, roll(halo, 8 - 64 * half), roll(halo, SALT - 64 * half))
        qa[0, to] = jnp.where(beside, y, either(0, k))
        x = []
        for f in XF + YF:
            y = roll(jnp.where(place[f], halo, again), 8 - 8 * f - 64 * half)
            x.append(jnp.where(beside, y, either(f - 1, k)))
        if turn is not None:
            x[:3] = [jnp.where(turn, roll(z, -1), z) for z in x[:3]]
        store_x(cx, to, *x[:3])
        store_y(cy, to, *x[3:])

    def ghosts(k):
        assemble(beyond, k, k, 0)
        assemble(beyond, HALO + k, 2 * HALO + k, 1, top)

    loop(HALO, ghosts, 8)

    def own(k):
        assemble(base, k, HALO + k, 0)
        assemble(base, 2 * HALO + k, k, 1)

    loop(2 * HALO, own, 8)

    def two(_):
        for src, dst in ((qa, qb), (qb, qa)):
            loop(2, lambda i: rows_forward(src, dst, cx, cy, 2 + 22 * i, 22, 1, 1, seam=True, pad=PAD))

    loop(STEPS // 2, two)

    def patch(j):
        e = qa[0, PAD + HALO + j]
        for n, out in enumerate((temp_out, salt_out)):
            x = jnp.where(outer_first, result1[n, j], result2[n, j])
            w = jnp.where(lane < 8, roll(e, -16 - SALT * n), x[:, :128])
            z = jnp.where(lane >= 120, roll(e, 56 - SALT * n), x[:, 128:])
            for at, y in zip(places(j), (w, z)):
                out[at, :] = y

    copies = []
    for i in range(HEIGHT // 8):
        loop(8, lambda j: patch(8 * i + j), 8)
        for n, (x, y) in enumerate(((temp_out, temp), (salt_out, salt))):
            x = x.reshape(LEVELS, 2 * HEIGHT, 128)
            part = pl.ds(16 * i, 16)
            copies.append(pltpu.make_async_copy(x.at[:, part, :], y.at[:, part, :], sems.at[n, i]))
            copies[-1].start()
    for copy in copies:
        copy.wait()


def call(kernel, outs, args, scratch=(), args_in=None, flags=None, outs_in=VMEM):
    first = [] if flags is None else [flags]
    return pl.pallas_call(
        kernel,
        out_shape=[jax.ShapeDtypeStruct(s, F32) for s in outs],
        in_specs=[SMEM] * len(first) + (args_in or [VMEM] * len(args)),
        out_specs=[outs_in] * len(outs),
        scratch_shapes=[pltpu.VMEM(s, F32) if isinstance(s, tuple) else s for s in scratch],
        compiler_params=PARAMS,
        cost_estimate=COST,
    )(*first, *args)


ROW = (LEVELS, WIDTH)
TILE = (LEVELS, 128)
STRIP = (EXT // 2, *TILE)
STATE = (2, EXT, *ROW)
FLAT = (2 * LEVELS * HEIGHT, 128)


STATES = [STATE] * 5 + [(6, EXT, *ROW), (5, EXT, *ROW)]
OUTER = [STATE, (6, EXT, *ROW), (5, EXT, *ROW)]
RESULT = (2, HEIGHT, *ROW)
CUTS, MID, BASE, BEYOND = (STEPS, 2, 8, *ROW), (2, 2 * HALO, *ROW), (7, HEIGHT, *TILE), (7, 2 * HALO, *TILE)
GHOST = (8, 2 * HALO, *ROW)
IN_HBM = pl.BlockSpec(memory_space=pltpu.HBM)


def pack(flags, args):
    held = [pltpu.VMEM((2, LEVELS, 16, 128), x.dtype) for x in args]
    args = [pltpu.with_memory_space_constraint(x.reshape(LEVELS, -1, 128), pltpu.HBM) for x in args]
    return call(
        pack_kernel,
        [(MESSAGE, *ROW)] * 2 + [TILE],
        args,
        [*held, pltpu.SemaphoreType.DMA((9, 2))],
        [IN_HBM] * 9,
        flags,
    )


def transpose(flags, args, after):
    held = [pltpu.VMEM(FLAT, x.dtype) for x in args]
    args = [pltpu.with_memory_space_constraint(x, pltpu.HBM) for x in args]
    return call(
        rows_kernel,
        [(8, HEIGHT, *ROW), STRIP, STRIP, CUTS, MID, BASE],
        [*args, after],
        [*held, pltpu.SemaphoreType.DMA((9,)), *STATES],
        [IN_HBM] * 9 + [VMEM],
        flags,
    )


def fill_ghost(flags, *args):
    return call(
        ghost_kernel,
        [GHOST, STRIP, STRIP, RESULT, BEYOND, *OUTER],
        args,
        [STATE] * 2,
        flags=flags,
    )


def late(flags, *args):
    return call(
        late_kernel,
        [RESULT, BASE, BEYOND],
        args,
        [CUTS, MID, *STATES],
        flags=flags,
    )


def edge(flags, *args):
    return call(
        edge_kernel,
        [(LEVELS, 2 * HEIGHT, 128)] * 2,
        args,
        [(1, EDGE_DEPTH, *TILE)] * 2
        + [(6, EDGE_DEPTH, *TILE), (5, EDGE_DEPTH, *TILE), FLAT, FLAT, pltpu.SemaphoreType.DMA((2, HEIGHT // 8))],
        flags=flags,
        outs_in=IN_HBM,
    )


def on_device(lon_count, lat_count, *args):
    lon, lat = lax.axis_index("lon"), lax.axis_index("lat")
    top = (lat == lat_count - 1).astype(jnp.int32)
    place = lon % 8
    inner_first = ((place < INNER_FIRST) | (lat >= lat_count - 2)).astype(jnp.int32)
    outer_first = ((place < OUTER_FIRST) & (lat < lat_count - 2)).astype(jnp.int32)
    sides_first = ((place < SIDES_FIRST) & (lat != lat_count - 2)).astype(jnp.int32)
    flags = jnp.stack([lat % 2, top, lon % 2, inner_first, outer_first, sides_first])
    flat = [level_major(x) for x in args]

    def index(i, j):
        return i * lat_count + j

    lons, lats = range(lon_count), range(lat_count)
    lat_even = [(index(i, j), index(i, j ^ 1)) for i in lons for j in lats]
    lat_odd = [
        (index(i, j), index(lon_count - 1 - i, j) if j == lat_count - 1 else index(i, j + 1 if j % 2 else j - 1))
        for i in lons
        for j in lats
        if j > 0
    ]
    lon_even = [(i, i ^ 1) for i in lons]
    lon_odd = [(i, (i + 1 if i % 2 else i - 1) % lon_count) for i in lons]
    both = ("lon", "lat")
    odd_msg, even_msg, packed = pack(flags, flat)
    odd_in = lax.ppermute(odd_msg, both, lat_odd)
    even_in = lax.ppermute(even_msg, both, lat_even)
    rows, east, west, cuts, mid, base1 = transpose(flags, flat, packed)
    ghost, odd_strip, even_strip, result1, beyond1, *prepared = fill_ghost(
        flags, rows, odd_in, even_in, east, west, cuts, mid
    )
    odd_strip = lax.ppermute(odd_strip, "lon", lon_odd)
    even_strip = lax.ppermute(even_strip, "lon", lon_even)
    result2, base2, beyond2 = late(flags, rows, ghost, cuts, mid, *prepared)
    temp, salt = edge(flags, base1, base2, beyond1, beyond2, odd_strip, even_strip, result1, result2)
    return from_level_major(temp), from_level_major(salt)


def solution(mesh):
    spec = P(None, "lat", "lon")
    return jax.shard_map(
        functools.partial(on_device, mesh.shape["lon"], mesh.shape["lat"]),
        mesh=mesh,
        in_specs=(spec,) * 9,
        out_specs=(spec, spec),
        check_vma=False,
    )
```
